32 devices in a mesh: group: 2 (over y), blk: 4 (over z), tensor: 4 (over x, core).
Axes of the slice: x: 2, y: 2, z: 4, core: 2. Of those that a mesh axis runs over, the one named last changes fastest.
Arguments:
- queries: bfloat16 [8, 256, 64, 128], P(('group', 'blk'), None, 'tensor'), parts along dimension 0, may hold values from -36 to 36
- new_kv: bfloat16 [2, 8, 256, 8, 128], P(None, ('group', 'blk'), None, 'tensor'), parts along dimension 1, may hold values from -24 to 24
- pool: bfloat16 [192, 2, 128, 8, 128], P(('group', 'blk'), None, None, 'tensor'), parts along dimension 0, may hold values from -6 to 6
- prefix_slot: int32 [8, 32], P(('group', 'blk')), parts along dimension 0, may hold values from 0 to 23
- prefix_owner: int32 [8, 32], P(('group', 'blk')), parts along dimension 0, may hold values from 0 to 3, as said below
- prefix_len: int32 [8], P(('group', 'blk')), parts along dimension 0, may hold values from 1 to 32, as said below
- write_slot: int32 [8, 2], P(('group', 'blk')), parts along dimension 0, may hold values from 0 to 23
- write_owner: int32 [8, 2], P(('group', 'blk')), parts along dimension 0, may hold values from 0 to 3, as said below
Outputs:
- attended: bfloat16 [8, 256, 64, 128], P(('group', 'blk'), None, 'tensor'), parts along dimension 0
- new_pool: bfloat16 [192, 2, 128, 8, 128], P(('group', 'blk'), None, None, 'tensor'), parts along dimension 0
The draws below stay inside these ranges and needn't reach their ends.
There are 2 independent parts, one for each index of `group`. The reference program is written for one: setup_inputs(seed, part) draws one part's arguments, and reference() takes and returns one part's arrays. A program takes and returns all parts, laid end to end along the dimension named above; each array names one. Nothing has to cross between parts.
Inputs may be any that keep to these rules, and one draw needn't show every extreme that they name: `prefix_owner`: in the rows of one request no owner appears more than 8 times; some owner appears exactly 8 times in every request's row. `prefix_len`: some request has exactly 32 prefix blocks. `write_owner`: no two new blocks go to the same pool row; the new blocks of the requests of one index of blk go to different owners; every owner receives exactly 2 new blocks (the requests' new blocks spread evenly over the owners).
All inputs are finite; a program needn't handle non-finite values.
Results may differ from the reference program's by a relative error of at most 0.0065.
Values may be sent and summed in bfloat16 or wider, within the bound.
No kernel may reach another device: no remote copies, remote signals or barrier semaphores. Data moves between devices by JAX's collectives and lax.ppermute only.
A program may use at most 64 MiB of HBM per device.

```python
import jax
import jax.numpy as jnp
from jax import lax

H = 64
KVH = 8
HD = 128
BLK_TOK = 128
SUF = 256
PBLK = 32
POOL_DEV = 24
CAP = 8
NEWB = 2
REQ = 4
POOLS = 96
N_BLK = 4


def draw_queries(key, part):
    key = jax.random.fold_in(key, 3)
    base = jnp.clip(jax.random.normal(key, (REQ, SUF, H, HD), jnp.float32), -4.0, 4.0) * 1.5
    return base.astype(jnp.bfloat16)


def draw_new_kv(key, part):
    key = jax.random.fold_in(key, 5)
    base = jnp.clip(jax.random.normal(key, (2, REQ, SUF, KVH, HD), jnp.float32), -4.0, 4.0)
    return base.astype(jnp.bfloat16)


def draw_prefix_owner(key, part):
    key = jax.random.fold_in(key, 11)
    hot_key, order_key = jax.random.split(key, 2)
    hottest = jax.random.randint(hot_key, (), 0, N_BLK)
    rest = jnp.arange(1, N_BLK, dtype=jnp.int32)

    def one_row(row_key):
        first_key, second_key = jax.random.split(row_key)
        order = jnp.concatenate([jnp.zeros((1,), jnp.int32), jax.random.permutation(first_key, rest)])
        pattern = order[jnp.arange(PBLK) // CAP]
        shuffle = jax.random.permutation(second_key, PBLK)
        return (hottest + pattern[shuffle]) % N_BLK
    return jax.vmap(one_row)(jax.random.split(order_key, REQ)).astype(jnp.int32)


def draw_prefix_len(key, part):
    key = jax.random.fold_in(key, 13)
    first_key, second_key = jax.random.split(key)
    lengths = jax.random.randint(first_key, (REQ,), 1, PBLK + 1)
    longest = jax.random.randint(second_key, (), 0, REQ)
    return jnp.where(jnp.arange(REQ) == longest, PBLK, lengths).astype(jnp.int32)


def write_targets(key):
    first_key, second_key = jax.random.split(key)
    spread = jax.random.permutation(first_key, N_BLK)
    orders = jax.vmap(lambda row_key: jax.random.permutation(row_key, POOL_DEV))(jax.random.split(second_key, N_BLK))
    numbers = jnp.arange(REQ * NEWB)
    owners = spread[numbers % N_BLK]
    slot_ids = orders[owners, numbers // N_BLK]
    return (owners.reshape(REQ, NEWB).astype(jnp.int32), slot_ids.reshape(REQ, NEWB).astype(jnp.int32))


def draw_write_owner(key, part):
    owners, slot_ids = write_targets(key)
    return owners


def draw_write_slot(key, part):
    owners, slot_ids = write_targets(key)
    return slot_ids


def place_ends(values, own_key, least, top_value):
    longest = values.shape.index(max(values.shape))
    spots = []
    for shift in (0, 1):
        where = [jax.random.randint(jax.random.fold_in(own_key, axis), (), 0, length) for axis, length in enumerate(values.shape)]
        where[longest] = (where[longest] + shift) % values.shape[longest]
        spots.append(tuple(where))
    return values.at[spots[0]].set(least).at[spots[1]].set(top_value)


def block_scale(own_key, shape, cuts, least, top_value):
    def one(axis_at, blocks):
        heights = jax.random.uniform(jax.random.fold_in(jax.random.fold_in(own_key, 6), axis_at), (blocks,), jnp.float32, least / len(cuts), top_value / len(cuts))
        return jnp.repeat(jnp.exp(heights), shape[axis_at] // blocks).reshape((-1,) + (1,) * (len(shape) - axis_at - 1))

    factor_of = one(*cuts[0])
    for cut in cuts[1:]:
        factor_of = factor_of * one(*cut)
    return factor_of


def noise(stream_key, dims, scale, reach, shards=(), held_as=jnp.bfloat16):
    drawn = jax.random.normal(stream_key, dims, jnp.float32) * scale
    if len(shards) > 0:
        drawn = block_scale(stream_key, dims, shards, -0.22, 0.18) * drawn
    return jnp.clip(drawn, min=-reach, max=reach).astype(held_as)


def setup_inputs(seed: int = 0, part: int = 0) -> dict:
    key_of = jax.random.split(jax.random.key(seed), 9)
    part_splits = jax.random.split(jax.random.fold_in(key_of[8], part), 9)
    return {
        "queries": draw_queries(jax.random.fold_in(jax.random.fold_in(key_of[8], part), 71), part),
        "new_kv": draw_new_kv(jax.random.fold_in(jax.random.fold_in(key_of[8], part), 71), part),
        "pool": noise(part_splits[2], (POOLS, 2, BLK_TOK, KVH, HD), 1.0, 6.0, ((0, 4), (3, 4))),
        "prefix_slot": place_ends(jax.random.randint(part_splits[3], (REQ, PBLK), 0, POOL_DEV), jax.random.fold_in(part_splits[3], 1), 0, POOL_DEV - 1).astype(jnp.int32),
        "prefix_owner": draw_prefix_owner(jax.random.fold_in(jax.random.fold_in(key_of[8], part), 71), part),
        "prefix_len": draw_prefix_len(jax.random.fold_in(jax.random.fold_in(key_of[8], part), 71), part),
        "write_slot": draw_write_slot(jax.random.fold_in(jax.random.fold_in(key_of[8], part), 71), part),
        "write_owner": draw_write_owner(jax.random.fold_in(jax.random.fold_in(key_of[8], part), 71), part),
    }


def reference(queries, new_kv, pool, prefix_slot, prefix_owner, prefix_len, write_slot, write_owner):
    group = H // KVH
    scale = HD ** -0.5
    prefix_tok = PBLK * BLK_TOK

    def one_request(inputs):
        query_rows, fresh_kv, slot_ids, owner_ids, length = inputs
        rows = (owner_ids * POOL_DEV + slot_ids).astype(jnp.int32)
        blocks = pool[rows]
        keys = jnp.concatenate([blocks[:, 0].reshape(prefix_tok, KVH, HD), fresh_kv[0]], axis=0)
        values = jnp.concatenate([blocks[:, 1].reshape(prefix_tok, KVH, HD), fresh_kv[1]], axis=0)
        query_f = query_rows.astype(jnp.float32).reshape(SUF, KVH, group, HD)
        scores = jnp.einsum("ikgd,jkd->kgij", query_f, keys.astype(jnp.float32)) * scale
        before = jnp.arange(prefix_tok) < length * BLK_TOK
        before = jnp.broadcast_to(before[None, :], (SUF, prefix_tok))
        causal = jnp.arange(SUF)[None, :] <= jnp.arange(SUF)[:, None]
        allowed = jnp.concatenate([before, causal], axis=1)
        scores = jnp.where(allowed, scores, -jnp.inf)
        peak = jnp.max(scores, axis=3, keepdims=True)
        weights = jnp.exp(scores - peak)
        total = jnp.sum(weights, axis=3)
        rounded = weights.astype(jnp.bfloat16)
        summed = jnp.einsum("kgij,jkd->kgid", rounded.astype(jnp.float32), values.astype(jnp.float32))
        result = summed / total[..., None]
        return jnp.transpose(result, (2, 0, 1, 3)).reshape(SUF, H, HD).astype(jnp.bfloat16)

    attended = lax.map(one_request, (queries, jnp.moveaxis(new_kv, 1, 0), prefix_slot, prefix_owner, prefix_len))
    fresh = new_kv.reshape(2, REQ, NEWB, BLK_TOK, KVH, HD)
    fresh = jnp.transpose(fresh, (1, 2, 0, 3, 4, 5)).reshape(REQ * NEWB, 2, BLK_TOK, KVH, HD)
    targets = (write_owner * POOL_DEV + write_slot).reshape(-1).astype(jnp.int32)
    new_pool = pool.at[targets].set(fresh)
    return attended, new_pool
```

```python
import functools
import math

import jax
import jax.numpy as jnp
from jax import lax
from jax.experimental import pallas as pl
from jax.experimental.pallas import tpu as pltpu
from jax.sharding import PartitionSpec as P

HBM = pl.BlockSpec(memory_space=pl.ANY)
SMEM = pl.BlockSpec(memory_space=pltpu.SMEM)
VMEM_LIMIT = 48 * 1024 * 1024


def pick_fresh_kernel(num_blk, block_tok, owner_ref, new_ref, *rest):
    outs, sems = rest[:-1], rest[-1]
    me = lax.axis_index("blk")
    copies = []
    for d, out in enumerate(outs, start=1):
        target = lax.rem(me + d, num_blk)
        chosen = jnp.int32(0)
        for b in range(1, owner_ref.shape[1]):
            chosen = jnp.where(owner_ref[0, b] == target, b, chosen)
        for kv in range(2):
            copies.append(
                pltpu.make_async_copy(
                    new_ref.at[kv, 0, pl.ds(chosen * block_tok, block_tok)],
                    out.at[kv],
                    sems.at[d - 1, kv],
                )
            )
    for copy in copies:
        copy.start()
    for copy in copies:
        copy.wait()


def slots_of(meta_ref, first, pool_dev, prefix_blocks, table_ref, row, capacity):
    for k in range(capacity + 1):
        table_ref[row, k] = 0

    def step(j, count):
        slot = meta_ref[0, j] - first
        mine = (slot >= 0) & (slot < pool_dev)
        table_ref[row, count] = jnp.where(mine, slot, 0)
        return jnp.where(mine, jnp.minimum(count + 1, capacity), count)

    lax.fori_loop(0, prefix_blocks, step, jnp.int32(0))


def gather_kernel(plan, pool_dev, prefix_blocks, capacity, *refs):
    count = len(plan)
    metas, pool_ref, refs = refs[:count], refs[count], refs[count + 1 :]
    outs, table_ref, sems = refs[:-2], refs[-2], refs[-1]
    first = lax.axis_index("blk") * pool_dev
    copies = []
    at = 0
    for row, sizes in enumerate(plan):
        slots_of(metas[row], first, pool_dev, prefix_blocks, table_ref, row, capacity)
        k = 0
        for size in sizes:
            for place in range(size):
                copy = pltpu.make_async_copy(
                    pool_ref.at[table_ref[row, k]], outs[at].at[place], sems.at[row, k]
                )
                copy.start()
                copies.append(copy)
                k += 1
            at += 1
    for copy in copies:
        copy.wait()


def gather(metas, pool, plan, capacity, prefix_blocks):
    pool_dev = pool.shape[0]
    shapes = [
        jax.ShapeDtypeStruct((size,) + pool.shape[1:], pool.dtype)
        for sizes in plan
        for size in sizes
    ]
    return pl.pallas_call(
        functools.partial(gather_kernel, plan, pool_dev, prefix_blocks, capacity),
        out_shape=shapes,
        in_specs=[SMEM] * len(metas) + [HBM],
        out_specs=[HBM] * len(shapes),
        scratch_shapes=[
            pltpu.SMEM((len(metas), capacity + 1), jnp.int32),
            pltpu.SemaphoreType.DMA((len(metas), capacity)),
        ],
        cost_estimate=pl.CostEstimate(
            flops=0,
            bytes_accessed=2 * sum(math.prod(s.shape) for s in shapes) * 2,
            transcendentals=0,
        ),
    )(*metas, pool)


def write_back_kernel(num_blk, prefix_blocks, new_count, block_tok, *refs):
    metas, refs = refs[:num_blk], refs[num_blk:]
    pool_ref, new_ref, refs = refs[0], refs[1], refs[2:]
    fresh, out_ref, sems, last = refs[: num_blk - 1], refs[-3], refs[-2], refs[-1]
    pool_dev = pool_ref.shape[0]
    first = lax.axis_index("blk") * pool_dev
    for b in range(pool_dev):
        pltpu.make_async_copy(pool_ref.at[b], out_ref.at[b], sems.at[b]).start()
    for b in range(pool_dev):
        pltpu.make_async_copy(pool_ref.at[b], out_ref.at[b], sems.at[b]).wait()
    for source in range(num_blk):
        for b in range(new_count):
            slot = metas[source][0, prefix_blocks + b] - first

            @pl.when((slot >= 0) & (slot < pool_dev))
            def write():
                for kv in range(2):
                    if source == 0:
                        src = new_ref.at[kv, 0, pl.ds(b * block_tok, block_tok)]
                    else:
                        src = fresh[source - 1].at[kv]
                    copy = pltpu.make_async_copy(src, out_ref.at[slot, kv], last)
                    copy.start()
                    copy.wait()


def write_back(metas, pool, new_kv, fresh, prefix_blocks, new_count):
    num_blk = len(metas)
    return pl.pallas_call(
        functools.partial(write_back_kernel, num_blk, prefix_blocks, new_count, pool.shape[2]),
        out_shape=jax.ShapeDtypeStruct(pool.shape, pool.dtype),
        in_specs=[SMEM] * num_blk + [HBM] * (num_blk + 1),
        out_specs=HBM,
        scratch_shapes=[
            pltpu.SemaphoreType.DMA((pool.shape[0],)),
            pltpu.SemaphoreType.DMA,
        ],
        cost_estimate=pl.CostEstimate(
            flops=0, bytes_accessed=4 * math.prod(pool.shape), transcendentals=0
        ),
    )(*metas, pool, new_kv, *fresh)


def attend_kernel(
    sizes, kv_dev, group, block_tok, rows, first, final, valid_ref, q_ref, *refs
):
    parts, refs = refs[: len(sizes)], refs[len(sizes) :]
    if first:
        new_ref, refs = refs[0], refs[1:]
    else:
        acc_in, stat_in, refs = refs[0], refs[1], refs[2:]
    if final:
        out_ref, refs = refs[0], refs[1:]
    else:
        acc_out, stat_out, refs = refs[0], refs[1], refs[2:]
    key_ref, value_ref, stage_ref = refs
    tile = pl.program_id(0)
    tile_tok, heads_dev, head_dim = q_ref.shape
    factor = head_dim**-0.5 * math.log2(math.e)
    prefix_keys = sum(sizes) * block_tok
    suffix = new_ref.shape[1] // kv_dev if first else 0
    keys = prefix_keys + suffix

    def unpack(raw, kv, at, length):
        target = key_ref if kv == 0 else value_ref
        if kv_dev == 1:
            target[0, pl.ds(at, length), pl.ds(0, head_dim)] = raw
            return
        stage_ref[...] = raw.astype(jnp.float32)
        for h in range(kv_dev):
            target[h, pl.ds(at, length), pl.ds(0, head_dim)] = stage_ref[
                pl.ds(h, length, stride=kv_dev), :
            ].astype(jnp.bfloat16)

    @pl.when(tile == 0)
    def prepare():
        value_ref[:, :, head_dim:] = jnp.ones(
            (kv_dev, keys, value_ref.shape[2] - head_dim), jnp.bfloat16
        )
        base = 0
        for part, size in zip(parts, sizes):

            def block(b, carry, part=part, base=base):
                at = pl.multiple_of(base + b * block_tok, block_tok)
                for kv in range(2):
                    unpack(part[b, kv], kv, at, block_tok)
                return carry

            lax.fori_loop(0, size, block, 0)
            base += size * block_tok
        for piece in range(suffix // block_tok):
            for kv in range(2):
                unpack(
                    new_ref[kv, pl.ds(piece * block_tok * kv_dev, block_tok * kv_dev), :],
                    kv,
                    base + piece * block_tok,
                    block_tok,
                )

    def run(masked):
        tok_rows = rows // group

        def sub(index, carry):
            tok = pl.multiple_of(index * tok_rows, tok_rows)
            q_all = q_ref[pl.ds(tok, tok_rows)].astype(jnp.float32)
            results = []
            for h in range(kv_dev):
                q = (
                    q_all[:, h * group : (h + 1) * group, :]
                    .reshape(rows, head_dim)
                    .astype(jnp.bfloat16)
                )
                scores = (
                    lax.dot_general(
                        q, key_ref[h], (((1,), (1,)), ((), ())), preferred_element_type=jnp.float32
                    )
                    * factor
                )
                if masked or first:
                    column = lax.broadcasted_iota(jnp.int32, (1, keys), 1)
                    allowed = jnp.zeros((1, keys), jnp.bool_)
                    base = 0
                    for i, size in enumerate(sizes):
                        allowed |= (column >= base) & (
                            column < base + jnp.minimum(valid_ref[0, i], size) * block_tok
                        )
                        base += size * block_tok
                    if first:
                        place = (
                            lax.broadcasted_iota(jnp.int32, (rows, 1), 0) // group
                            + tok
                            + tile * tile_tok
                        )
                        limit = place + prefix_keys
                        allowed = allowed | ((column >= prefix_keys) & (column <= limit))
                    scores = jnp.where(allowed, scores, -jnp.inf)
                peak = jnp.max(scores, axis=1, keepdims=True)
                at = pl.ds(pl.multiple_of(index * rows, rows), rows)
                if not first:
                    old = stat_in[h, at, 0:1]
                    old_total = stat_in[h, at, head_dim // 2 : head_dim // 2 + 1]
                    peak = jnp.maximum(peak, old)
                weights = jnp.exp2(scores - peak).astype(jnp.bfloat16)
                both = jnp.dot(weights, value_ref[h], preferred_element_type=jnp.float32)
                summed = both[:, :head_dim]
                total = both[:, head_dim:]
                if not first:
                    shrink = jnp.exp2(old - peak)
                    summed += acc_in[h, at, :] * shrink
                    total += old_total * shrink
                if final:
                    results.append((summed / total).reshape(tok_rows, group, head_dim))
                else:
                    acc_out[h, at, :] = summed
                    lane = lax.broadcasted_iota(jnp.int32, (rows, head_dim), 1)
                    stat_out[h, at, :] = jnp.where(lane < head_dim // 2, peak, total)
            if final:
                out_ref[pl.ds(tok, tok_rows)] = jnp.concatenate(results, axis=1).astype(
                    jnp.bfloat16
                )
            return carry

        lax.fori_loop(0, tile_tok // tok_rows, sub, 0)

    if first:
        run(True)
    else:
        full = valid_ref[0, 0] >= sizes[0]
        for i in range(1, len(sizes)):
            full = full & (valid_ref[0, i] >= sizes[i])

        @pl.when(full)
        def unmasked():
            run(False)

        @pl.when(jnp.logical_not(full))
        def masked():
            run(True)


def attend(valid, queries, parts, new_kv, state, final):
    suffix, heads_dev, head_dim = queries.shape
    kv_dev = parts[0].shape[3]
    block_tok = parts[0].shape[2]
    group = heads_dev // kv_dev
    sizes = tuple(part.shape[0] for part in parts)
    first = state is None
    tile_tok = min(suffix, 64)
    rows = min(256, tile_tok * group)
    keys = sum(sizes) * block_tok + (suffix if first else 0)
    raw = [part.reshape(part.shape[0], 2, block_tok * kv_dev, head_dim) for part in parts]
    whole = pl.BlockSpec(memory_space=pltpu.VMEM)
    q_spec = pl.BlockSpec((tile_tok, heads_dev, head_dim), lambda t: (t, 0, 0))
    state_spec = pl.BlockSpec((kv_dev, tile_tok * group, head_dim), lambda t: (0, t, 0))
    state_shape = jax.ShapeDtypeStruct((kv_dev, suffix * group, head_dim), jnp.float32)
    if first:
        extra, extra_specs = [new_kv.reshape(2, suffix * kv_dev, head_dim)], [whole]
    else:
        extra, extra_specs = list(state), [state_spec] * 2
    if final:
        out_shape = jax.ShapeDtypeStruct(queries.shape, queries.dtype)
        out_specs = q_spec
    else:
        out_shape = [state_shape] * 2
        out_specs = [state_spec] * 2
    return pl.pallas_call(
        functools.partial(
            attend_kernel, sizes, kv_dev, group, block_tok, rows, first, final
        ),
        out_shape=out_shape,
        grid=(suffix // tile_tok,),
        in_specs=[SMEM, q_spec] + [whole] * len(raw) + extra_specs,
        out_specs=out_specs,
        scratch_shapes=[
            pltpu.VMEM((kv_dev, keys, head_dim), jnp.bfloat16),
            pltpu.VMEM((kv_dev, keys, 2 * head_dim), jnp.bfloat16),
            pltpu.VMEM((block_tok * kv_dev, head_dim), jnp.float32),
        ],
        compiler_params=pltpu.CompilerParams(vmem_limit_bytes=VMEM_LIMIT),
        cost_estimate=pl.CostEstimate(
            flops=4 * suffix * heads_dev * keys * head_dim,
            bytes_accessed=keys * kv_dev * head_dim * 4 + 16 * suffix * heads_dev * head_dim,
            transcendentals=suffix * heads_dev * keys,
        ),
    )(valid, queries, *raw, *extra)


def per_device(
    queries, new_kv, pool, prefix_slot, prefix_owner, prefix_len, write_slot, write_owner
):
    num_blk = lax.axis_size("blk")
    me = lax.axis_index("blk")
    pool_dev, block_tok = pool.shape[0], pool.shape[2]
    prefix_blocks = prefix_slot.shape[1]
    new_count = write_slot.shape[1]
    capacity = max(2, (prefix_blocks + num_blk - 1) // num_blk)

    def shift(array, d):
        return lax.ppermute(array, "blk", [(i, (i + d) % num_blk) for i in range(num_blk)])

    meta = jnp.concatenate(
        [prefix_owner * pool_dev + prefix_slot, write_owner * pool_dev + write_slot], axis=1
    )
    metas = [meta] + [shift(meta, num_blk - d) for d in range(1, num_blk)]

    fresh_shape = jax.ShapeDtypeStruct((2,) + pool.shape[2:], pool.dtype)
    fresh_out = pl.pallas_call(
        functools.partial(pick_fresh_kernel, num_blk, block_tok),
        out_shape=[fresh_shape] * (num_blk - 1),
        in_specs=[SMEM, HBM],
        out_specs=[HBM] * (num_blk - 1),
        scratch_shapes=[pltpu.SemaphoreType.DMA((num_blk - 1, 2))],
    )(write_owner, new_kv)
    arrived_fresh = {d: shift(fresh_out[d - 1], d) for d in range(1, num_blk)}

    half = capacity // 2
    sizes = (half, capacity - half)
    outgoing = gather(metas[1:], pool, (sizes,) * (num_blk - 1), capacity, prefix_blocks)
    order = sorted(range(1, num_blk), key=lambda d: -min(d, num_blk - d))
    arrived = {}
    for c in range(len(sizes)):
        for d in order:
            arrived[c, d] = shift(outgoing[(d - 1) * len(sizes) + c], d)

    places = jnp.arange(prefix_blocks, dtype=jnp.int32)[None, :]
    sources = lax.rem(me - jnp.arange(num_blk, dtype=jnp.int32) + num_blk, num_blk)[:, None]
    counted = jnp.sum(
        ((prefix_owner == sources) & (places < prefix_len[:, None])).astype(jnp.int32), axis=1
    )

    def valid(keys):
        return jnp.stack([counted[d] - sum(sizes[:c]) for c, d in keys])[None, :]

    (local,) = gather(metas[:1], pool, ((capacity,),), capacity, prefix_blocks)
    state = attend(counted[0][None, None], queries[0], [local], new_kv, None, False)
    new_pool = write_back(
        metas,
        pool,
        new_kv,
        [arrived_fresh[num_blk - d] for d in range(1, num_blk)],
        prefix_blocks,
        new_count,
    )
    calls = []
    for c in range(len(sizes)):
        calls.append([(c, order[0])])
        rest = [(c, d) for d in order[1:]]
        calls += [rest[i : i + 4] for i in range(0, len(rest), 4)]
    calls = [call for call in calls if call]
    for i, call in enumerate(calls):
        state = attend(
            valid(call), queries[0], [arrived[k] for k in call], None, state, i == len(calls) - 1
        )
    return state[None], new_pool


def solution(mesh):
    in_specs = (
        P(("group", "blk"), None, "tensor", None),
        P(None, ("group", "blk"), None, "tensor", None),
        P(("group", "blk"), None, None, "tensor", None),
        P(("group", "blk"), None),
        P(("group", "blk"), None),
        P(("group", "blk")),
        P(("group", "blk"), None),
        P(("group", "blk"), None),
    )
    out_specs = (
        P(("group", "blk"), None, "tensor", None),
        P(("group", "blk"), None, None, "tensor", None),
    )
    return jax.shard_map(
        per_device, mesh=mesh, in_specs=in_specs, out_specs=out_specs, check_vma=False
    )
```

```python
import functools
import math

import jax
import jax.numpy as jnp
from jax import lax
from jax.experimental import pallas as pl
from jax.experimental.pallas import tpu as pltpu
from jax.sharding import PartitionSpec as P

ANY = pl.BlockSpec(memory_space=pl.ANY)
HBM = pl.BlockSpec(memory_space=pltpu.HBM)
SMEM = pl.BlockSpec(memory_space=pltpu.SMEM)
VMEM = pl.BlockSpec(memory_space=pltpu.VMEM)
WHOLE_LIMIT = 60 * 1024 * 1024
VMEM_LIMIT = 16 * 1024 * 1024
ATTEND_LIMIT = 32 * 1024 * 1024
QUERY_ROWS = 1024
LEVELS = (3, 2, 2, 1)


def prepare_kernel(capacity, *refs):
    sources, refs = refs[:5], refs[5:]
    num_blk = refs[0].shape[1] // 2
    count_ref, asked, refs = refs[0], refs[1 : 1 + num_blk], refs[1 + num_blk :]
    held, (table_ref, used_ref, counted_ref, load_sems) = refs[:5], refs[5:]
    loads = [
        pltpu.make_async_copy(source, target, load_sems.at[i])
        for i, (source, target) in enumerate(zip(sources, held))
    ]
    for load in loads:
        load.start()
    slot_ref, owner_ref, len_ref, write_slot_ref, write_owner_ref = held
    me = lax.axis_index("blk")
    for owner in range(num_blk):
        used_ref[owner] = 0
        counted_ref[owner] = 0
        for k in range(capacity):
            table_ref[owner, k] = 0
    for load in loads:
        load.wait()

    def step(j, carry):
        owner = owner_ref[0, j]
        place = used_ref[owner]
        table_ref[owner, jnp.minimum(place, capacity)] = slot_ref[0, j]
        used_ref[owner] = place + 1
        counted_ref[owner] += jnp.where(j < len_ref[0], 1, 0)
        return carry

    lax.fori_loop(0, owner_ref.shape[1], step, 0, unroll=8)
    for d in range(num_blk):
        owner = lax.rem(me + d, num_blk)
        count_ref[0, d] = counted_ref[owner]
        for k in range(capacity):
            asked[d][0, k] = table_ref[owner, k]
        slot = jnp.int32(-1)
        chosen = jnp.int32(0)
        for b in range(write_owner_ref.shape[1]):
            goes = write_owner_ref[0, b] == owner
            slot = jnp.where(goes, write_slot_ref[0, b], slot)
            chosen = jnp.where(goes, b, chosen)
        asked[d][0, capacity] = slot
        count_ref[0, num_blk + d] = chosen


def prepare(prefix_slot, prefix_owner, prefix_len, write_slot, write_owner, capacity, num_blk):
    operands = (prefix_slot, prefix_owner, prefix_len, write_slot, write_owner)
    row = jax.ShapeDtypeStruct((1, capacity + 1), jnp.int32)
    results = pl.pallas_call(
        functools.partial(prepare_kernel, capacity),
        out_shape=[jax.ShapeDtypeStruct((1, 2 * num_blk), jnp.int32)] + [row] * num_blk,
        in_specs=[HBM] * 5,
        out_specs=[SMEM] * (num_blk + 1),
        scratch_shapes=[pltpu.SMEM(operand.shape, operand.dtype) for operand in operands]
        + [
            pltpu.SMEM((num_blk, capacity + 1), jnp.int32),
            pltpu.SMEM((num_blk,), jnp.int32),
            pltpu.SMEM((num_blk,), jnp.int32),
            pltpu.SemaphoreType.DMA((5,)),
        ],
        compiler_params=pltpu.CompilerParams(vmem_limit_bytes=WHOLE_LIMIT),
    )(*operands)
    return results[0], results[1:]


def pick_fresh_kernel(num_blk, block_rows, count_ref, new_ref, *refs):
    fresh, (held, load_sem, sems) = refs[: num_blk - 1], refs[num_blk - 1 :]
    load = pltpu.make_async_copy(new_ref, held, load_sem)
    load.start()
    load.wait()
    copies = []
    for d in range(1, num_blk):
        chosen = count_ref[0, num_blk + d]
        at = pl.ds(pl.multiple_of(chosen * block_rows, block_rows), block_rows)
        copies.append(pltpu.make_async_copy(held.at[:, at], fresh[d - 1], sems.at[d - 1]))
    for copy in copies:
        copy.start()
    for copy in copies:
        copy.wait()


def pick_fresh(counts, new_rows, block_rows, num_blk):
    shape = jax.ShapeDtypeStruct((2, block_rows, new_rows.shape[2]), new_rows.dtype)
    return pl.pallas_call(
        functools.partial(pick_fresh_kernel, num_blk, block_rows),
        out_shape=[shape] * (num_blk - 1),
        in_specs=[SMEM, HBM],
        out_specs=[HBM] * (num_blk - 1),
        scratch_shapes=[
            pltpu.VMEM(new_rows.shape, new_rows.dtype),
            pltpu.SemaphoreType.DMA,
            pltpu.SemaphoreType.DMA((num_blk - 1,)),
        ],
        compiler_params=pltpu.CompilerParams(vmem_limit_bytes=VMEM_LIMIT),
    )(counts, new_rows)


def gather_kernel(plan, count, *refs):
    asked, pool_ref, refs = refs[:count], refs[count], refs[-len(plan) - 3 :]
    outs, held, in_sems, out_sems = refs[:-3], refs[-3], refs[-2], refs[-1]
    moves = []
    for (row, start, size), out in zip(plan, outs):
        for place in range(size):
            i = len(moves)
            load = pltpu.make_async_copy(
                pool_ref.at[asked[row][0, start + place]], held.at[i], in_sems.at[i]
            )
            moves.append((load, pltpu.make_async_copy(held.at[i], out.at[place], out_sems.at[i])))
            load.start()
    for load, store in moves:
        load.wait()
        store.start()
    for load, store in moves:
        store.wait()


def gather(asked, pool, plan, after=()):
    shapes = [jax.ShapeDtypeStruct((size,) + pool.shape[1:], pool.dtype) for _, _, size in plan]
    blocks = sum(size for _, _, size in plan)
    return pl.pallas_call(
        functools.partial(gather_kernel, plan, len(asked)),
        out_shape=shapes,
        in_specs=[SMEM] * len(asked) + [HBM] + [ANY] * len(after),
        out_specs=[HBM] * len(shapes),
        scratch_shapes=[
            pltpu.VMEM((blocks,) + pool.shape[1:], pool.dtype),
            pltpu.SemaphoreType.DMA((blocks,)),
            pltpu.SemaphoreType.DMA((blocks,)),
        ],
        compiler_params=pltpu.CompilerParams(vmem_limit_bytes=VMEM_LIMIT),
        cost_estimate=pl.CostEstimate(
            flops=0, bytes_accessed=4 * blocks * math.prod(pool.shape[1:]), transcendentals=0
        ),
    )(*asked, pool, *after)


def write_back_kernel(capacity, block_rows, count, owner_ref, slot_ref, *refs):
    asked, refs = refs[:count], refs[count:]
    pool_ref, new_ref, refs = refs[0], refs[1], refs[2:]
    fresh, (out_ref, held, sems, last) = refs[:count], refs[-4:]
    me = lax.axis_index("blk")
    blocks = range(pool_ref.shape[0])
    loads = [pltpu.make_async_copy(pool_ref.at[b], held.at[b], sems.at[b]) for b in blocks]
    stores = [pltpu.make_async_copy(held.at[b], out_ref.at[b], sems.at[b]) for b in blocks]
    for load in loads:
        load.start()
    for load in loads:
        load.wait()

    def put(wanted, src, slot):
        @pl.when(wanted)
        def write():
            copy = pltpu.make_async_copy(src, held.at[slot], last)
            copy.start()
            copy.wait()

    for i in range(count):
        slot = asked[i][0, capacity]
        put(slot >= 0, fresh[i], slot)
    for b in range(owner_ref.shape[1]):
        rows = pl.ds(b * block_rows, block_rows)
        put(owner_ref[0, b] == me, new_ref.at[:, rows], slot_ref[0, b])
    for store in stores:
        store.start()
    for store in stores:
        store.wait()


def write_back(write_owner, write_slot, asked, pool, new_rows, fresh, capacity, after):
    count = len(asked)
    return pl.pallas_call(
        functools.partial(write_back_kernel, capacity, pool.shape[2], count),
        out_shape=jax.ShapeDtypeStruct(pool.shape, pool.dtype),
        in_specs=[SMEM] * (count + 2) + [HBM] * (count + 2) + [ANY] * len(after),
        out_specs=HBM,
        scratch_shapes=[
            pltpu.VMEM(pool.shape, pool.dtype),
            pltpu.SemaphoreType.DMA((pool.shape[0],)),
            pltpu.SemaphoreType.DMA,
        ],
        compiler_params=pltpu.CompilerParams(vmem_limit_bytes=VMEM_LIMIT),
        cost_estimate=pl.CostEstimate(
            flops=0, bytes_accessed=4 * math.prod(pool.shape), transcendentals=0
        ),
    )(write_owner, write_slot, *asked, pool, new_rows, *fresh, *after)


def attend_kernel(spans, kv_dev, group, block_tok, rows, first, final, count_ref, q_ref, *refs):
    parts, refs = refs[: len(spans)], refs[len(spans) :]
    if first:
        new_ref, q_out, acc_out, stat_out = refs[:4]
        head_dim = q_ref.shape[2]
        suffix = new_ref.shape[1] // kv_dev
    else:
        acc_in, stat_in = refs[:2]
        head_dim = q_ref.shape[2]
        suffix = 0
        if final:
            out_ref = refs[2]
        else:
            acc_out, stat_out = refs[2:4]
    key_ref, value_ref, stage_ref = refs[-3:]
    factor = head_dim**-0.5 * math.log2(math.e)
    prefix_keys = sum(size for _, _, size in spans) * block_tok
    keys = prefix_keys + suffix

    def unpack(raw, kv, at):
        stage_ref[...] = raw.astype(jnp.float32)
        for h in range(kv_dev):
            head = stage_ref[pl.ds(h, block_tok, stride=kv_dev), :]
            if kv == 0:
                key_ref[h, pl.ds(at, block_tok)] = head.astype(jnp.bfloat16)
            else:
                value_ref[h, :head_dim, pl.ds(at, block_tok)] = head.T.astype(jnp.bfloat16)

    value_ref[:, head_dim:, :] = jnp.ones(
        (kv_dev, value_ref.shape[1] - head_dim, keys), jnp.bfloat16
    )
    base = 0
    for part, (_, _, size) in zip(parts, spans):
        for b in range(size):
            for kv in range(2):
                unpack(part[b, kv], kv, base + b * block_tok)
        base += size * block_tok
    for piece in range(suffix // block_tok):
        for kv in range(2):
            raw = new_ref[kv, pl.ds(piece * block_tok * kv_dev, block_tok * kv_dev), :]
            unpack(raw, kv, base + piece * block_tok)

    if first:
        for h in range(kv_dev):
            heads = q_ref[...].astype(jnp.float32)[:, h * group : (h + 1) * group, :]
            q_out[h] = heads.reshape(-1, head_dim).astype(jnp.bfloat16)
        q_rows = q_out
    else:
        q_rows = q_ref

    def run(masked):
        def product(start, stop, h, at):
            return lax.dot_general(
                key_ref[h, start:stop],
                q_rows[h, at],
                (((1,), (1,)), ((), ())),
                preferred_element_type=jnp.float32,
            )

        def sub(index, carry):
            at = pl.ds(pl.multiple_of(index * rows, rows), rows)
            results = []
            for h in range(kv_dev):
                pieces = []
                if spans:
                    scores = product(0, prefix_keys, h, at)
                    if masked:
                        place = lax.broadcasted_iota(jnp.int32, (prefix_keys, 1), 0)
                        allowed = jnp.zeros((prefix_keys, 1), jnp.bool_)
                        base = 0
                        for row, start, size in spans:
                            end = base + jnp.minimum(count_ref[0, row] - start, size) * block_tok
                            allowed |= (place >= base) & (place < end)
                            base += size * block_tok
                        scores = jnp.where(allowed, scores, -jnp.inf)
                    pieces.append((scores, 0))
                if first:
                    scores = product(prefix_keys, keys, h, at)
                    token = lax.broadcasted_iota(jnp.int32, (1, rows), 1) + index * rows
                    place = lax.broadcasted_iota(jnp.int32, (suffix, rows), 0)
                    scores = jnp.where(place * group <= token, scores, -jnp.inf)
                    pieces.append((scores, prefix_keys))
                peak = factor * functools.reduce(
                    jnp.maximum, [jnp.max(scores, axis=0, keepdims=True) for scores, _ in pieces]
                )
                if not first:
                    old = stat_in[h, 0:1, at]
                    peak = jnp.maximum(peak, old)
                both = sum(
                    jnp.dot(
                        value_ref[h, :, start : start + scores.shape[0]],
                        jnp.exp2(scores * factor - peak).astype(jnp.bfloat16),
                        preferred_element_type=jnp.float32,
                    )
                    for scores, start in pieces
                )
                summed = both[:head_dim]
                total = both[head_dim : head_dim + 1]
                if not first:
                    shrink = jnp.exp2(old - peak)
                    summed += acc_in[h, :, at] * shrink
                    total += stat_in[h, 1:2, at] * shrink
                if final:
                    results.append((summed / total).T.reshape(rows // group, group, head_dim))
                else:
                    acc_out[h, :, at] = summed
                    stat_out[h, 0:1, at] = peak
                    stat_out[h, 1:2, at] = total
            if final:
                tok = pl.multiple_of(index * (rows // group), rows // group)
                out_ref[pl.ds(tok, rows // group)] = jnp.concatenate(results, axis=1).astype(
                    jnp.bfloat16
                )
            return carry

        lax.fori_loop(0, q_rows.shape[1] // rows, sub, 0)

    full = functools.reduce(
        jnp.logical_and, [count_ref[0, row] >= start + size for row, start, size in spans]
    )

    @pl.when(full)
    def unmasked():
        run(False)

    @pl.when(jnp.logical_not(full))
    def masked():
        run(True)


def attend(counts, queries, parts, spans, kv_dev, block_tok, new_rows, state, final):
    suffix, heads_dev, head_dim = queries.shape
    group = heads_dev // kv_dev
    first = state is None
    rows = min(QUERY_ROWS, suffix * group)
    keys = sum(size for _, _, size in spans) * block_tok + (suffix if first else 0)
    state_shape = [
        jax.ShapeDtypeStruct((kv_dev, suffix * group, head_dim), jnp.bfloat16),
        jax.ShapeDtypeStruct((kv_dev, head_dim, suffix * group), jnp.float32),
        jax.ShapeDtypeStruct((kv_dev, 8, suffix * group), jnp.float32),
    ]
    if first:
        operands = [queries, *parts, new_rows]
        out_shape = state_shape
    else:
        operands = [state[0], *parts, *state[1:]]
        out_shape = jax.ShapeDtypeStruct(queries.shape, queries.dtype) if final else state_shape[1:]
    result = pl.pallas_call(
        functools.partial(attend_kernel, spans, kv_dev, group, block_tok, rows, first, final),
        out_shape=out_shape,
        in_specs=[SMEM] + [VMEM] * len(operands),
        out_specs=VMEM if final else [VMEM] * len(out_shape),
        scratch_shapes=[
            pltpu.VMEM((kv_dev, keys, head_dim), jnp.bfloat16),
            pltpu.VMEM((kv_dev, head_dim + 16, keys), jnp.bfloat16),
            pltpu.VMEM((block_tok * kv_dev, head_dim), jnp.float32),
        ],
        compiler_params=pltpu.CompilerParams(vmem_limit_bytes=ATTEND_LIMIT),
        cost_estimate=pl.CostEstimate(
            flops=4 * suffix * heads_dev * keys * head_dim,
            bytes_accessed=keys * kv_dev * head_dim * 4 + 16 * suffix * heads_dev * head_dim,
            transcendentals=suffix * heads_dev * keys,
        ),
    )(counts, *operands)
    if first or final:
        return result
    return [state[0], *result]


def per_device(
    queries, new_kv, pool, prefix_slot, prefix_owner, prefix_len, write_slot, write_owner
):
    num_blk = lax.axis_size("blk")
    pool_dev, _, block_tok, kv_dev, head_dim = pool.shape
    suffix = queries.shape[1]
    prefix_blocks = prefix_slot.shape[1]
    capacity = max(2, (prefix_blocks + num_blk - 1) // num_blk)
    shifts = sorted(range(1, num_blk), key=lambda d: -min(d, num_blk - d))
    pool_rows = pool.reshape(pool_dev, 2, block_tok * kv_dev, head_dim)
    new_rows = new_kv.reshape(2, suffix * kv_dev, head_dim)

    def shift(array, d):
        return lax.ppermute(array, "blk", [(i, (i + d) % num_blk) for i in range(num_blk)])

    counts, asks = prepare(
        prefix_slot, prefix_owner, prefix_len, write_slot, write_owner, capacity, num_blk
    )
    asked = {d: shift(asks[d], d) for d in shifts}
    fresh = pick_fresh(counts, new_rows, block_tok * kv_dev, num_blk)
    arrived_fresh = {d: shift(fresh[d - 1], d) for d in shifts}

    levels = []
    left = capacity
    for size in LEVELS:
        if left:
            levels.append((capacity - left, min(size, left)))
            left -= min(size, left)
    if left:
        levels.append((capacity - left, left))

    arrived = {}

    def send(start, size, after):
        plan = tuple((i, start, size) for i in range(num_blk - 1))
        sent = gather([asked[d] for d in shifts], pool_rows, plan, after)
        for d, blocks in zip(shifts, sent):
            arrived[start, d] = shift(blocks, num_blk - d)
        return sent

    sent = send(*levels[0], ())
    (local,) = gather([asks[0]], pool_rows, ((0, 0, capacity),), sent[:1])
    state = attend(
        counts,
        queries[0],
        [local],
        ((0, 0, capacity),),
        kv_dev,
        block_tok,
        new_rows,
        None,
        False,
    )
    for i, (start, size) in enumerate(levels):
        if i + 1 < len(levels):
            send(*levels[i + 1], state[2:])
        for at in range(0, len(shifts), 4):
            spans = tuple((d, start, size) for d in shifts[at : at + 4])
            state = attend(
                counts,
                queries[0],
                [arrived[start, d] for d, _, _ in spans],
                spans,
                kv_dev,
                block_tok,
                None,
                state,
                i == len(levels) - 1 and at + 4 >= len(shifts),
            )
        if i == 0:
            new_pool = write_back(
                write_owner,
                write_slot,
                [asked[d] for d in shifts],
                pool_rows,
                new_rows,
                [arrived_fresh[d] for d in shifts],
                capacity,
                state[2:],
            )
    return state[None], new_pool.reshape(pool.shape)


def solution(mesh):
    in_specs = (
        P(("group", "blk"), None, "tensor", None),
        P(None, ("group", "blk"), None, "tensor", None),
        P(("group", "blk"), None, None, "tensor", None),
        P(("group", "blk"), None),
        P(("group", "blk"), None),
        P(("group", "blk")),
        P(("group", "blk"), None),
        P(("group", "blk"), None),
    )
    out_specs = (
        P(("group", "blk"), None, "tensor", None),
        P(("group", "blk"), None, None, "tensor", None),
    )
    return jax.shard_map(
        per_device, mesh=mesh, in_specs=in_specs, out_specs=out_specs, check_vma=False
    )
```

```python
import functools
import math

import jax
import jax.numpy as jnp
from jax import lax
from jax.experimental import pallas as pl
from jax.experimental.pallas import tpu as pltpu
from jax.sharding import PartitionSpec as P

ANY = pl.BlockSpec(memory_space=pl.ANY)
HBM = pl.BlockSpec(memory_space=pltpu.HBM)
SMEM = pl.BlockSpec(memory_space=pltpu.SMEM)
VMEM = pl.BlockSpec(memory_space=pltpu.VMEM)
WHOLE_LIMIT = 60 * 1024 * 1024
VMEM_LIMIT = 16 * 1024 * 1024
ATTEND_LIMIT = 32 * 1024 * 1024
QUERY_ROWS = 1024


def prepare_kernel(capacity, *refs):
    sources, refs = refs[:5], refs[5:]
    num_blk = refs[0].shape[1] // 2
    count_ref, asked, refs = refs[0], refs[1 : 1 + num_blk], refs[1 + num_blk :]
    held, (table_ref, used_ref, counted_ref, load_sems) = refs[:5], refs[5:]
    loads = [
        pltpu.make_async_copy(source, target, load_sems.at[i])
        for i, (source, target) in enumerate(zip(sources, held))
    ]
    for load in loads:
        load.start()
    slot_ref, owner_ref, len_ref, write_slot_ref, write_owner_ref = held
    me = lax.axis_index("blk")
    for owner in range(num_blk):
        used_ref[owner] = 0
        counted_ref[owner] = 0
        for k in range(capacity):
            table_ref[owner, k] = 0
    for load in loads:
        load.wait()

    def step(j, carry):
        owner = owner_ref[0, j]
        place = used_ref[owner]
        table_ref[owner, jnp.minimum(place, capacity)] = slot_ref[0, j]
        used_ref[owner] = place + 1
        counted_ref[owner] += jnp.where(j < len_ref[0], 1, 0)
        return carry

    lax.fori_loop(0, owner_ref.shape[1], step, 0, unroll=8)
    for d in range(num_blk):
        owner = lax.rem(me + d, num_blk)
        count_ref[0, d] = counted_ref[owner]
        for k in range(capacity):
            asked[d][0, k] = table_ref[owner, k]
        slot = jnp.int32(-1)
        chosen = jnp.int32(0)
        for b in range(write_owner_ref.shape[1]):
            goes = write_owner_ref[0, b] == owner
            slot = jnp.where(goes, write_slot_ref[0, b], slot)
            chosen = jnp.where(goes, b, chosen)
        asked[d][0, capacity] = slot
        count_ref[0, num_blk + d] = chosen


def prepare(prefix_slot, prefix_owner, prefix_len, write_slot, write_owner, capacity, num_blk):
    operands = (prefix_slot, prefix_owner, prefix_len, write_slot, write_owner)
    row = jax.ShapeDtypeStruct((1, capacity + 1), jnp.int32)
    results = pl.pallas_call(
        functools.partial(prepare_kernel, capacity),
        out_shape=[jax.ShapeDtypeStruct((1, 2 * num_blk), jnp.int32)] + [row] * num_blk,
        in_specs=[HBM] * 5,
        out_specs=[SMEM] * (num_blk + 1),
        scratch_shapes=[pltpu.SMEM(operand.shape, operand.dtype) for operand in operands]
        + [
            pltpu.SMEM((num_blk, capacity + 1), jnp.int32),
            pltpu.SMEM((num_blk,), jnp.int32),
            pltpu.SMEM((num_blk,), jnp.int32),
            pltpu.SemaphoreType.DMA((5,)),
        ],
        compiler_params=pltpu.CompilerParams(vmem_limit_bytes=WHOLE_LIMIT),
    )(*operands)
    return results[0], results[1:]


def gather_kernel(plan, count, block_rows, count_ref, *refs):
    asked, pool_ref, new_ref = refs[:count], refs[count], refs[count + 1]
    outs, sems = refs[-len(plan) - 1 : -1], refs[-1]
    copies = []

    def move(source, target):
        copy = pltpu.make_async_copy(source, target, sems.at[len(copies)])
        copy.start()
        copies.append(copy)

    for (row, start, size, to), out in zip(plan, outs):
        for place in range(size):
            move(pool_ref.at[asked[row][0, start + place]], out.at[place])
        if to is not None:
            chosen = count_ref[0, count_ref.shape[1] // 2 + to]
            at = pl.ds(pl.multiple_of(chosen * block_rows, block_rows), block_rows)
            move(new_ref.at[:, at], out.at[size])
    for copy in copies:
        copy.wait()


def gather(counts, asked, pool, new_rows, plan, after=()):
    sizes = [size + (to is not None) for _, _, size, to in plan]
    return pl.pallas_call(
        functools.partial(gather_kernel, plan, len(asked), pool.shape[2]),
        out_shape=[jax.ShapeDtypeStruct((size,) + pool.shape[1:], pool.dtype) for size in sizes],
        in_specs=[SMEM] * (1 + len(asked)) + [VMEM] * 2 + [ANY] * len(after),
        out_specs=[ANY] * len(plan),
        scratch_shapes=[pltpu.SemaphoreType.DMA((sum(sizes),))],
        compiler_params=pltpu.CompilerParams(vmem_limit_bytes=VMEM_LIMIT),
        cost_estimate=pl.CostEstimate(
            flops=0, bytes_accessed=4 * sum(sizes) * math.prod(pool.shape[1:]), transcendentals=0
        ),
    )(counts, *asked, pool, new_rows, *after)


def write_back_kernel(capacity, block_rows, count, owner_ref, slot_ref, *refs):
    asked, refs = refs[:count], refs[count:]
    pool_ref, new_ref, fresh, refs = refs[0], refs[1], refs[2 : count + 2], refs[count + 2 :]
    out_ref, sems, last = refs
    me = lax.axis_index("blk")
    copies = [
        pltpu.make_async_copy(pool_ref.at[b], out_ref.at[b], sems.at[b])
        for b in range(pool_ref.shape[0])
    ]
    for copy in copies:
        copy.start()
    for copy in copies:
        copy.wait()

    def put(wanted, src, slot):
        @pl.when(wanted)
        def write():
            copy = pltpu.make_async_copy(src, out_ref.at[slot], last)
            copy.start()
            copy.wait()

    for i in range(count):
        slot = asked[i][0, capacity]
        put(slot >= 0, fresh[i].at[fresh[i].shape[0] - 1], slot)
    for b in range(owner_ref.shape[1]):
        rows = pl.ds(b * block_rows, block_rows)
        put(owner_ref[0, b] == me, new_ref.at[:, rows], slot_ref[0, b])


def write_back(write_owner, write_slot, asked, pool, new_rows, fresh, capacity):
    count = len(asked)
    return pl.pallas_call(
        functools.partial(write_back_kernel, capacity, pool.shape[2], count),
        out_shape=jax.ShapeDtypeStruct(pool.shape, pool.dtype),
        in_specs=[SMEM] * (count + 2) + [VMEM] * (count + 2),
        out_specs=ANY,
        scratch_shapes=[
            pltpu.SemaphoreType.DMA((pool.shape[0],)),
            pltpu.SemaphoreType.DMA,
        ],
        compiler_params=pltpu.CompilerParams(vmem_limit_bytes=VMEM_LIMIT),
        cost_estimate=pl.CostEstimate(
            flops=0, bytes_accessed=4 * math.prod(pool.shape), transcendentals=0
        ),
    )(write_owner, write_slot, *asked, pool, new_rows, *fresh)


def attend_kernel(
    spans, relays, kv_dev, group, block_tok, rows, first, final, count_ref, q_ref, *refs
):
    parts, refs = refs[: len(spans)], refs[len(spans) :]
    ins = 1 if first else 2
    outs = 1 if final else 3 if first else 2
    refs = refs[:ins] + refs[ins + relays : ins + relays + outs] + refs[-3:]
    if first:
        new_ref, q_out, acc_out, stat_out = refs[:4]
        head_dim = q_ref.shape[2]
        suffix = new_ref.shape[1] // kv_dev
    else:
        acc_in, stat_in = refs[:2]
        head_dim = q_ref.shape[2]
        suffix = 0
        if final:
            out_ref = refs[2]
        else:
            acc_out, stat_out = refs[2:4]
    key_ref, value_ref, stage_ref = refs[-3:]
    factor = head_dim**-0.5 * math.log2(math.e)
    prefix_keys = sum(size for _, _, size in spans) * block_tok
    keys = prefix_keys + suffix

    def unpack(raw, kv, at):
        stage_ref[...] = raw.astype(jnp.float32)
        for h in range(kv_dev):
            head = stage_ref[pl.ds(h, block_tok, stride=kv_dev), :]
            if kv == 0:
                key_ref[h, pl.ds(at, block_tok)] = head.astype(jnp.bfloat16)
            else:
                value_ref[h, :head_dim, pl.ds(at, block_tok)] = head.T.astype(jnp.bfloat16)

    value_ref[:, head_dim:, :] = jnp.ones(
        (kv_dev, value_ref.shape[1] - head_dim, keys), jnp.bfloat16
    )
    base = 0
    for part, (_, _, size) in zip(parts, spans):
        for b in range(size):
            for kv in range(2):
                unpack(part[b, kv], kv, base + b * block_tok)
        base += size * block_tok
    for piece in range(suffix // block_tok):
        for kv in range(2):
            raw = new_ref[kv, pl.ds(piece * block_tok * kv_dev, block_tok * kv_dev), :]
            unpack(raw, kv, base + piece * block_tok)

    if first:
        for h in range(kv_dev):
            heads = q_ref[...].astype(jnp.float32)[:, h * group : (h + 1) * group, :]
            q_out[h] = heads.reshape(-1, head_dim).astype(jnp.bfloat16)
        q_rows = q_out
    else:
        q_rows = q_ref

    def run(masked):
        def product(start, stop, h, at):
            return lax.dot_general(
                key_ref[h, start:stop],
                q_rows[h, at],
                (((1,), (1,)), ((), ())),
                preferred_element_type=jnp.float32,
            )

        def sub(index, carry):
            at = pl.ds(pl.multiple_of(index * rows, rows), rows)
            results = []
            for h in range(kv_dev):
                pieces = []
                if spans:
                    scores = product(0, prefix_keys, h, at)
                    if masked:
                        place = lax.broadcasted_iota(jnp.int32, (prefix_keys, 1), 0)
                        allowed = jnp.zeros((prefix_keys, 1), jnp.bool_)
                        base = 0
                        for row, start, size in spans:
                            end = base + jnp.minimum(count_ref[0, row] - start, size) * block_tok
                            allowed |= (place >= base) & (place < end)
                            base += size * block_tok
                        scores = jnp.where(allowed, scores, -jnp.inf)
                    pieces.append((scores, 0))
                if first:
                    scores = product(prefix_keys, keys, h, at)
                    token = lax.broadcasted_iota(jnp.int32, (1, rows), 1) + index * rows
                    place = lax.broadcasted_iota(jnp.int32, (suffix, rows), 0)
                    scores = jnp.where(place * group <= token, scores, -jnp.inf)
                    pieces.append((scores, prefix_keys))
                peak = factor * functools.reduce(
                    jnp.maximum, [jnp.max(scores, axis=0, keepdims=True) for scores, _ in pieces]
                )
                if not first:
                    old = stat_in[h, 0:1, at]
                    peak = jnp.maximum(peak, old)
                both = sum(
                    jnp.dot(
                        value_ref[h, :, start : start + scores.shape[0]],
                        jnp.exp2(scores * factor - peak).astype(jnp.bfloat16),
                        preferred_element_type=jnp.float32,
                    )
                    for scores, start in pieces
                )
                summed = both[:head_dim]
                total = both[head_dim : head_dim + 1]
                if not first:
                    shrink = jnp.exp2(old - peak)
                    summed += acc_in[h, :, at] * shrink
                    total += stat_in[h, 1:2, at] * shrink
                if final:
                    results.append((summed / total).T.reshape(rows // group, group, head_dim))
                else:
                    acc_out[h, :, at] = summed
                    stat_out[h, 0:1, at] = peak
                    stat_out[h, 1:2, at] = total
            if final:
                tok = pl.multiple_of(index * (rows // group), rows // group)
                out_ref[pl.ds(tok, rows // group)] = jnp.concatenate(results, axis=1).astype(
                    jnp.bfloat16
                )
            return carry

        lax.fori_loop(0, q_rows.shape[1] // rows, sub, 0)

    full = functools.reduce(
        jnp.logical_and, [count_ref[0, row] >= start + size for row, start, size in spans]
    )

    @pl.when(full)
    def unmasked():
        run(False)

    @pl.when(jnp.logical_not(full))
    def masked():
        run(True)


def attend(
    counts, queries, parts, spans, kv_dev, block_tok, new_rows=None, state=None, final=False, relay=()
):
    suffix, heads_dev, head_dim = queries.shape
    group = heads_dev // kv_dev
    first = state is None
    rows = min(QUERY_ROWS, suffix * group)
    keys = sum(size for _, _, size in spans) * block_tok + (suffix if first else 0)
    state_shape = [
        jax.ShapeDtypeStruct((kv_dev, suffix * group, head_dim), jnp.bfloat16),
        jax.ShapeDtypeStruct((kv_dev, head_dim, suffix * group), jnp.float32),
        jax.ShapeDtypeStruct((kv_dev, 8, suffix * group), jnp.float32),
    ]
    if first:
        operands = [queries, *parts, new_rows]
        out_shape = state_shape
    else:
        operands = [state[0], *parts, *state[1:]]
        out_shape = state_shape[1:]
        if final:
            out_shape = [jax.ShapeDtypeStruct(queries.shape, queries.dtype)]
    result = pl.pallas_call(
        functools.partial(
            attend_kernel, spans, len(relay), kv_dev, group, block_tok, rows, first, final
        ),
        out_shape=out_shape + [jax.ShapeDtypeStruct(x.shape, x.dtype) for x in relay],
        in_specs=[SMEM] + [VMEM] * len(operands) + [ANY] * len(relay),
        out_specs=[VMEM] * len(out_shape) + [ANY] * len(relay),
        input_output_aliases={
            1 + len(operands) + i: len(out_shape) + i for i in range(len(relay))
        },
        scratch_shapes=[
            pltpu.VMEM((kv_dev, keys, head_dim), jnp.bfloat16),
            pltpu.VMEM((kv_dev, head_dim + 16, keys), jnp.bfloat16),
            pltpu.VMEM((block_tok * kv_dev, head_dim), jnp.float32),
        ],
        compiler_params=pltpu.CompilerParams(vmem_limit_bytes=ATTEND_LIMIT),
        cost_estimate=pl.CostEstimate(
            flops=4 * suffix * heads_dev * keys * head_dim,
            bytes_accessed=keys * kv_dev * head_dim * 4 + 16 * suffix * heads_dev * head_dim,
            transcendentals=suffix * heads_dev * keys,
        ),
    )(counts, *operands, *relay)
    step, relayed = result[: len(out_shape)], result[len(out_shape) :]
    return (step if first or final else [state[0], *step]), relayed


def per_device(
    queries, new_kv, pool, prefix_slot, prefix_owner, prefix_len, write_slot, write_owner
):
    num_blk = lax.axis_size("blk")
    pool_dev, _, block_tok, kv_dev, head_dim = pool.shape
    suffix = queries.shape[1]
    prefix_blocks = prefix_slot.shape[1]
    capacity = max(2, (prefix_blocks + num_blk - 1) // num_blk)
    shifts = sorted(range(1, num_blk), key=lambda d: -min(d, num_blk - d))
    pool_rows = pool.reshape(pool_dev, 2, block_tok * kv_dev, head_dim)
    new_rows = new_kv.reshape(2, suffix * kv_dev, head_dim)

    def shift(array, d):
        return lax.ppermute(array, "blk", [(i, (i + d) % num_blk) for i in range(num_blk)])

    counts, asks = prepare(
        prefix_slot, prefix_owner, prefix_len, write_slot, write_owner, capacity, num_blk
    )
    asked = {d: shift(asks[d], d) for d in shifts}
    rows = [asked[d] for d in shifts]

    most, half = 3 * capacity // 4, capacity // 2
    plans = [
        [(d, 0, most if d == shifts[0] else half) for d in shifts],
        [(d, half, capacity - half) for d in shifts[1:]],
        [(shifts[0], most, capacity - most)],
    ]

    def load(plan, first, after=()):
        return gather(
            counts,
            rows,
            pool_rows,
            new_rows,
            tuple(
                (shifts.index(d), start, size, num_blk - d if first else None)
                for d, start, size in plan
            ),
            after,
        )

    def send(plan, blocks):
        return [shift(x, num_blk - d) for (d, _, _), x in zip(plan, blocks)]

    loaded = load(plans[0], True)
    arrived = [send(plans[0], loaded)]
    local = gather(counts, [asks[0]], pool_rows, new_rows, ((0, 0, capacity, None),), loaded[:1])
    step = functools.partial(attend, counts, queries[0], kv_dev=kv_dev, block_tok=block_tok)
    state, _ = step(local, ((0, 0, capacity),), new_rows=new_rows)

    later = load(plans[1] + plans[2], False, [arrived[0][1], state[2]])
    arrived.append(send(plans[1], later[: len(plans[1])]))
    for i, plan in enumerate(plans):
        groups = [slice(at, at + 8) for at in range(0, len(plan), 8)]
        for j, group in enumerate(groups):
            ends = j == len(groups) - 1
            state, relayed = step(
                arrived[i][group],
                tuple(plan[group]),
                state=state,
                final=ends and i == len(plans) - 1,
                relay=later[len(plans[1]) :] if ends and i == 0 else [],
            )
            if relayed:
                arrived.append(send(plans[2], relayed))
    new_pool = write_back(
        write_owner,
        write_slot,
        [asked[num_blk - d] for d in shifts],
        pool_rows,
        new_rows,
        arrived[0],
        capacity,
    )
    return state[0][None], new_pool.reshape(pool.shape)


def solution(mesh):
    in_specs = (
        P(("group", "blk"), None, "tensor", None),
        P(None, ("group", "blk"), None, "tensor", None),
        P(("group", "blk"), None, None, "tensor", None),
        P(("group", "blk"), None),
        P(("group", "blk"), None),
        P(("group", "blk")),
        P(("group", "blk"), None),
        P(("group", "blk"), None),
    )
    out_specs = (
        P(("group", "blk"), None, "tensor", None),
        P(("group", "blk"), None, None, "tensor", None),
    )
    return jax.shard_map(
        per_device, mesh=mesh, in_specs=in_specs, out_specs=out_specs, check_vma=False
    )
```

```python
import functools
import math

import jax
import jax.numpy as jnp
from jax import lax
from jax.experimental import pallas as pl
from jax.experimental.pallas import tpu as pltpu
from jax.sharding import PartitionSpec as P

ANY = pl.BlockSpec(memory_space=pl.ANY)
HBM = pl.BlockSpec(memory_space=pltpu.HBM)
SMEM = pl.BlockSpec(memory_space=pltpu.SMEM)
VMEM = pl.BlockSpec(memory_space=pltpu.VMEM)
WHOLE_LIMIT = 60 * 1024 * 1024
VMEM_LIMIT = 16 * 1024 * 1024
ATTEND_LIMIT = 32 * 1024 * 1024
QUERY_ROWS = 1024


def prepare_kernel(capacity, *refs):
    sources, refs = refs[:5], refs[5:]
    num_blk = refs[0].shape[1] // 2
    count_ref, asked, refs = refs[0], refs[1 : 1 + num_blk], refs[1 + num_blk :]
    held, (table_ref, used_ref, counted_ref, load_sems) = refs[:5], refs[5:]
    loads = [
        pltpu.make_async_copy(source, target, load_sems.at[i])
        for i, (source, target) in enumerate(zip(sources, held))
    ]
    for load in loads:
        load.start()
    slot_ref, owner_ref, len_ref, write_slot_ref, write_owner_ref = held
    me = lax.axis_index("blk")
    for owner in range(num_blk):
        used_ref[owner] = 0
        counted_ref[owner] = 0
        for k in range(capacity):
            table_ref[owner, k] = 0
    for load in loads:
        load.wait()

    def step(j, carry):
        owner = owner_ref[0, j]
        place = used_ref[owner]
        table_ref[owner, jnp.minimum(place, capacity)] = slot_ref[0, j]
        used_ref[owner] = place + 1
        counted_ref[owner] += jnp.where(j < len_ref[0], 1, 0)
        return carry

    lax.fori_loop(0, owner_ref.shape[1], step, 0, unroll=8)
    for d in range(num_blk):
        owner = lax.rem(me + d, num_blk)
        count_ref[0, d] = counted_ref[owner]
        for k in range(capacity):
            asked[d][0, k] = table_ref[owner, k]
        slot = jnp.int32(-1)
        chosen = jnp.int32(0)
        for b in range(write_owner_ref.shape[1]):
            goes = write_owner_ref[0, b] == owner
            slot = jnp.where(goes, write_slot_ref[0, b], slot)
            chosen = jnp.where(goes, b, chosen)
        asked[d][0, capacity] = slot
        count_ref[0, num_blk + d] = chosen


def prepare(prefix_slot, prefix_owner, prefix_len, write_slot, write_owner, capacity, num_blk):
    operands = (prefix_slot, prefix_owner, prefix_len, write_slot, write_owner)
    row = jax.ShapeDtypeStruct((1, capacity + 1), jnp.int32)
    results = pl.pallas_call(
        functools.partial(prepare_kernel, capacity),
        out_shape=[jax.ShapeDtypeStruct((1, 2 * num_blk), jnp.int32)] + [row] * num_blk,
        in_specs=[HBM] * 5,
        out_specs=[SMEM] * (num_blk + 1),
        scratch_shapes=[pltpu.SMEM(operand.shape, operand.dtype) for operand in operands]
        + [
            pltpu.SMEM((num_blk, capacity + 1), jnp.int32),
            pltpu.SMEM((num_blk,), jnp.int32),
            pltpu.SMEM((num_blk,), jnp.int32),
            pltpu.SemaphoreType.DMA((5,)),
        ],
        compiler_params=pltpu.CompilerParams(vmem_limit_bytes=WHOLE_LIMIT),
    )(*operands)
    return results[0], results[1:]


def gather_kernel(plan, count, block_rows, direct, count_ref, *refs):
    asked, pool_ref, new_ref = refs[:count], refs[count], refs[count + 1]
    refs = refs[-len(plan) - (1 if direct else 3) :]
    outs, sems = refs[: len(plan)], refs[len(plan)]
    moves = []

    def move(source, target):
        i = len(moves)
        if direct:
            load, store = None, pltpu.make_async_copy(source, target, sems.at[i])
            store.start()
        else:
            held, in_sems = refs[len(plan) + 1 :]
            load = pltpu.make_async_copy(source, held.at[i], in_sems.at[i])
            store = pltpu.make_async_copy(held.at[i], target, sems.at[i])
            load.start()
        moves.append((load, store))

    for (row, start, size, to), out in zip(plan, outs):
        for place in range(size):
            move(pool_ref.at[asked[row][0, start + place]], out.at[place])
        if to is not None:
            chosen = count_ref[0, count_ref.shape[1] // 2 + to]
            at = pl.ds(pl.multiple_of(chosen * block_rows, block_rows), block_rows)
            move(new_ref.at[:, at], out.at[size])
    if not direct:
        for load, store in moves:
            load.wait()
            store.start()
    for _, store in moves:
        store.wait()


def gather(counts, asked, pool, new_rows, plan, after=(), direct=True):
    sizes = [size + (to is not None) for _, _, size, to in plan]
    blocks = sum(size for size in sizes)
    scratch = [pltpu.SemaphoreType.DMA((blocks,))]
    if not direct:
        scratch.append(pltpu.VMEM((blocks,) + pool.shape[1:], pool.dtype))
        scratch.append(pltpu.SemaphoreType.DMA((blocks,)))
    return pl.pallas_call(
        functools.partial(gather_kernel, plan, len(asked), pool.shape[2], direct),
        out_shape=[jax.ShapeDtypeStruct((size,) + pool.shape[1:], pool.dtype) for size in sizes],
        in_specs=[SMEM] * (1 + len(asked)) + [VMEM if direct else HBM] * 2 + [ANY] * len(after),
        out_specs=[ANY if direct else HBM] * len(plan),
        scratch_shapes=scratch,
        compiler_params=pltpu.CompilerParams(
            vmem_limit_bytes=VMEM_LIMIT if direct else WHOLE_LIMIT
        ),
        cost_estimate=pl.CostEstimate(
            flops=0, bytes_accessed=4 * blocks * math.prod(pool.shape[1:]), transcendentals=0
        ),
    )(counts, *asked, pool, new_rows, *after)


def write_back_kernel(capacity, block_rows, count, owner_ref, slot_ref, *refs):
    asked, refs = refs[:count], refs[count:]
    pool_ref, new_ref, fresh, refs = refs[0], refs[1], refs[2 : count + 2], refs[count + 2 :]
    out_ref, sems, last = refs
    me = lax.axis_index("blk")
    copies = [
        pltpu.make_async_copy(pool_ref.at[b], out_ref.at[b], sems.at[b])
        for b in range(pool_ref.shape[0])
    ]
    for copy in copies:
        copy.start()
    for copy in copies:
        copy.wait()

    def put(wanted, src, slot):
        @pl.when(wanted)
        def write():
            copy = pltpu.make_async_copy(src, out_ref.at[slot], last)
            copy.start()
            copy.wait()

    for i in range(count):
        slot = asked[i][0, capacity]
        put(slot >= 0, fresh[i].at[fresh[i].shape[0] - 1], slot)
    for b in range(owner_ref.shape[1]):
        rows = pl.ds(b * block_rows, block_rows)
        put(owner_ref[0, b] == me, new_ref.at[:, rows], slot_ref[0, b])


def write_back(write_owner, write_slot, asked, pool, new_rows, fresh, capacity):
    count = len(asked)
    return pl.pallas_call(
        functools.partial(write_back_kernel, capacity, pool.shape[2], count),
        out_shape=jax.ShapeDtypeStruct(pool.shape, pool.dtype),
        in_specs=[SMEM] * (count + 2) + [VMEM] * (count + 2),
        out_specs=ANY,
        scratch_shapes=[
            pltpu.SemaphoreType.DMA((pool.shape[0],)),
            pltpu.SemaphoreType.DMA,
        ],
        compiler_params=pltpu.CompilerParams(vmem_limit_bytes=VMEM_LIMIT),
        cost_estimate=pl.CostEstimate(
            flops=0, bytes_accessed=4 * math.prod(pool.shape), transcendentals=0
        ),
    )(write_owner, write_slot, *asked, pool, new_rows, *fresh)


def attend_kernel(
    spans, relays, kv_dev, group, block_tok, rows, first, final, count_ref, q_ref, *refs
):
    parts, refs = refs[: len(spans)], refs[len(spans) :]
    ins = 1 if first else 2
    outs = 1 if final else 3 if first else 2
    refs = refs[:ins] + refs[ins + relays : ins + relays + outs] + refs[-3:]
    if first:
        new_ref, q_out, acc_out, stat_out = refs[:4]
        head_dim = q_ref.shape[2]
        suffix = new_ref.shape[1] // kv_dev
    else:
        acc_in, stat_in = refs[:2]
        head_dim = q_ref.shape[2]
        suffix = 0
        if final:
            out_ref = refs[2]
        else:
            acc_out, stat_out = refs[2:4]
    key_ref, value_ref, stage_ref = refs[-3:]
    factor = head_dim**-0.5 * math.log2(math.e)
    prefix_keys = sum(size for _, _, size in spans) * block_tok
    keys = prefix_keys + suffix

    def unpack(raw, kv, at):
        stage_ref[...] = raw.astype(jnp.float32)
        for h in range(kv_dev):
            head = stage_ref[pl.ds(h, block_tok, stride=kv_dev), :]
            if kv == 0:
                key_ref[h, pl.ds(at, block_tok)] = head.astype(jnp.bfloat16)
            else:
                value_ref[h, :head_dim, pl.ds(at, block_tok)] = head.T.astype(jnp.bfloat16)

    value_ref[:, head_dim:, :] = jnp.ones(
        (kv_dev, value_ref.shape[1] - head_dim, keys), jnp.bfloat16
    )
    base = 0
    for part, (_, _, size) in zip(parts, spans):
        for b in range(size):
            for kv in range(2):
                unpack(part[b, kv], kv, base + b * block_tok)
        base += size * block_tok
    for piece in range(suffix // block_tok):
        for kv in range(2):
            raw = new_ref[kv, pl.ds(piece * block_tok * kv_dev, block_tok * kv_dev), :]
            unpack(raw, kv, base + piece * block_tok)

    if first:
        for h in range(kv_dev):
            heads = q_ref[...].astype(jnp.float32)[:, h * group : (h + 1) * group, :]
            q_out[h] = heads.reshape(-1, head_dim).astype(jnp.bfloat16)
        q_rows = q_out
    else:
        q_rows = q_ref

    def run(masked):
        def product(start, stop, h, at):
            return lax.dot_general(
                key_ref[h, start:stop],
                q_rows[h, at],
                (((1,), (1,)), ((), ())),
                preferred_element_type=jnp.float32,
            )

        def sub(index, carry):
            at = pl.ds(pl.multiple_of(index * rows, rows), rows)
            results = []
            for h in range(kv_dev):
                pieces = []
                if spans:
                    scores = product(0, prefix_keys, h, at)
                    if masked:
                        place = lax.broadcasted_iota(jnp.int32, (prefix_keys, 1), 0)
                        allowed = jnp.zeros((prefix_keys, 1), jnp.bool_)
                        base = 0
                        for row, start, size in spans:
                            end = base + jnp.minimum(count_ref[0, row] - start, size) * block_tok
                            allowed |= (place >= base) & (place < end)
                            base += size * block_tok
                        scores = jnp.where(allowed, scores, -jnp.inf)
                    pieces.append((scores, 0))
                if first:
                    scores = product(prefix_keys, keys, h, at)
                    token = lax.broadcasted_iota(jnp.int32, (1, rows), 1) + index * rows
                    place = lax.broadcasted_iota(jnp.int32, (suffix, rows), 0)
                    scores = jnp.where(place * group <= token, scores, -jnp.inf)
                    pieces.append((scores, prefix_keys))
                peak = factor * functools.reduce(
                    jnp.maximum, [jnp.max(scores, axis=0, keepdims=True) for scores, _ in pieces]
                )
                if not first:
                    old = stat_in[h, 0:1, at]
                    peak = jnp.maximum(peak, old)
                both = sum(
                    jnp.dot(
                        value_ref[h, :, start : start + scores.shape[0]],
                        jnp.exp2(scores * factor - peak).astype(jnp.bfloat16),
                        preferred_element_type=jnp.float32,
                    )
                    for scores, start in pieces
                )
                summed = both[:head_dim]
                total = both[head_dim : head_dim + 1]
                if not first:
                    shrink = jnp.exp2(old - peak)
                    summed += acc_in[h, :, at] * shrink
                    total += stat_in[h, 1:2, at] * shrink
                if final:
                    results.append((summed / total).T.reshape(rows // group, group, head_dim))
                else:
                    acc_out[h, :, at] = summed
                    stat_out[h, 0:1, at] = peak
                    stat_out[h, 1:2, at] = total
            if final:
                tok = pl.multiple_of(index * (rows // group), rows // group)
                out_ref[pl.ds(tok, rows // group)] = jnp.concatenate(results, axis=1).astype(
                    jnp.bfloat16
                )
            return carry

        lax.fori_loop(0, q_rows.shape[1] // rows, sub, 0)

    full = functools.reduce(
        jnp.logical_and, [count_ref[0, row] >= start + size for row, start, size in spans]
    )

    @pl.when(full)
    def unmasked():
        run(False)

    @pl.when(jnp.logical_not(full))
    def masked():
        run(True)


def attend(
    counts, queries, parts, spans, kv_dev, block_tok, new_rows=None, state=None, final=False, relay=()
):
    suffix, heads_dev, head_dim = queries.shape
    group = heads_dev // kv_dev
    first = state is None
    rows = min(QUERY_ROWS, suffix * group)
    keys = sum(size for _, _, size in spans) * block_tok + (suffix if first else 0)
    state_shape = [
        jax.ShapeDtypeStruct((kv_dev, suffix * group, head_dim), jnp.bfloat16),
        jax.ShapeDtypeStruct((kv_dev, head_dim, suffix * group), jnp.float32),
        jax.ShapeDtypeStruct((kv_dev, 8, suffix * group), jnp.float32),
    ]
    if first:
        operands = [queries, *parts, new_rows]
        out_shape = state_shape
    else:
        operands = [state[0], *parts, *state[1:]]
        out_shape = state_shape[1:]
        if final:
            out_shape = [jax.ShapeDtypeStruct(queries.shape, queries.dtype)]
    result = pl.pallas_call(
        functools.partial(
            attend_kernel, spans, len(relay), kv_dev, group, block_tok, rows, first, final
        ),
        out_shape=out_shape + [jax.ShapeDtypeStruct(x.shape, x.dtype) for x in relay],
        in_specs=[SMEM] + [VMEM] * len(operands) + [ANY] * len(relay),
        out_specs=[VMEM] * len(out_shape) + [ANY] * len(relay),
        input_output_aliases={
            1 + len(operands) + i: len(out_shape) + i for i in range(len(relay))
        },
        scratch_shapes=[
            pltpu.VMEM((kv_dev, keys, head_dim), jnp.bfloat16),
            pltpu.VMEM((kv_dev, head_dim + 16, keys), jnp.bfloat16),
            pltpu.VMEM((block_tok * kv_dev, head_dim), jnp.float32),
        ],
        compiler_params=pltpu.CompilerParams(vmem_limit_bytes=ATTEND_LIMIT),
        cost_estimate=pl.CostEstimate(
            flops=4 * suffix * heads_dev * keys * head_dim,
            bytes_accessed=keys * kv_dev * head_dim * 4 + 16 * suffix * heads_dev * head_dim,
            transcendentals=suffix * heads_dev * keys,
        ),
    )(counts, *operands, *relay)
    step, relayed = result[: len(out_shape)], result[len(out_shape) :]
    return (step if first or final else [state[0], *step]), relayed


def per_device(
    queries, new_kv, pool, prefix_slot, prefix_owner, prefix_len, write_slot, write_owner
):
    num_blk = lax.axis_size("blk")
    pool_dev, _, block_tok, kv_dev, head_dim = pool.shape
    suffix = queries.shape[1]
    prefix_blocks = prefix_slot.shape[1]
    capacity = max(2, (prefix_blocks + num_blk - 1) // num_blk)
    shifts = sorted(range(1, num_blk), key=lambda d: -min(d, num_blk - d))
    pool_rows = pool.reshape(pool_dev, 2, block_tok * kv_dev, head_dim)
    new_rows = new_kv.reshape(2, suffix * kv_dev, head_dim)

    def shift(array, d):
        return lax.ppermute(array, "blk", [(i, (i + d) % num_blk) for i in range(num_blk)])

    counts, asks = prepare(
        prefix_slot, prefix_owner, prefix_len, write_slot, write_owner, capacity, num_blk
    )
    asked = {d: shift(asks[d], d) for d in shifts}
    rows = [asked[d] for d in shifts]

    first = max(1, 3 * capacity // 8)
    cuts = sorted({0, first, min(2 * first, capacity), capacity - 1, capacity})
    plans = [[(d, start, end - start) for d in shifts] for start, end in zip(cuts, cuts[1:])]

    def load(plan, first, after=()):
        return gather(
            counts,
            rows,
            pool_rows,
            new_rows,
            tuple(
                (shifts.index(d), start, size, num_blk - d if first else None)
                for d, start, size in plan
            ),
            after,
            not first,
        )

    def send(plan, blocks):
        return [shift(x, num_blk - d) for (d, _, _), x in zip(plan, blocks)]

    loaded = load(plans[0], True)
    arrived = [send(plans[0], loaded)]
    local = gather(counts, [asks[0]], pool_rows, new_rows, ((0, 0, capacity, None),), loaded[:1])
    step = functools.partial(attend, counts, queries[0], kv_dev=kv_dev, block_tok=block_tok)
    state, _ = step(local, ((0, 0, capacity),), new_rows=new_rows)

    later = load(sum(plans[1:], []), False, [state[2]])
    waiting = [later[i * len(shifts) : (i + 1) * len(shifts)] for i in range(len(plans) - 1)]
    arrived.append(send(plans[1], waiting[0]))
    for i, plan in enumerate(plans):
        relay = waiting[i + 1] if i + 2 < len(plans) else []
        groups = [slice(at, at + 8) for at in range(0, len(plan), 8)]
        for j, group in enumerate(groups):
            ends = j == len(groups) - 1
            state, relayed = step(
                arrived[i][group],
                tuple(plan[group]),
                state=state,
                final=ends and i == len(plans) - 1,
                relay=relay if ends else [],
            )
        if relay:
            arrived.append(send(plans[i + 2], relayed))
    new_pool = write_back(
        write_owner,
        write_slot,
        [asked[num_blk - d] for d in shifts],
        pool_rows,
        new_rows,
        arrived[0],
        capacity,
    )
    return state[0][None], new_pool.reshape(pool.shape)


def solution(mesh):
    in_specs = (
        P(("group", "blk"), None, "tensor", None),
        P(None, ("group", "blk"), None, "tensor", None),
        P(("group", "blk"), None, None, "tensor", None),
        P(("group", "blk"), None),
        P(("group", "blk"), None),
        P(("group", "blk")),
        P(("group", "blk"), None),
        P(("group", "blk"), None),
    )
    out_specs = (
        P(("group", "blk"), None, "tensor", None),
        P(("group", "blk"), None, None, "tensor", None),
    )
    return jax.shard_map(
        per_device, mesh=mesh, in_specs=in_specs, out_specs=out_specs, check_vma=False
    )
```

```python
import functools
import math

import jax
import jax.numpy as jnp
from jax import lax
from jax.experimental import pallas as pl
from jax.experimental.pallas import tpu as pltpu
from jax.sharding import PartitionSpec as P

ANY = pl.BlockSpec(memory_space=pl.ANY)
HBM = pl.BlockSpec(memory_space=pltpu.HBM)
SMEM = pl.BlockSpec(memory_space=pltpu.SMEM)
VMEM = pl.BlockSpec(memory_space=pltpu.VMEM)
WHOLE_LIMIT = 60 * 1024 * 1024
VMEM_LIMIT = 16 * 1024 * 1024
ATTEND_LIMIT = 32 * 1024 * 1024
QUERY_ROWS = 1024


def prepare_kernel(capacity, *refs):
    sources, refs = refs[:5], refs[5:]
    num_blk = refs[0].shape[1] // 2
    count_ref, asked, refs = refs[0], refs[1 : 1 + num_blk], refs[1 + num_blk :]
    held, (table_ref, used_ref, counted_ref, load_sems) = refs[:5], refs[5:]
    loads = [
        pltpu.make_async_copy(source, target, load_sems.at[i])
        for i, (source, target) in enumerate(zip(sources, held))
    ]
    for load in loads:
        load.start()
    slot_ref, owner_ref, len_ref, write_slot_ref, write_owner_ref = held
    me = lax.axis_index("blk")
    for owner in range(num_blk):
        used_ref[owner] = 0
        counted_ref[owner] = 0
        for k in range(capacity):
            table_ref[owner, k] = 0
    for load in loads:
        load.wait()

    def step(j, carry):
        owner = owner_ref[0, j]
        place = used_ref[owner]
        table_ref[owner, jnp.minimum(place, capacity)] = slot_ref[0, j]
        used_ref[owner] = place + 1
        counted_ref[owner] += jnp.where(j < len_ref[0], 1, 0)
        return carry

    lax.fori_loop(0, owner_ref.shape[1], step, 0, unroll=8)
    for d in range(num_blk):
        owner = lax.rem(me + d, num_blk)
        count_ref[0, d] = counted_ref[owner]
        for k in range(capacity):
            asked[d][0, k] = table_ref[owner, k]
        slot = jnp.int32(-1)
        chosen = jnp.int32(0)
        for b in range(write_owner_ref.shape[1]):
            goes = write_owner_ref[0, b] == owner
            slot = jnp.where(goes, write_slot_ref[0, b], slot)
            chosen = jnp.where(goes, b, chosen)
        asked[d][0, capacity] = slot
        count_ref[0, num_blk + d] = chosen


def prepare(prefix_slot, prefix_owner, prefix_len, write_slot, write_owner, capacity, num_blk):
    operands = (prefix_slot, prefix_owner, prefix_len, write_slot, write_owner)
    row = jax.ShapeDtypeStruct((1, capacity + 1), jnp.int32)
    results = pl.pallas_call(
        functools.partial(prepare_kernel, capacity),
        out_shape=[jax.ShapeDtypeStruct((1, 2 * num_blk), jnp.int32)] + [row] * num_blk,
        in_specs=[HBM] * 5,
        out_specs=[SMEM] * (num_blk + 1),
        scratch_shapes=[pltpu.SMEM(operand.shape, operand.dtype) for operand in operands]
        + [
            pltpu.SMEM((num_blk, capacity + 1), jnp.int32),
            pltpu.SMEM((num_blk,), jnp.int32),
            pltpu.SMEM((num_blk,), jnp.int32),
            pltpu.SemaphoreType.DMA((5,)),
        ],
        compiler_params=pltpu.CompilerParams(vmem_limit_bytes=WHOLE_LIMIT),
    )(*operands)
    return results[0], results[1:]


def gather_kernel(plan, count, block_rows, direct, count_ref, *refs):
    asked, pool_ref, new_ref = refs[:count], refs[count], refs[count + 1]
    refs = refs[-len(plan) - (1 if direct else 3) :]
    outs, sems = refs[: len(plan)], refs[len(plan)]
    moves = []

    def move(source, target):
        i = len(moves)
        if direct:
            load, store = None, pltpu.make_async_copy(source, target, sems.at[i])
            store.start()
        else:
            held, in_sems = refs[len(plan) + 1 :]
            load = pltpu.make_async_copy(source, held.at[i], in_sems.at[i])
            store = pltpu.make_async_copy(held.at[i], target, sems.at[i])
            load.start()
        moves.append((load, store))

    for (row, start, size, to), out in zip(plan, outs):
        for place in range(size):
            move(pool_ref.at[asked[row][0, start + place]], out.at[place])
        if to is not None:
            chosen = count_ref[0, count_ref.shape[1] // 2 + to]
            at = pl.ds(pl.multiple_of(chosen * block_rows, block_rows), block_rows)
            move(new_ref.at[:, at], out.at[size])
    if not direct:
        for load, store in moves:
            load.wait()
            store.start()
    for _, store in moves:
        store.wait()


def gather(counts, asked, pool, new_rows, plan, after=(), direct=True):
    sizes = [size + (to is not None) for _, _, size, to in plan]
    blocks = sum(size for size in sizes)
    scratch = [pltpu.SemaphoreType.DMA((blocks,))]
    if not direct:
        scratch.append(pltpu.VMEM((blocks,) + pool.shape[1:], pool.dtype))
        scratch.append(pltpu.SemaphoreType.DMA((blocks,)))
    return pl.pallas_call(
        functools.partial(gather_kernel, plan, len(asked), pool.shape[2], direct),
        out_shape=[jax.ShapeDtypeStruct((size,) + pool.shape[1:], pool.dtype) for size in sizes],
        in_specs=[SMEM] * (1 + len(asked)) + [VMEM if direct else HBM] * 2 + [ANY] * len(after),
        out_specs=[ANY if direct else HBM] * len(plan),
        scratch_shapes=scratch,
        compiler_params=pltpu.CompilerParams(
            vmem_limit_bytes=VMEM_LIMIT if direct else WHOLE_LIMIT
        ),
        cost_estimate=pl.CostEstimate(
            flops=0, bytes_accessed=4 * blocks * math.prod(pool.shape[1:]), transcendentals=0
        ),
    )(counts, *asked, pool, new_rows, *after)


def write_back_kernel(capacity, block_rows, count, owner_ref, slot_ref, *refs):
    asked, refs = refs[:count], refs[count:]
    pool_ref, new_ref, fresh, refs = refs[0], refs[1], refs[2 : count + 2], refs[count + 2 :]
    out_ref, sems, last = refs
    me = lax.axis_index("blk")
    copies = [
        pltpu.make_async_copy(pool_ref.at[b], out_ref.at[b], sems.at[b])
        for b in range(pool_ref.shape[0])
    ]
    for copy in copies:
        copy.start()
    for copy in copies:
        copy.wait()

    def put(wanted, src, slot):
        @pl.when(wanted)
        def write():
            copy = pltpu.make_async_copy(src, out_ref.at[slot], last)
            copy.start()
            copy.wait()

    for i in range(count):
        slot = asked[i][0, capacity]
        put(slot >= 0, fresh[i].at[fresh[i].shape[0] - 1], slot)
    for b in range(owner_ref.shape[1]):
        rows = pl.ds(b * block_rows, block_rows)
        put(owner_ref[0, b] == me, new_ref.at[:, rows], slot_ref[0, b])


def write_back(write_owner, write_slot, asked, pool, new_rows, fresh, capacity):
    count = len(asked)
    return pl.pallas_call(
        functools.partial(write_back_kernel, capacity, pool.shape[2], count),
        out_shape=jax.ShapeDtypeStruct(pool.shape, pool.dtype),
        in_specs=[SMEM] * (count + 2) + [VMEM] * (count + 2),
        out_specs=ANY,
        scratch_shapes=[
            pltpu.SemaphoreType.DMA((pool.shape[0],)),
            pltpu.SemaphoreType.DMA,
        ],
        compiler_params=pltpu.CompilerParams(vmem_limit_bytes=VMEM_LIMIT),
        cost_estimate=pl.CostEstimate(
            flops=0, bytes_accessed=4 * math.prod(pool.shape), transcendentals=0
        ),
    )(write_owner, write_slot, *asked, pool, new_rows, *fresh)


def attend_kernel(
    spans, relays, afters, kv_dev, group, block_tok, rows, first, final, count_ref, q_ref, *refs
):
    parts, refs = refs[: len(spans)], refs[len(spans) :]
    ins = 1 if first else 2
    outs = 1 if final else 3 if first else 2
    rest = refs[ins + relays + afters :]
    refs = refs[:ins] + rest[:outs] + rest[-3:]
    if first:
        new_ref, q_out, acc_out, stat_out = refs[:4]
        head_dim = q_ref.shape[2]
        suffix = new_ref.shape[1] // kv_dev
    else:
        acc_in, stat_in = refs[:2]
        head_dim = q_ref.shape[2]
        suffix = 0
        if final:
            out_ref = refs[2]
        else:
            acc_out, stat_out = refs[2:4]
    key_ref, value_ref, stage_ref = refs[-3:]
    factor = head_dim**-0.5 * math.log2(math.e)
    prefix_keys = sum(size for _, _, size in spans) * block_tok
    keys = prefix_keys + suffix

    def unpack(raw, kv, at):
        stage_ref[...] = raw.astype(jnp.float32)
        for h in range(kv_dev):
            head = stage_ref[pl.ds(h, block_tok, stride=kv_dev), :]
            if kv == 0:
                key_ref[h, pl.ds(at, block_tok)] = head.astype(jnp.bfloat16)
            else:
                value_ref[h, :head_dim, pl.ds(at, block_tok)] = head.T.astype(jnp.bfloat16)

    value_ref[:, head_dim:, :] = jnp.ones(
        (kv_dev, value_ref.shape[1] - head_dim, keys), jnp.bfloat16
    )
    base = 0
    for part, (_, _, size) in zip(parts, spans):
        for b in range(size):
            for kv in range(2):
                unpack(part[b, kv], kv, base + b * block_tok)
        base += size * block_tok
    for piece in range(suffix // block_tok):
        for kv in range(2):
            raw = new_ref[kv, pl.ds(piece * block_tok * kv_dev, block_tok * kv_dev), :]
            unpack(raw, kv, base + piece * block_tok)

    if first:
        for h in range(kv_dev):
            heads = q_ref[...].astype(jnp.float32)[:, h * group : (h + 1) * group, :]
            q_out[h] = heads.reshape(-1, head_dim).astype(jnp.bfloat16)
        q_rows = q_out
    else:
        q_rows = q_ref

    def run(masked):
        def product(start, stop, h, at):
            return lax.dot_general(
                key_ref[h, start:stop],
                q_rows[h, at],
                (((1,), (1,)), ((), ())),
                preferred_element_type=jnp.float32,
            )

        def sub(index, carry):
            at = pl.ds(pl.multiple_of(index * rows, rows), rows)
            results = []
            for h in range(kv_dev):
                pieces = []
                if spans:
                    scores = product(0, prefix_keys, h, at)
                    if masked:
                        place = lax.broadcasted_iota(jnp.int32, (prefix_keys, 1), 0)
                        allowed = jnp.zeros((prefix_keys, 1), jnp.bool_)
                        base = 0
                        for row, start, size in spans:
                            end = base + jnp.minimum(count_ref[0, row] - start, size) * block_tok
                            allowed |= (place >= base) & (place < end)
                            base += size * block_tok
                        scores = jnp.where(allowed, scores, -jnp.inf)
                    pieces.append((scores, 0))
                if first:
                    scores = product(prefix_keys, keys, h, at)
                    token = lax.broadcasted_iota(jnp.int32, (1, rows), 1) + index * rows
                    place = lax.broadcasted_iota(jnp.int32, (suffix, rows), 0)
                    scores = jnp.where(place * group <= token, scores, -jnp.inf)
                    pieces.append((scores, prefix_keys))
                peak = factor * functools.reduce(
                    jnp.maximum, [jnp.max(scores, axis=0, keepdims=True) for scores, _ in pieces]
                )
                if not first:
                    old = stat_in[h, 0:1, at]
                    peak = jnp.maximum(peak, old)
                both = sum(
                    jnp.dot(
                        value_ref[h, :, start : start + scores.shape[0]],
                        jnp.exp2(scores * factor - peak).astype(jnp.bfloat16),
                        preferred_element_type=jnp.float32,
                    )
                    for scores, start in pieces
                )
                summed = both[:head_dim]
                total = both[head_dim : head_dim + 1]
                if not first:
                    shrink = jnp.exp2(old - peak)
                    summed += acc_in[h, :, at] * shrink
                    total += stat_in[h, 1:2, at] * shrink
                if final:
                    results.append((summed / total).T.reshape(rows // group, group, head_dim))
                else:
                    acc_out[h, :, at] = summed
                    stat_out[h, 0:1, at] = peak
                    stat_out[h, 1:2, at] = total
            if final:
                tok = pl.multiple_of(index * (rows // group), rows // group)
                out_ref[pl.ds(tok, rows // group)] = jnp.concatenate(results, axis=1).astype(
                    jnp.bfloat16
                )
            return carry

        lax.fori_loop(0, q_rows.shape[1] // rows, sub, 0)

    full = functools.reduce(
        jnp.logical_and, [count_ref[0, row] >= start + size for row, start, size in spans]
    )

    @pl.when(full)
    def unmasked():
        run(False)

    @pl.when(jnp.logical_not(full))
    def masked():
        run(True)


def attend(
    counts, queries, parts, spans, kv_dev, block_tok, new_rows=None, state=None, final=False, relay=(), after=()
):
    suffix, heads_dev, head_dim = queries.shape
    group = heads_dev // kv_dev
    first = state is None
    rows = min(QUERY_ROWS, suffix * group)
    keys = sum(size for _, _, size in spans) * block_tok + (suffix if first else 0)
    state_shape = [
        jax.ShapeDtypeStruct((kv_dev, suffix * group, head_dim), jnp.bfloat16),
        jax.ShapeDtypeStruct((kv_dev, head_dim, suffix * group), jnp.float32),
        jax.ShapeDtypeStruct((kv_dev, 8, suffix * group), jnp.float32),
    ]
    if first:
        operands = [queries, *parts, new_rows]
        out_shape = state_shape
    else:
        operands = [state[0], *parts, *state[1:]]
        out_shape = state_shape[1:]
        if final:
            out_shape = [jax.ShapeDtypeStruct(queries.shape, queries.dtype)]
    result = pl.pallas_call(
        functools.partial(
            attend_kernel, spans, len(relay), len(after), kv_dev, group, block_tok, rows, first, final
        ),
        out_shape=out_shape + [jax.ShapeDtypeStruct(x.shape, x.dtype) for x in relay],
        in_specs=[SMEM] + [VMEM] * len(operands) + [ANY] * (len(relay) + len(after)),
        out_specs=[VMEM] * len(out_shape) + [ANY] * len(relay),
        input_output_aliases={
            1 + len(operands) + i: len(out_shape) + i for i in range(len(relay))
        },
        scratch_shapes=[
            pltpu.VMEM((kv_dev, keys, head_dim), jnp.bfloat16),
            pltpu.VMEM((kv_dev, head_dim + 16, keys), jnp.bfloat16),
            pltpu.VMEM((block_tok * kv_dev, head_dim), jnp.float32),
        ],
        compiler_params=pltpu.CompilerParams(vmem_limit_bytes=ATTEND_LIMIT),
        cost_estimate=pl.CostEstimate(
            flops=4 * suffix * heads_dev * keys * head_dim,
            bytes_accessed=keys * kv_dev * head_dim * 4 + 16 * suffix * heads_dev * head_dim,
            transcendentals=suffix * heads_dev * keys,
        ),
    )(counts, *operands, *relay, *after)
    step, relayed = result[: len(out_shape)], result[len(out_shape) :]
    return (step if first or final else [state[0], *step]), relayed


def per_device(
    queries, new_kv, pool, prefix_slot, prefix_owner, prefix_len, write_slot, write_owner
):
    num_blk = lax.axis_size("blk")
    pool_dev, _, block_tok, kv_dev, head_dim = pool.shape
    suffix = queries.shape[1]
    prefix_blocks = prefix_slot.shape[1]
    capacity = max(2, (prefix_blocks + num_blk - 1) // num_blk)
    shifts = sorted(range(1, num_blk), key=lambda d: -min(d, num_blk - d))
    pool_rows = pool.reshape(pool_dev, 2, block_tok * kv_dev, head_dim)
    new_rows = new_kv.reshape(2, suffix * kv_dev, head_dim)

    def shift(array, d):
        return lax.ppermute(array, "blk", [(i, (i + d) % num_blk) for i in range(num_blk)])

    counts, asks = prepare(
        prefix_slot, prefix_owner, prefix_len, write_slot, write_owner, capacity, num_blk
    )
    asked = {d: shift(asks[d], d) for d in shifts}
    rows = [asked[d] for d in shifts]

    first = max(1, 3 * capacity // 8)
    cuts = sorted({0, first, 2 * first, capacity})
    plans = [[(d, start, end - start) for d in shifts] for start, end in zip(cuts, cuts[1:])]

    def load(plan, first, after=()):
        return gather(
            counts,
            rows,
            pool_rows,
            new_rows,
            tuple(
                (shifts.index(d), start, size, num_blk - d if first else None)
                for d, start, size in plan
            ),
            after,
            not first,
        )

    def send(plan, blocks):
        return [shift(x, num_blk - d) for (d, _, _), x in zip(plan, blocks)]

    loaded = load(plans[0], True)
    arrived = [send(plans[0], loaded)]
    local = gather(counts, [asks[0]], pool_rows, new_rows, ((0, 0, capacity, None),), loaded[:1])
    step = functools.partial(attend, counts, queries[0], kv_dev=kv_dev, block_tok=block_tok)
    state, _ = step(local, ((0, 0, capacity),), new_rows=new_rows)

    later = load(sum(plans[1:], []), False, [state[2]])
    arrived.append(send(plans[1], later[: len(shifts)]))
    new_pool = None
    for i, plan in enumerate(plans):
        relay = later[len(shifts) :] if i == 0 else []
        groups = [slice(at, at + 8) for at in range(0, len(plan), 8)]
        for j, group in enumerate(groups):
            ends = j == len(groups) - 1
            state, relayed = step(
                arrived[i][group],
                tuple(plan[group]),
                state=state,
                final=ends and i == len(plans) - 1,
                relay=relay if ends else [],
                after=[new_pool] if i == 1 and j == 0 else [],
            )
        if i == 0:
            for k in range(2, len(plans)):
                blocks, relayed = relayed[: len(plans[k])], relayed[len(plans[k]) :]
                arrived.append(send(plans[k], blocks))
            new_pool = write_back(
                write_owner,
                write_slot,
                [asked[num_blk - d] for d in shifts],
                pool_rows,
                new_rows,
                arrived[0],
                capacity,
            )
    return state[0][None], new_pool.reshape(pool.shape)


def solution(mesh):
    in_specs = (
        P(("group", "blk"), None, "tensor", None),
        P(None, ("group", "blk"), None, "tensor", None),
        P(("group", "blk"), None, None, "tensor", None),
        P(("group", "blk"), None),
        P(("group", "blk"), None),
        P(("group", "blk")),
        P(("group", "blk"), None),
        P(("group", "blk"), None),
    )
    out_specs = (
        P(("group", "blk"), None, "tensor", None),
        P(("group", "blk"), None, None, "tensor", None),
    )
    return jax.shard_map(
        per_device, mesh=mesh, in_specs=in_specs, out_specs=out_specs, check_vma=False
    )
```

```python
import functools
import math

import jax
import jax.numpy as jnp
from jax import lax
from jax.experimental import pallas as pl
from jax.experimental.pallas import tpu as pltpu
from jax.sharding import PartitionSpec as P

ANY = pl.BlockSpec(memory_space=pl.ANY)
HBM = pl.BlockSpec(memory_space=pltpu.HBM)
SMEM = pl.BlockSpec(memory_space=pltpu.SMEM)
VMEM = pl.BlockSpec(memory_space=pltpu.VMEM)
WHOLE_LIMIT = 60 * 1024 * 1024
VMEM_LIMIT = 16 * 1024 * 1024
ATTEND_LIMIT = 32 * 1024 * 1024
QUERY_ROWS = 1024
HEADROOM = 60.0


def prepare_kernel(capacity, *refs):
    sources, refs = refs[:5], refs[5:]
    num_blk = refs[0].shape[1] // 2
    count_ref, asked, refs = refs[0], refs[1 : 1 + num_blk], refs[1 + num_blk :]
    held, (table_ref, used_ref, counted_ref, load_sems) = refs[:5], refs[5:]
    loads = [
        pltpu.make_async_copy(source, target, load_sems.at[i])
        for i, (source, target) in enumerate(zip(sources, held))
    ]
    for load in loads:
        load.start()
    slot_ref, owner_ref, len_ref, write_slot_ref, write_owner_ref = held
    me = lax.axis_index("blk")
    for owner in range(num_blk):
        used_ref[owner] = 0
        counted_ref[owner] = 0
        for k in range(capacity):
            table_ref[owner, k] = 0
    for load in loads:
        load.wait()

    def step(j, carry):
        owner = owner_ref[0, j]
        place = used_ref[owner]
        table_ref[owner, jnp.minimum(place, capacity)] = slot_ref[0, j]
        used_ref[owner] = place + 1
        counted_ref[owner] += jnp.where(j < len_ref[0], 1, 0)
        return carry

    lax.fori_loop(0, owner_ref.shape[1], step, 0, unroll=8)
    for d in range(num_blk):
        owner = lax.rem(me + d, num_blk)
        count_ref[0, d] = counted_ref[owner]
        for k in range(capacity):
            asked[d][0, k] = table_ref[owner, k]
        slot = jnp.int32(-1)
        chosen = jnp.int32(0)
        for b in range(write_owner_ref.shape[1]):
            goes = write_owner_ref[0, b] == owner
            slot = jnp.where(goes, write_slot_ref[0, b], slot)
            chosen = jnp.where(goes, b, chosen)
        asked[d][0, capacity] = slot
        count_ref[0, num_blk + d] = chosen


def prepare(prefix_slot, prefix_owner, prefix_len, write_slot, write_owner, capacity, num_blk):
    operands = (prefix_slot, prefix_owner, prefix_len, write_slot, write_owner)
    row = jax.ShapeDtypeStruct((1, capacity + 1), jnp.int32)
    results = pl.pallas_call(
        functools.partial(prepare_kernel, capacity),
        out_shape=[jax.ShapeDtypeStruct((1, 2 * num_blk), jnp.int32)] + [row] * num_blk,
        in_specs=[HBM] * 5,
        out_specs=[SMEM] * (num_blk + 1),
        scratch_shapes=[pltpu.SMEM(operand.shape, operand.dtype) for operand in operands]
        + [
            pltpu.SMEM((num_blk, capacity + 1), jnp.int32),
            pltpu.SMEM((num_blk,), jnp.int32),
            pltpu.SMEM((num_blk,), jnp.int32),
            pltpu.SemaphoreType.DMA((5,)),
        ],
        compiler_params=pltpu.CompilerParams(vmem_limit_bytes=WHOLE_LIMIT),
    )(*operands)
    return results[0], results[1:]


def gather_kernel(plan, count, block_rows, direct, whole, count_ref, *refs):
    asked, pool_ref, new_ref = refs[:count], refs[count], refs[count + 1]
    refs = refs[-len(plan) - whole - (1 if direct else 3) :]
    outs, refs = refs[: len(plan) + whole], refs[len(plan) + whole :]
    sems = refs[0]
    moves = []

    def move(source, target):
        i = len(moves)
        if direct:
            load, store = None, pltpu.make_async_copy(source, target, sems.at[i])
            store.start()
        else:
            held, in_sems = refs[1:]
            load = pltpu.make_async_copy(source, held.at[i], in_sems.at[i])
            store = pltpu.make_async_copy(held.at[i], target, sems.at[i])
            load.start()
        moves.append((load, store))

    for (row, start, size, to), out in zip(plan, outs):
        for place in range(size):
            move(pool_ref.at[asked[row][0, start + place]], out.at[place])
        if to is not None:
            chosen = count_ref[0, count_ref.shape[1] // 2 + to]
            at = pl.ds(pl.multiple_of(chosen * block_rows, block_rows), block_rows)
            move(new_ref.at[:, at], out.at[size])
    if whole:
        for b in range(pool_ref.shape[0]):
            move(pool_ref.at[b], outs[-1].at[b])
    if not direct:
        for load, store in moves:
            load.wait()
            store.start()
    for _, store in moves:
        store.wait()


def gather(counts, asked, pool, new_rows, plan, after=(), direct=True, whole=False):
    sizes = [size + (to is not None) for _, _, size, to in plan] + [pool.shape[0]] * whole
    blocks = sum(sizes)
    scratch = [pltpu.SemaphoreType.DMA((blocks,))]
    if not direct:
        scratch.append(pltpu.VMEM((blocks,) + pool.shape[1:], pool.dtype))
        scratch.append(pltpu.SemaphoreType.DMA((blocks,)))
    return pl.pallas_call(
        functools.partial(gather_kernel, plan, len(asked), pool.shape[2], direct, whole),
        out_shape=[jax.ShapeDtypeStruct((size,) + pool.shape[1:], pool.dtype) for size in sizes],
        in_specs=[SMEM] * (1 + len(asked)) + [VMEM if direct else HBM] * 2 + [ANY] * len(after),
        out_specs=[ANY if direct else HBM] * len(sizes),
        scratch_shapes=scratch,
        compiler_params=pltpu.CompilerParams(
            vmem_limit_bytes=VMEM_LIMIT if direct else WHOLE_LIMIT
        ),
        cost_estimate=pl.CostEstimate(
            flops=0, bytes_accessed=4 * blocks * math.prod(pool.shape[1:]), transcendentals=0
        ),
    )(counts, *asked, pool, new_rows, *after)


def write_back_kernel(capacity, block_rows, count, owner_ref, slot_ref, *refs):
    asked, refs = refs[:count], refs[count:]
    new_ref, fresh = refs[0], refs[1 : count + 1]
    out_ref, token_ref, sem = refs[count + 2 :]
    me = lax.axis_index("blk")
    token_ref[0, 0] = 0

    def put(wanted, src, slot):
        @pl.when(wanted)
        def write():
            copy = pltpu.make_async_copy(src, out_ref.at[slot], sem)
            copy.start()
            copy.wait()

    for i in range(count):
        slot = asked[i][0, capacity]
        put(slot >= 0, fresh[i].at[fresh[i].shape[0] - 1], slot)
    for b in range(owner_ref.shape[1]):
        rows = pl.ds(b * block_rows, block_rows)
        put(owner_ref[0, b] == me, new_ref.at[:, rows], slot_ref[0, b])


def write_back(write_owner, write_slot, asked, new_rows, fresh, pool, capacity):
    count = len(asked)
    return pl.pallas_call(
        functools.partial(write_back_kernel, capacity, pool.shape[2], count),
        out_shape=[
            jax.ShapeDtypeStruct(pool.shape, pool.dtype),
            jax.ShapeDtypeStruct((1, 1), jnp.int32),
        ],
        in_specs=[SMEM] * (count + 2) + [VMEM] * (count + 1) + [ANY],
        out_specs=[ANY, SMEM],
        scratch_shapes=[pltpu.SemaphoreType.DMA],
        input_output_aliases={2 * count + 3: 0},
        compiler_params=pltpu.CompilerParams(vmem_limit_bytes=VMEM_LIMIT),
        cost_estimate=pl.CostEstimate(flops=0, bytes_accessed=1 << 20, transcendentals=0),
    )(write_owner, write_slot, *asked, new_rows, *fresh, pool)


def attend_kernel(
    spans, relays, afters, kv_dev, group, block_tok, rows, first, final, count_ref, q_ref, *refs
):
    parts, refs = refs[: len(spans)], refs[len(spans) :]
    ins = 1 if first else 2
    outs = 1 if final else 3 if first else 2
    rest = refs[ins + relays + afters :]
    refs = refs[:ins] + rest[:outs] + rest[-3:]
    if first:
        new_ref, q_out, acc_out, stat_out = refs[:4]
        head_dim = q_ref.shape[2]
        suffix = new_ref.shape[1] // kv_dev
    else:
        acc_in, stat_in = refs[:2]
        head_dim = q_ref.shape[2]
        suffix = 0
        if final:
            out_ref = refs[2]
        else:
            acc_out, stat_out = refs[2:4]
    key_ref, value_ref, stage_ref = refs[-3:]
    factor = head_dim**-0.5 * math.log2(math.e)
    prefix_keys = sum(size for _, _, size in spans) * block_tok
    keys = prefix_keys + suffix

    def unpack(raw, kv, at):
        stage_ref[...] = raw.astype(jnp.float32)
        for h in range(kv_dev):
            head = stage_ref[pl.ds(h, block_tok, stride=kv_dev), :]
            if kv == 0:
                key_ref[h, pl.ds(at, block_tok)] = head.astype(jnp.bfloat16)
            else:
                value_ref[h, :head_dim, pl.ds(at, block_tok)] = head.T.astype(jnp.bfloat16)

    value_ref[:, head_dim:, :] = jnp.ones(
        (kv_dev, value_ref.shape[1] - head_dim, keys), jnp.bfloat16
    )
    base = 0
    for part, (_, _, size) in zip(parts, spans):
        for b in range(size):
            for kv in range(2):
                unpack(part[b, kv], kv, base + b * block_tok)
        base += size * block_tok
    for piece in range(suffix // block_tok):
        for kv in range(2):
            raw = new_ref[kv, pl.ds(piece * block_tok * kv_dev, block_tok * kv_dev), :]
            unpack(raw, kv, base + piece * block_tok)

    if first:
        for h in range(kv_dev):
            heads = q_ref[...].astype(jnp.float32)[:, h * group : (h + 1) * group, :]
            q_out[h] = heads.reshape(-1, head_dim).astype(jnp.bfloat16)
        q_rows = q_out
    else:
        q_rows = q_ref

    def run(masked, safe):
        def product(start, stop, h, at):
            return lax.dot_general(
                key_ref[h, start:stop],
                q_rows[h, at],
                (((1,), (1,)), ((), ())),
                preferred_element_type=jnp.float32,
            )

        def sub(index, worst):
            at = pl.ds(pl.multiple_of(index * rows, rows), rows)
            results = []
            for h in range(kv_dev):
                pieces = []
                if spans:
                    scores = product(0, prefix_keys, h, at)
                    if masked:
                        place = lax.broadcasted_iota(jnp.int32, (prefix_keys, 1), 0)
                        allowed = jnp.zeros((prefix_keys, 1), jnp.bool_)
                        base = 0
                        for row, start, size in spans:
                            end = base + jnp.minimum(count_ref[0, row] - start, size) * block_tok
                            allowed |= (place >= base) & (place < end)
                            base += size * block_tok
                        scores = jnp.where(allowed, scores, -jnp.inf)
                    pieces.append((scores, 0))
                if first:
                    scores = product(prefix_keys, keys, h, at)
                    token = lax.broadcasted_iota(jnp.int32, (1, rows), 1) + index * rows
                    place = lax.broadcasted_iota(jnp.int32, (suffix, rows), 0)
                    scores = jnp.where(place * group <= token, scores, -jnp.inf)
                    pieces.append((scores, prefix_keys))
                peak = factor * functools.reduce(
                    jnp.maximum, [jnp.max(scores, axis=0, keepdims=True) for scores, _ in pieces]
                )
                if not first:
                    old = stat_in[h, 0:1, at]
                    if safe:
                        peak = jnp.maximum(peak, old)
                    else:
                        worst = jnp.maximum(worst, peak - old)
                        peak = old
                both = sum(
                    jnp.dot(
                        value_ref[h, :, start : start + scores.shape[0]],
                        jnp.exp2(scores * factor - peak).astype(jnp.bfloat16),
                        preferred_element_type=jnp.float32,
                    )
                    for scores, start in pieces
                )
                summed = both[:head_dim]
                total = both[head_dim : head_dim + 1]
                if not first:
                    shrink = jnp.exp2(old - peak) if safe else 1.0
                    summed += acc_in[h, :, at] * shrink
                    total += stat_in[h, 1:2, at] * shrink
                if final:
                    results.append((summed / total).T.reshape(rows // group, group, head_dim))
                else:
                    acc_out[h, :, at] = summed
                    stat_out[h, 0:1, at] = peak
                    stat_out[h, 1:2, at] = total
            if final:
                tok = pl.multiple_of(index * (rows // group), rows // group)
                out_ref[pl.ds(tok, rows // group)] = jnp.concatenate(results, axis=1).astype(
                    jnp.bfloat16
                )
            return worst

        worst = lax.fori_loop(
            0, q_rows.shape[1] // rows, sub, jnp.full((1, rows), -jnp.inf, jnp.float32)
        )
        if not first and not safe:

            @pl.when(jnp.max(worst) > HEADROOM)
            def again():
                run(True, True)

    full = functools.reduce(
        jnp.logical_and, [count_ref[0, row] >= start + size for row, start, size in spans]
    )

    @pl.when(full)
    def unmasked():
        run(False, first)

    @pl.when(jnp.logical_not(full))
    def masked():
        run(True, first)


def attend(
    counts, queries, parts, spans, kv_dev, block_tok, new_rows=None, state=None, final=False, relay=(), after=()
):
    suffix, heads_dev, head_dim = queries.shape
    group = heads_dev // kv_dev
    first = state is None
    rows = min(QUERY_ROWS, suffix * group)
    keys = sum(size for _, _, size in spans) * block_tok + (suffix if first else 0)
    state_shape = [
        jax.ShapeDtypeStruct((kv_dev, suffix * group, head_dim), jnp.bfloat16),
        jax.ShapeDtypeStruct((kv_dev, head_dim, suffix * group), jnp.float32),
        jax.ShapeDtypeStruct((kv_dev, 8, suffix * group), jnp.float32),
    ]
    if first:
        operands = [queries, *parts, new_rows]
        out_shape = state_shape
    else:
        operands = [state[0], *parts, *state[1:]]
        out_shape = state_shape[1:]
        if final:
            out_shape = [jax.ShapeDtypeStruct(queries.shape, queries.dtype)]
    result = pl.pallas_call(
        functools.partial(
            attend_kernel, spans, len(relay), len(after), kv_dev, group, block_tok, rows, first, final
        ),
        out_shape=out_shape + [jax.ShapeDtypeStruct(x.shape, x.dtype) for x in relay],
        in_specs=[SMEM] + [VMEM] * len(operands) + [ANY] * (len(relay) + len(after)),
        out_specs=[VMEM] * len(out_shape) + [ANY] * len(relay),
        input_output_aliases={
            1 + len(operands) + i: len(out_shape) + i for i in range(len(relay))
        },
        scratch_shapes=[
            pltpu.VMEM((kv_dev, keys, head_dim), jnp.bfloat16),
            pltpu.VMEM((kv_dev, head_dim + 16, keys), jnp.bfloat16),
            pltpu.VMEM((block_tok * kv_dev, head_dim), jnp.float32),
        ],
        compiler_params=pltpu.CompilerParams(vmem_limit_bytes=ATTEND_LIMIT),
        cost_estimate=pl.CostEstimate(
            flops=4 * suffix * heads_dev * keys * head_dim,
            bytes_accessed=keys * kv_dev * head_dim * 4 + 16 * suffix * heads_dev * head_dim,
            transcendentals=suffix * heads_dev * keys,
        ),
    )(counts, *operands, *relay, *after)
    step, relayed = result[: len(out_shape)], result[len(out_shape) :]
    return (step if first or final else [state[0], *step]), relayed


def per_device(
    queries, new_kv, pool, prefix_slot, prefix_owner, prefix_len, write_slot, write_owner
):
    num_blk = lax.axis_size("blk")
    pool_dev, _, block_tok, kv_dev, head_dim = pool.shape
    suffix = queries.shape[1]
    prefix_blocks = prefix_slot.shape[1]
    capacity = max(2, (prefix_blocks + num_blk - 1) // num_blk)
    shifts = sorted(range(1, num_blk), key=lambda d: -min(d, num_blk - d))
    pool_rows = pool.reshape(pool_dev, 2, block_tok * kv_dev, head_dim)
    new_rows = new_kv.reshape(2, suffix * kv_dev, head_dim)

    def shift(array, d):
        return lax.ppermute(array, "blk", [(i, (i + d) % num_blk) for i in range(num_blk)])

    counts, asks = prepare(
        prefix_slot, prefix_owner, prefix_len, write_slot, write_owner, capacity, num_blk
    )
    asked = {d: shift(asks[d], d) for d in shifts}
    rows = [asked[d] for d in shifts]

    first = max(1, 3 * capacity // 8)
    cuts = sorted({0, first, 2 * first, capacity})
    plans = [[(d, start, end - start) for d in shifts] for start, end in zip(cuts, cuts[1:])]

    def load(plan, first, after=()):
        return gather(
            counts,
            rows,
            pool_rows,
            new_rows,
            tuple(
                (shifts.index(d), start, size, num_blk - d if first else None)
                for d, start, size in plan
            ),
            after,
            not first,
        )

    def send(plan, blocks):
        return [shift(x, num_blk - d) for (d, _, _), x in zip(plan, blocks)]

    loaded = load(plans[0], True)
    arrived = [send(plans[0], loaded)]
    local, new_pool = gather(
        counts, [asks[0]], pool_rows, new_rows, ((0, 0, capacity, None),), loaded[:1], whole=True
    )
    step = functools.partial(attend, counts, queries[0], kv_dev=kv_dev, block_tok=block_tok)
    state, _ = step([local], ((0, 0, capacity),), new_rows=new_rows)

    later = load(sum(plans[1:], []), False, [state[2]])
    arrived.append(send(plans[1], later[: len(shifts)]))
    token = None
    for i, plan in enumerate(plans):
        relay = later[len(shifts) :] if i == 0 else []
        groups = [slice(at, at + 8) for at in range(0, len(plan), 8)]
        for j, group in enumerate(groups):
            ends = j == len(groups) - 1
            state, relayed = step(
                arrived[i][group],
                tuple(plan[group]),
                state=state,
                final=ends and i == len(plans) - 1,
                relay=relay if ends else [],
                after=[token] if i == 1 and j == 0 else [],
            )
        if i == 0:
            for k in range(2, len(plans)):
                blocks, relayed = relayed[: len(plans[k])], relayed[len(plans[k]) :]
                arrived.append(send(plans[k], blocks))
            new_pool, token = write_back(
                write_owner,
                write_slot,
                [asked[num_blk - d] for d in shifts],
                new_rows,
                arrived[0],
                new_pool,
                capacity,
            )
    return state[0][None], new_pool.reshape(pool.shape)


def solution(mesh):
    in_specs = (
        P(("group", "blk"), None, "tensor", None),
        P(None, ("group", "blk"), None, "tensor", None),
        P(("group", "blk"), None, None, "tensor", None),
        P(("group", "blk"), None),
        P(("group", "blk"), None),
        P(("group", "blk")),
        P(("group", "blk"), None),
        P(("group", "blk"), None),
    )
    out_specs = (
        P(("group", "blk"), None, "tensor", None),
        P(("group", "blk"), None, None, "tensor", None),
    )
    return jax.shard_map(
        per_device, mesh=mesh, in_specs=in_specs, out_specs=out_specs, check_vma=False
    )
```

```python
import functools
import math

import jax
import jax.numpy as jnp
from jax import lax
from jax.experimental import pallas as pl
from jax.experimental.pallas import tpu as pltpu
from jax.sharding import PartitionSpec as P

ANY = pl.BlockSpec(memory_space=pl.ANY)
HBM = pl.BlockSpec(memory_space=pltpu.HBM)
SMEM = pl.BlockSpec(memory_space=pltpu.SMEM)
VMEM = pl.BlockSpec(memory_space=pltpu.VMEM)
WHOLE_LIMIT = 60 * 1024 * 1024
VMEM_LIMIT = 16 * 1024 * 1024
ATTEND_LIMIT = 32 * 1024 * 1024
QUERY_ROWS = 1024
SAFE_ROWS = 256
HEADROOM = 60.0


def prepare_kernel(capacity, *refs):
    sources, refs = refs[:5], refs[5:]
    num_blk = refs[0].shape[1] // 2
    count_ref, asked, refs = refs[0], refs[1 : 1 + num_blk], refs[1 + num_blk :]
    held, (table_ref, used_ref, counted_ref, load_sems) = refs[:5], refs[5:]
    loads = [
        pltpu.make_async_copy(source, target, load_sems.at[i])
        for i, (source, target) in enumerate(zip(sources, held))
    ]
    for load in loads:
        load.start()
    slot_ref, owner_ref, len_ref, write_slot_ref, write_owner_ref = held
    me = lax.axis_index("blk")
    for owner in range(num_blk):
        used_ref[owner] = 0
        counted_ref[owner] = 0
        for k in range(capacity):
            table_ref[owner, k] = 0
    for load in loads:
        load.wait()

    def step(j, carry):
        owner = owner_ref[0, j]
        place = used_ref[owner]
        table_ref[owner, jnp.minimum(place, capacity)] = slot_ref[0, j]
        used_ref[owner] = place + 1
        counted_ref[owner] += jnp.where(j < len_ref[0], 1, 0)
        return carry

    lax.fori_loop(0, owner_ref.shape[1], step, 0, unroll=8)
    for d in range(num_blk):
        owner = lax.rem(me + d, num_blk)
        count_ref[0, d] = counted_ref[owner]
        for k in range(capacity):
            asked[d][0, k] = table_ref[owner, k]
        slot = jnp.int32(-1)
        chosen = jnp.int32(0)
        for b in range(write_owner_ref.shape[1]):
            goes = write_owner_ref[0, b] == owner
            slot = jnp.where(goes, write_slot_ref[0, b], slot)
            chosen = jnp.where(goes, b, chosen)
        asked[d][0, capacity] = slot
        count_ref[0, num_blk + d] = chosen


def prepare(prefix_slot, prefix_owner, prefix_len, write_slot, write_owner, capacity, num_blk):
    operands = (prefix_slot, prefix_owner, prefix_len, write_slot, write_owner)
    row = jax.ShapeDtypeStruct((1, capacity + 1), jnp.int32)
    results = pl.pallas_call(
        functools.partial(prepare_kernel, capacity),
        out_shape=[jax.ShapeDtypeStruct((1, 2 * num_blk), jnp.int32)] + [row] * num_blk,
        in_specs=[HBM] * 5,
        out_specs=[SMEM] * (num_blk + 1),
        scratch_shapes=[pltpu.SMEM(operand.shape, operand.dtype) for operand in operands]
        + [
            pltpu.SMEM((num_blk, capacity + 1), jnp.int32),
            pltpu.SMEM((num_blk,), jnp.int32),
            pltpu.SMEM((num_blk,), jnp.int32),
            pltpu.SemaphoreType.DMA((5,)),
        ],
        compiler_params=pltpu.CompilerParams(vmem_limit_bytes=WHOLE_LIMIT),
    )(*operands)
    return results[0], results[1:]


def gather_kernel(plan, count, block_rows, direct, whole, count_ref, *refs):
    asked, pool_ref, new_ref = refs[:count], refs[count], refs[count + 1]
    refs = refs[-len(plan) - whole - (1 if direct else 3) :]
    outs, refs = refs[: len(plan) + whole], refs[len(plan) + whole :]
    sems = refs[0]
    moves = []

    def move(source, target):
        i = len(moves)
        if direct:
            load, store = None, pltpu.make_async_copy(source, target, sems.at[i])
            store.start()
        else:
            held, in_sems = refs[1:]
            load = pltpu.make_async_copy(source, held.at[i], in_sems.at[i])
            store = pltpu.make_async_copy(held.at[i], target, sems.at[i])
            load.start()
        moves.append((load, store))

    for (row, start, size, to), out in zip(plan, outs):
        for place in range(size):
            move(pool_ref.at[asked[row][0, start + place]], out.at[place])
        if to is not None:
            chosen = count_ref[0, count_ref.shape[1] // 2 + to]
            at = pl.ds(pl.multiple_of(chosen * block_rows, block_rows), block_rows)
            move(new_ref.at[:, at], out.at[size])
    if whole:
        for b in range(pool_ref.shape[0]):
            move(pool_ref.at[b], outs[-1].at[b])
    if not direct:
        for load, store in moves:
            load.wait()
            store.start()
    for _, store in moves:
        store.wait()


def gather(counts, asked, pool, new_rows, plan, after=(), direct=True, whole=False):
    sizes = [size + (to is not None) for _, _, size, to in plan] + [pool.shape[0]] * whole
    blocks = sum(sizes)
    scratch = [pltpu.SemaphoreType.DMA((blocks,))]
    if not direct:
        scratch.append(pltpu.VMEM((blocks,) + pool.shape[1:], pool.dtype))
        scratch.append(pltpu.SemaphoreType.DMA((blocks,)))
    return pl.pallas_call(
        functools.partial(gather_kernel, plan, len(asked), pool.shape[2], direct, whole),
        out_shape=[jax.ShapeDtypeStruct((size,) + pool.shape[1:], pool.dtype) for size in sizes],
        in_specs=[SMEM] * (1 + len(asked)) + [VMEM if direct else HBM] * 2 + [ANY] * len(after),
        out_specs=[ANY if direct else HBM] * len(sizes),
        scratch_shapes=scratch,
        compiler_params=pltpu.CompilerParams(
            vmem_limit_bytes=VMEM_LIMIT if direct else WHOLE_LIMIT
        ),
        cost_estimate=pl.CostEstimate(
            flops=0, bytes_accessed=4 * blocks * math.prod(pool.shape[1:]), transcendentals=0
        ),
    )(counts, *asked, pool, new_rows, *after)


def write_back_kernel(capacity, block_rows, count, owner_ref, slot_ref, *refs):
    asked, refs = refs[:count], refs[count:]
    new_ref, fresh = refs[0], refs[1 : count + 1]
    out_ref, token_ref, sem = refs[count + 2 :]
    me = lax.axis_index("blk")
    token_ref[0, 0] = 0

    def put(wanted, src, slot):
        @pl.when(wanted)
        def write():
            copy = pltpu.make_async_copy(src, out_ref.at[slot], sem)
            copy.start()
            copy.wait()

    for i in range(count):
        slot = asked[i][0, capacity]
        put(slot >= 0, fresh[i].at[fresh[i].shape[0] - 1], slot)
    for b in range(owner_ref.shape[1]):
        rows = pl.ds(b * block_rows, block_rows)
        put(owner_ref[0, b] == me, new_ref.at[:, rows], slot_ref[0, b])


def write_back(write_owner, write_slot, asked, new_rows, fresh, pool, capacity):
    count = len(asked)
    return pl.pallas_call(
        functools.partial(write_back_kernel, capacity, pool.shape[2], count),
        out_shape=[
            jax.ShapeDtypeStruct(pool.shape, pool.dtype),
            jax.ShapeDtypeStruct((1, 1), jnp.int32),
        ],
        in_specs=[SMEM] * (count + 2) + [VMEM] * (count + 1) + [ANY],
        out_specs=[ANY, SMEM],
        scratch_shapes=[pltpu.SemaphoreType.DMA],
        input_output_aliases={2 * count + 3: 0},
        compiler_params=pltpu.CompilerParams(vmem_limit_bytes=VMEM_LIMIT),
        cost_estimate=pl.CostEstimate(flops=0, bytes_accessed=1 << 20, transcendentals=0),
    )(write_owner, write_slot, *asked, new_rows, *fresh, pool)


def attend_kernel(
    spans, relays, afters, kv_dev, group, block_tok, rows, first, final, count_ref, q_ref, *refs
):
    parts, refs = refs[: len(spans)], refs[len(spans) :]
    ins = 1 if first else 2
    outs = 1 if final else 3 if first else 2
    rest = refs[ins + relays + afters :]
    refs = refs[:ins] + rest[:outs] + rest[-3:]
    if first:
        new_ref, q_out, acc_out, stat_out = refs[:4]
        head_dim = q_ref.shape[2]
        suffix = new_ref.shape[1] // kv_dev
    else:
        acc_in, stat_in = refs[:2]
        head_dim = q_ref.shape[2]
        suffix = 0
        if final:
            out_ref = refs[2]
        else:
            acc_out, stat_out = refs[2:4]
    key_ref, value_ref, stage_ref = refs[-3:]
    factor = head_dim**-0.5 * math.log2(math.e)
    prefix_keys = sum(size for _, _, size in spans) * block_tok
    keys = prefix_keys + suffix

    def unpack(raw, kv, at):
        stage_ref[...] = raw.astype(jnp.float32)
        for h in range(kv_dev):
            head = stage_ref[pl.ds(h, block_tok, stride=kv_dev), :]
            if kv == 0:
                key_ref[h, pl.ds(at, block_tok)] = head.astype(jnp.bfloat16)
            else:
                value_ref[h, :head_dim, pl.ds(at, block_tok)] = head.T.astype(jnp.bfloat16)

    value_ref[:, head_dim:, :] = jnp.ones(
        (kv_dev, value_ref.shape[1] - head_dim, keys), jnp.bfloat16
    )
    base = 0
    for part, (row, start, size) in zip(parts, spans):
        for b in range(size):
            counts = count_ref[0, row] > start + b
            at = pl.ds(base + b * block_tok, block_tok)

            @pl.when(counts)
            def take(part=part, b=b, base=base):
                for kv in range(2):
                    unpack(part[b, kv], kv, base + b * block_tok)

            @pl.when(jnp.logical_not(counts))
            def leave_out(at=at):
                for h in range(kv_dev):
                    key_ref[h, at] = jnp.zeros((block_tok, head_dim), jnp.bfloat16)
                    value_ref[h, :, at] = jnp.zeros((value_ref.shape[1], block_tok), jnp.bfloat16)

        base += size * block_tok
    for piece in range(suffix // block_tok):
        for kv in range(2):
            raw = new_ref[kv, pl.ds(piece * block_tok * kv_dev, block_tok * kv_dev), :]
            unpack(raw, kv, base + piece * block_tok)

    if first:
        for h in range(kv_dev):
            heads = q_ref[...].astype(jnp.float32)[:, h * group : (h + 1) * group, :]
            q_out[h] = heads.reshape(-1, head_dim).astype(jnp.bfloat16)
        q_rows = q_out
    else:
        q_rows = q_ref

    def run(safe, rows):
        def product(start, stop, h, at):
            return lax.dot_general(
                key_ref[h, start:stop],
                q_rows[h, at],
                (((1,), (1,)), ((), ())),
                preferred_element_type=jnp.float32,
            )

        def sub(index, worst):
            at = pl.ds(pl.multiple_of(index * rows, rows), rows)
            results = []
            for h in range(kv_dev):
                pieces = []
                if spans:
                    scores = product(0, prefix_keys, h, at)
                    if first or safe:
                        place = lax.broadcasted_iota(jnp.int32, (prefix_keys, 1), 0)
                        allowed = jnp.zeros((prefix_keys, 1), jnp.bool_)
                        base = 0
                        for row, start, size in spans:
                            end = base + jnp.minimum(count_ref[0, row] - start, size) * block_tok
                            allowed |= (place >= base) & (place < end)
                            base += size * block_tok
                        scores = jnp.where(allowed, scores, -jnp.inf)
                    pieces.append((scores, 0))
                if first:
                    scores = product(prefix_keys, keys, h, at)
                    token = lax.broadcasted_iota(jnp.int32, (1, rows), 1) + index * rows
                    place = lax.broadcasted_iota(jnp.int32, (suffix, rows), 0)
                    scores = jnp.where(place * group <= token, scores, -jnp.inf)
                    pieces.append((scores, prefix_keys))
                peak = factor * functools.reduce(
                    jnp.maximum, [jnp.max(scores, axis=0, keepdims=True) for scores, _ in pieces]
                )
                if not first:
                    old = stat_in[h, 0:1, at]
                    if safe:
                        peak = jnp.maximum(peak, old)
                    else:
                        worst = jnp.maximum(worst, peak - old)
                        peak = old
                both = sum(
                    jnp.dot(
                        value_ref[h, :, start : start + scores.shape[0]],
                        jnp.exp2(scores * factor - peak).astype(jnp.bfloat16),
                        preferred_element_type=jnp.float32,
                    )
                    for scores, start in pieces
                )
                summed = both[:head_dim]
                total = both[head_dim : head_dim + 1]
                if not first:
                    shrink = jnp.exp2(old - peak) if safe else 1.0
                    summed += acc_in[h, :, at] * shrink
                    total += stat_in[h, 1:2, at] * shrink
                if final:
                    results.append((summed / total).T.reshape(rows // group, group, head_dim))
                else:
                    acc_out[h, :, at] = summed
                    stat_out[h, 0:1, at] = peak
                    stat_out[h, 1:2, at] = total
            if final:
                tok = pl.multiple_of(index * (rows // group), rows // group)
                out_ref[pl.ds(tok, rows // group)] = jnp.concatenate(results, axis=1).astype(
                    jnp.bfloat16
                )
            return worst

        worst = lax.fori_loop(
            0, q_rows.shape[1] // rows, sub, jnp.full((1, rows), -jnp.inf, jnp.float32)
        )
        if not first and not safe:

            @pl.when(jnp.max(worst) > HEADROOM)
            def again():
                run(True, min(rows, SAFE_ROWS))

    run(first, rows)


def attend(
    counts, queries, parts, spans, kv_dev, block_tok, new_rows=None, state=None, final=False, relay=(), after=()
):
    suffix, heads_dev, head_dim = queries.shape
    group = heads_dev // kv_dev
    first = state is None
    rows = min(QUERY_ROWS, suffix * group)
    keys = sum(size for _, _, size in spans) * block_tok + (suffix if first else 0)
    state_shape = [
        jax.ShapeDtypeStruct((kv_dev, suffix * group, head_dim), jnp.bfloat16),
        jax.ShapeDtypeStruct((kv_dev, head_dim, suffix * group), jnp.float32),
        jax.ShapeDtypeStruct((kv_dev, 8, suffix * group), jnp.float32),
    ]
    if first:
        operands = [queries, *parts, new_rows]
        out_shape = state_shape
    else:
        operands = [state[0], *parts, *state[1:]]
        out_shape = state_shape[1:]
        if final:
            out_shape = [jax.ShapeDtypeStruct(queries.shape, queries.dtype)]
    result = pl.pallas_call(
        functools.partial(
            attend_kernel, spans, len(relay), len(after), kv_dev, group, block_tok, rows, first, final
        ),
        out_shape=out_shape + [jax.ShapeDtypeStruct(x.shape, x.dtype) for x in relay],
        in_specs=[SMEM] + [VMEM] * len(operands) + [ANY] * (len(relay) + len(after)),
        out_specs=[VMEM] * len(out_shape) + [ANY] * len(relay),
        input_output_aliases={
            1 + len(operands) + i: len(out_shape) + i for i in range(len(relay))
        },
        scratch_shapes=[
            pltpu.VMEM((kv_dev, keys, head_dim), jnp.bfloat16),
            pltpu.VMEM((kv_dev, head_dim + 16, keys), jnp.bfloat16),
            pltpu.VMEM((block_tok * kv_dev, head_dim), jnp.float32),
        ],
        compiler_params=pltpu.CompilerParams(vmem_limit_bytes=ATTEND_LIMIT),
        cost_estimate=pl.CostEstimate(
            flops=4 * suffix * heads_dev * keys * head_dim,
            bytes_accessed=keys * kv_dev * head_dim * 4 + 16 * suffix * heads_dev * head_dim,
            transcendentals=suffix * heads_dev * keys,
        ),
    )(counts, *operands, *relay, *after)
    step, relayed = result[: len(out_shape)], result[len(out_shape) :]
    return (step if first or final else [state[0], *step]), relayed


def per_device(
    queries, new_kv, pool, prefix_slot, prefix_owner, prefix_len, write_slot, write_owner
):
    num_blk = lax.axis_size("blk")
    pool_dev, _, block_tok, kv_dev, head_dim = pool.shape
    suffix = queries.shape[1]
    prefix_blocks = prefix_slot.shape[1]
    capacity = max(2, (prefix_blocks + num_blk - 1) // num_blk)
    shifts = sorted(range(1, num_blk), key=lambda d: -min(d, num_blk - d))
    pool_rows = pool.reshape(pool_dev, 2, block_tok * kv_dev, head_dim)
    new_rows = new_kv.reshape(2, suffix * kv_dev, head_dim)

    def shift(array, d):
        return lax.ppermute(array, "blk", [(i, (i + d) % num_blk) for i in range(num_blk)])

    counts, asks = prepare(
        prefix_slot, prefix_owner, prefix_len, write_slot, write_owner, capacity, num_blk
    )
    asked = {d: shift(asks[d], d) for d in shifts}
    rows = [asked[d] for d in shifts]

    first = max(1, 3 * capacity // 8)
    cuts = sorted({0, first, 2 * first, capacity})
    plans = [[(d, start, end - start) for d in shifts] for start, end in zip(cuts, cuts[1:])]

    def load(plan, first, after=()):
        return gather(
            counts,
            rows,
            pool_rows,
            new_rows,
            tuple(
                (shifts.index(d), start, size, num_blk - d if first else None)
                for d, start, size in plan
            ),
            after,
            not first,
        )

    def send(plan, blocks):
        return [shift(x, num_blk - d) for (d, _, _), x in zip(plan, blocks)]

    loaded = load(plans[0], True)
    arrived = [send(plans[0], loaded)]
    local, new_pool = gather(
        counts, [asks[0]], pool_rows, new_rows, ((0, 0, capacity, None),), loaded[:1], whole=True
    )
    step = functools.partial(attend, counts, queries[0], kv_dev=kv_dev, block_tok=block_tok)
    state, _ = step([local], ((0, 0, capacity),), new_rows=new_rows)

    later = load(sum(plans[1:], []), False, [state[2]])
    arrived.append(send(plans[1], later[: len(shifts)]))
    token = None
    for i, plan in enumerate(plans):
        relay = later[len(shifts) :] if i == 0 else []
        groups = [slice(at, at + 8) for at in range(0, len(plan), 8)]
        for j, group in enumerate(groups):
            ends = j == len(groups) - 1
            state, relayed = step(
                arrived[i][group],
                tuple(plan[group]),
                state=state,
                final=ends and i == len(plans) - 1,
                relay=relay if ends else [],
                after=[token] if i == 1 and j == 0 else [],
            )
        if i == 0:
            for k in range(2, len(plans)):
                blocks, relayed = relayed[: len(plans[k])], relayed[len(plans[k]) :]
                arrived.append(send(plans[k], blocks))
            new_pool, token = write_back(
                write_owner,
                write_slot,
                [asked[num_blk - d] for d in shifts],
                new_rows,
                arrived[0],
                new_pool,
                capacity,
            )
    return state[0][None], new_pool.reshape(pool.shape)


def solution(mesh):
    in_specs = (
        P(("group", "blk"), None, "tensor", None),
        P(None, ("group", "blk"), None, "tensor", None),
        P(("group", "blk"), None, None, "tensor", None),
        P(("group", "blk"), None),
        P(("group", "blk"), None),
        P(("group", "blk")),
        P(("group", "blk"), None),
        P(("group", "blk"), None),
    )
    out_specs = (
        P(("group", "blk"), None, "tensor", None),
        P(("group", "blk"), None, None, "tensor", None),
    )
    return jax.shard_map(
        per_device, mesh=mesh, in_specs=in_specs, out_specs=out_specs, check_vma=False
    )
```

```python
import functools
import math

import jax
import jax.numpy as jnp
from jax import lax
from jax.experimental import pallas as pl
from jax.experimental.pallas import tpu as pltpu
from jax.sharding import PartitionSpec as P

ANY = pl.BlockSpec(memory_space=pl.ANY)
HBM = pl.BlockSpec(memory_space=pltpu.HBM)
SMEM = pl.BlockSpec(memory_space=pltpu.SMEM)
VMEM = pl.BlockSpec(memory_space=pltpu.VMEM)
WHOLE_LIMIT = 60 * 1024 * 1024
VMEM_LIMIT = 16 * 1024 * 1024
ATTEND_LIMIT = 32 * 1024 * 1024
QUERY_ROWS = 1024
SAFE_ROWS = 256
HEADROOM = 60.0


def prepare_kernel(capacity, to, *refs):
    sources, refs = refs[:6], refs[6:]
    num_blk = refs[0].shape[1] // 2
    count_ref, asked, refs = refs[0], refs[1 : 1 + num_blk], refs[1 + num_blk :]
    fresh_ref, refs = refs[0], refs[1:]
    held, (table_ref, used_ref, counted_ref, load_sems, store_sem) = refs[:6], refs[6:]
    loads = [
        pltpu.make_async_copy(source, target, load_sems.at[i])
        for i, (source, target) in enumerate(zip(sources, held))
    ]
    for load in loads:
        load.start()
    slot_ref, owner_ref, len_ref, write_slot_ref, write_owner_ref, new_ref = held
    me = lax.axis_index("blk")
    for owner in range(num_blk):
        used_ref[owner] = 0
        counted_ref[owner] = 0
        for k in range(capacity):
            table_ref[owner, k] = 0
    for load in loads:
        load.wait()
    target = lax.rem(me + to, num_blk)
    chosen = jnp.int32(0)
    for b in range(write_owner_ref.shape[1]):
        chosen = jnp.where(write_owner_ref[0, b] == target, b, chosen)
    block_rows = fresh_ref.shape[2]
    rows = pl.ds(pl.multiple_of(chosen * block_rows, block_rows), block_rows)
    store = pltpu.make_async_copy(new_ref.at[:, rows], fresh_ref.at[0], store_sem)
    store.start()

    def step(j, carry):
        owner = owner_ref[0, j]
        place = used_ref[owner]
        table_ref[owner, jnp.minimum(place, capacity)] = slot_ref[0, j]
        used_ref[owner] = place + 1
        counted_ref[owner] += jnp.where(j < len_ref[0], 1, 0)
        return carry

    lax.fori_loop(0, owner_ref.shape[1], step, 0, unroll=8)
    for d in range(num_blk):
        owner = lax.rem(me + d, num_blk)
        count_ref[0, d] = counted_ref[owner]
        for k in range(capacity):
            asked[d][0, k] = table_ref[owner, k]
        slot = jnp.int32(-1)
        chosen = jnp.int32(0)
        for b in range(write_owner_ref.shape[1]):
            goes = write_owner_ref[0, b] == owner
            slot = jnp.where(goes, write_slot_ref[0, b], slot)
            chosen = jnp.where(goes, b, chosen)
        asked[d][0, capacity] = slot
        count_ref[0, num_blk + d] = chosen
    store.wait()


def prepare(
    prefix_slot, prefix_owner, prefix_len, write_slot, write_owner, new_rows, block_rows, to,
    capacity, num_blk,
):
    operands = (prefix_slot, prefix_owner, prefix_len, write_slot, write_owner, new_rows)
    block = jax.ShapeDtypeStruct((1, 2, block_rows, new_rows.shape[2]), new_rows.dtype)
    row = jax.ShapeDtypeStruct((1, capacity + 1), jnp.int32)
    results = pl.pallas_call(
        functools.partial(prepare_kernel, capacity, to),
        out_shape=[jax.ShapeDtypeStruct((1, 2 * num_blk), jnp.int32)]
        + [row] * num_blk
        + [block],
        in_specs=[HBM] * 6,
        out_specs=[SMEM] * (num_blk + 1) + [HBM],
        scratch_shapes=[pltpu.SMEM(operand.shape, operand.dtype) for operand in operands[:5]]
        + [
            pltpu.VMEM(new_rows.shape, new_rows.dtype),
            pltpu.SMEM((num_blk, capacity + 1), jnp.int32),
            pltpu.SMEM((num_blk,), jnp.int32),
            pltpu.SMEM((num_blk,), jnp.int32),
            pltpu.SemaphoreType.DMA((6,)),
            pltpu.SemaphoreType.DMA,
        ],
        compiler_params=pltpu.CompilerParams(vmem_limit_bytes=WHOLE_LIMIT),
    )(*operands)
    return results[0], results[1:-1], results[-1]


def gather_kernel(plan, count, block_rows, direct, whole, count_ref, *refs):
    asked, pool_ref, new_ref = refs[:count], refs[count], refs[count + 1]
    refs = refs[-len(plan) - whole - (1 if direct else 3) :]
    outs, refs = refs[: len(plan) + whole], refs[len(plan) + whole :]
    sems = refs[0]
    moves = []

    def move(source, target):
        i = len(moves)
        if direct:
            load, store = None, pltpu.make_async_copy(source, target, sems.at[i])
            store.start()
        else:
            held, in_sems = refs[1:]
            load = pltpu.make_async_copy(source, held.at[i], in_sems.at[i])
            store = pltpu.make_async_copy(held.at[i], target, sems.at[i])
            load.start()
        moves.append((load, store))

    for (row, start, size, to), out in zip(plan, outs):
        for place in range(size):
            move(pool_ref.at[asked[row][0, start + place]], out.at[place])
        if to is not None:
            chosen = count_ref[0, count_ref.shape[1] // 2 + to]
            at = pl.ds(pl.multiple_of(chosen * block_rows, block_rows), block_rows)
            move(new_ref.at[:, at], out.at[size])
    if whole:
        for b in range(pool_ref.shape[0]):
            move(pool_ref.at[b], outs[-1].at[b])
    if not direct:
        for load, store in moves:
            load.wait()
            store.start()
    for _, store in moves:
        store.wait()


def gather(counts, asked, pool, new_rows, plan, after=(), direct=True, whole=False):
    sizes = [size + (to is not None) for _, _, size, to in plan] + [pool.shape[0]] * whole
    blocks = sum(sizes)
    scratch = [pltpu.SemaphoreType.DMA((blocks,))]
    if not direct:
        scratch.append(pltpu.VMEM((blocks,) + pool.shape[1:], pool.dtype))
        scratch.append(pltpu.SemaphoreType.DMA((blocks,)))
    return pl.pallas_call(
        functools.partial(gather_kernel, plan, len(asked), pool.shape[2], direct, whole),
        out_shape=[jax.ShapeDtypeStruct((size,) + pool.shape[1:], pool.dtype) for size in sizes],
        in_specs=[SMEM] * (1 + len(asked)) + [VMEM if direct else HBM] * 2 + [ANY] * len(after),
        out_specs=[ANY if direct else HBM] * len(sizes),
        scratch_shapes=scratch,
        compiler_params=pltpu.CompilerParams(
            vmem_limit_bytes=VMEM_LIMIT if direct else WHOLE_LIMIT
        ),
        cost_estimate=pl.CostEstimate(
            flops=0, bytes_accessed=4 * blocks * math.prod(pool.shape[1:]), transcendentals=0
        ),
    )(counts, *asked, pool, new_rows, *after)


def write_back_kernel(capacity, block_rows, count, owner_ref, slot_ref, *refs):
    asked, refs = refs[:count], refs[count:]
    new_ref, fresh = refs[0], refs[1 : count + 1]
    out_ref, token_ref, sem = refs[count + 2 :]
    me = lax.axis_index("blk")
    token_ref[0, 0] = 0

    def put(wanted, src, slot):
        @pl.when(wanted)
        def write():
            copy = pltpu.make_async_copy(src, out_ref.at[slot], sem)
            copy.start()
            copy.wait()

    for i in range(count):
        slot = asked[i][0, capacity]
        put(slot >= 0, fresh[i].at[fresh[i].shape[0] - 1], slot)
    for b in range(owner_ref.shape[1]):
        rows = pl.ds(b * block_rows, block_rows)
        put(owner_ref[0, b] == me, new_ref.at[:, rows], slot_ref[0, b])


def write_back(write_owner, write_slot, asked, new_rows, fresh, pool, capacity):
    count = len(asked)
    return pl.pallas_call(
        functools.partial(write_back_kernel, capacity, pool.shape[2], count),
        out_shape=[
            jax.ShapeDtypeStruct(pool.shape, pool.dtype),
            jax.ShapeDtypeStruct((1, 1), jnp.int32),
        ],
        in_specs=[SMEM] * (count + 2) + [VMEM] * (count + 1) + [ANY],
        out_specs=[ANY, SMEM],
        scratch_shapes=[pltpu.SemaphoreType.DMA],
        input_output_aliases={2 * count + 3: 0},
        compiler_params=pltpu.CompilerParams(vmem_limit_bytes=VMEM_LIMIT),
        cost_estimate=pl.CostEstimate(flops=0, bytes_accessed=1 << 20, transcendentals=0),
    )(write_owner, write_slot, *asked, new_rows, *fresh, pool)


def attend_kernel(
    spans, relays, afters, kv_dev, group, block_tok, rows, first, final, count_ref, q_ref, *refs
):
    parts, refs = refs[: len(spans)], refs[len(spans) :]
    ins = 1 if first else 2
    outs = 1 if final else 3 if first else 2
    rest = refs[ins + relays + afters :]
    refs = refs[:ins] + rest[:outs] + rest[-3:]
    if first:
        new_ref, q_out, acc_out, stat_out = refs[:4]
        head_dim = q_ref.shape[2]
        suffix = new_ref.shape[1] // kv_dev
    else:
        acc_in, stat_in = refs[:2]
        head_dim = q_ref.shape[2]
        suffix = 0
        if final:
            out_ref = refs[2]
        else:
            acc_out, stat_out = refs[2:4]
    key_ref, value_ref, stage_ref = refs[-3:]
    factor = head_dim**-0.5 * math.log2(math.e)
    prefix_keys = sum(size for _, _, size in spans) * block_tok
    keys = prefix_keys + suffix

    def unpack(raw, kv, at):
        stage_ref[...] = raw.astype(jnp.float32)
        for h in range(kv_dev):
            head = stage_ref[pl.ds(h, block_tok, stride=kv_dev), :]
            if kv == 0:
                key_ref[h, pl.ds(at, block_tok)] = head.astype(jnp.bfloat16)
            else:
                value_ref[h, :head_dim, pl.ds(at, block_tok)] = head.T.astype(jnp.bfloat16)

    value_ref[:, head_dim:, :] = jnp.ones(
        (kv_dev, value_ref.shape[1] - head_dim, keys), jnp.bfloat16
    )
    base = 0
    for part, (row, start, size) in zip(parts, spans):
        for b in range(size):
            counts = count_ref[0, row] > start + b
            at = pl.ds(base + b * block_tok, block_tok)

            @pl.when(counts)
            def take(part=part, b=b, base=base):
                for kv in range(2):
                    unpack(part[b, kv], kv, base + b * block_tok)

            @pl.when(jnp.logical_not(counts))
            def leave_out(at=at):
                for h in range(kv_dev):
                    key_ref[h, at] = jnp.zeros((block_tok, head_dim), jnp.bfloat16)
                    value_ref[h, :, at] = jnp.zeros((value_ref.shape[1], block_tok), jnp.bfloat16)

        base += size * block_tok
    for piece in range(suffix // block_tok):
        for kv in range(2):
            raw = new_ref[kv, pl.ds(piece * block_tok * kv_dev, block_tok * kv_dev), :]
            unpack(raw, kv, base + piece * block_tok)

    if first:
        for h in range(kv_dev):
            heads = q_ref[...].astype(jnp.float32)[:, h * group : (h + 1) * group, :]
            q_out[h] = heads.reshape(-1, head_dim).astype(jnp.bfloat16)
        q_rows = q_out
    else:
        q_rows = q_ref

    def run(safe, rows):
        def product(start, stop, h, at):
            return lax.dot_general(
                key_ref[h, start:stop],
                q_rows[h, at],
                (((1,), (1,)), ((), ())),
                preferred_element_type=jnp.float32,
            )

        def sub(index, worst):
            at = pl.ds(pl.multiple_of(index * rows, rows), rows)
            results = []
            for h in range(kv_dev):
                pieces = []
                if spans:
                    scores = product(0, prefix_keys, h, at)
                    if first or safe:
                        place = lax.broadcasted_iota(jnp.int32, (prefix_keys, 1), 0)
                        allowed = jnp.zeros((prefix_keys, 1), jnp.bool_)
                        base = 0
                        for row, start, size in spans:
                            end = base + jnp.minimum(count_ref[0, row] - start, size) * block_tok
                            allowed |= (place >= base) & (place < end)
                            base += size * block_tok
                        scores = jnp.where(allowed, scores, -jnp.inf)
                    pieces.append((scores, 0))
                if first:
                    scores = product(prefix_keys, keys, h, at)
                    token = lax.broadcasted_iota(jnp.int32, (1, rows), 1) + index * rows
                    place = lax.broadcasted_iota(jnp.int32, (suffix, rows), 0)
                    scores = jnp.where(place * group <= token, scores, -jnp.inf)
                    pieces.append((scores, prefix_keys))
                peak = factor * functools.reduce(
                    jnp.maximum, [jnp.max(scores, axis=0, keepdims=True) for scores, _ in pieces]
                )
                if not first:
                    old = stat_in[h, 0:1, at]
                    if safe:
                        peak = jnp.maximum(peak, old)
                    else:
                        worst = jnp.maximum(worst, peak - old)
                        peak = old
                both = sum(
                    jnp.dot(
                        value_ref[h, :, start : start + scores.shape[0]],
                        jnp.exp2(scores * factor - peak).astype(jnp.bfloat16),
                        preferred_element_type=jnp.float32,
                    )
                    for scores, start in pieces
                )
                summed = both[:head_dim]
                total = both[head_dim : head_dim + 1]
                if not first:
                    shrink = jnp.exp2(old - peak) if safe else 1.0
                    summed += acc_in[h, :, at] * shrink
                    total += stat_in[h, 1:2, at] * shrink
                if final:
                    results.append((summed / total).T.reshape(rows // group, group, head_dim))
                else:
                    acc_out[h, :, at] = summed
                    stat_out[h, 0:1, at] = peak
                    stat_out[h, 1:2, at] = total
            if final:
                tok = pl.multiple_of(index * (rows // group), rows // group)
                out_ref[pl.ds(tok, rows // group)] = jnp.concatenate(results, axis=1).astype(
                    jnp.bfloat16
                )
            return worst

        worst = lax.fori_loop(
            0, q_rows.shape[1] // rows, sub, jnp.full((1, rows), -jnp.inf, jnp.float32)
        )
        if not first and not safe:

            @pl.when(jnp.max(worst) > HEADROOM)
            def again():
                run(True, min(rows, SAFE_ROWS))

    run(first, rows)


def attend(
    counts, queries, parts, spans, kv_dev, block_tok, new_rows=None, state=None, final=False, relay=(), after=()
):
    suffix, heads_dev, head_dim = queries.shape
    group = heads_dev // kv_dev
    first = state is None
    rows = min(QUERY_ROWS, suffix * group)
    keys = sum(size for _, _, size in spans) * block_tok + (suffix if first else 0)
    state_shape = [
        jax.ShapeDtypeStruct((kv_dev, suffix * group, head_dim), jnp.bfloat16),
        jax.ShapeDtypeStruct((kv_dev, head_dim, suffix * group), jnp.float32),
        jax.ShapeDtypeStruct((kv_dev, 8, suffix * group), jnp.float32),
    ]
    if first:
        operands = [queries, *parts, new_rows]
        out_shape = state_shape
    else:
        operands = [state[0], *parts, *state[1:]]
        out_shape = state_shape[1:]
        if final:
            out_shape = [jax.ShapeDtypeStruct(queries.shape, queries.dtype)]
    result = pl.pallas_call(
        functools.partial(
            attend_kernel, spans, len(relay), len(after), kv_dev, group, block_tok, rows, first, final
        ),
        out_shape=out_shape + [jax.ShapeDtypeStruct(x.shape, x.dtype) for x in relay],
        in_specs=[SMEM] + [VMEM] * len(operands) + [ANY] * (len(relay) + len(after)),
        out_specs=[VMEM] * len(out_shape) + [ANY] * len(relay),
        input_output_aliases={
            1 + len(operands) + i: len(out_shape) + i for i in range(len(relay))
        },
        scratch_shapes=[
            pltpu.VMEM((kv_dev, keys, head_dim), jnp.bfloat16),
            pltpu.VMEM((kv_dev, head_dim + 16, keys), jnp.bfloat16),
            pltpu.VMEM((block_tok * kv_dev, head_dim), jnp.float32),
        ],
        compiler_params=pltpu.CompilerParams(vmem_limit_bytes=ATTEND_LIMIT),
        cost_estimate=pl.CostEstimate(
            flops=4 * suffix * heads_dev * keys * head_dim,
            bytes_accessed=keys * kv_dev * head_dim * 4 + 16 * suffix * heads_dev * head_dim,
            transcendentals=suffix * heads_dev * keys,
        ),
    )(counts, *operands, *relay, *after)
    step, relayed = result[: len(out_shape)], result[len(out_shape) :]
    return (step if first or final else [state[0], *step]), relayed


def per_device(
    queries, new_kv, pool, prefix_slot, prefix_owner, prefix_len, write_slot, write_owner
):
    num_blk = lax.axis_size("blk")
    pool_dev, _, block_tok, kv_dev, head_dim = pool.shape
    suffix = queries.shape[1]
    prefix_blocks = prefix_slot.shape[1]
    capacity = max(2, (prefix_blocks + num_blk - 1) // num_blk)
    shifts = sorted(range(1, num_blk), key=lambda d: -min(d, num_blk - d))
    pool_rows = pool.reshape(pool_dev, 2, block_tok * kv_dev, head_dim)
    new_rows = new_kv.reshape(2, suffix * kv_dev, head_dim)

    def shift(array, d):
        return lax.ppermute(array, "blk", [(i, (i + d) % num_blk) for i in range(num_blk)])

    ahead = num_blk - shifts[0]
    counts, asks, farthest = prepare(
        prefix_slot,
        prefix_owner,
        prefix_len,
        write_slot,
        write_owner,
        new_rows,
        block_tok * kv_dev,
        ahead,
        capacity,
        num_blk,
    )
    farthest = shift(farthest, ahead)
    asked = {d: shift(asks[d], d) for d in shifts}
    rows = [asked[d] for d in shifts]

    first = max(1, 3 * capacity // 8)
    cuts = sorted({0, first, 2 * first, capacity})
    plans = [[(d, start, end - start) for d in shifts] for start, end in zip(cuts, cuts[1:])]

    def load(plan, first, after=()):
        return gather(
            counts,
            rows,
            pool_rows,
            new_rows,
            tuple(
                (shifts.index(d), start, size, num_blk - d if first and d != shifts[0] else None)
                for d, start, size in plan
            ),
            after,
            not first,
        )

    def send(plan, blocks):
        return [shift(x, num_blk - d) for (d, _, _), x in zip(plan, blocks)]

    loaded = load(plans[0], True)
    arrived = [send(plans[0], loaded)]
    local, new_pool = gather(
        counts, [asks[0]], pool_rows, new_rows, ((0, 0, capacity, None),), [loaded[0], farthest], whole=True
    )
    step = functools.partial(attend, counts, queries[0], kv_dev=kv_dev, block_tok=block_tok)
    state, _ = step([local], ((0, 0, capacity),), new_rows=new_rows)

    later = load(sum(plans[1:], []), False, [state[2]])
    arrived.append(send(plans[1], later[: len(shifts)]))
    token = None
    for i, plan in enumerate(plans):
        relay = later[len(shifts) :] if i == 0 else []
        groups = [slice(at, at + 8) for at in range(0, len(plan), 8)]
        for j, group in enumerate(groups):
            ends = j == len(groups) - 1
            state, relayed = step(
                arrived[i][group],
                tuple(plan[group]),
                state=state,
                final=ends and i == len(plans) - 1,
                relay=relay if ends else [],
                after=[token] if i == 1 and j == 0 else [],
            )
        if i == 0:
            for k in range(2, len(plans)):
                blocks, relayed = relayed[: len(plans[k])], relayed[len(plans[k]) :]
                arrived.append(send(plans[k], blocks))
            new_pool, token = write_back(
                write_owner,
                write_slot,
                [asked[num_blk - d] for d in shifts],
                new_rows,
                [farthest, *arrived[0][1:]],
                new_pool,
                capacity,
            )
    return state[0][None], new_pool.reshape(pool.shape)


def solution(mesh):
    in_specs = (
        P(("group", "blk"), None, "tensor", None),
        P(None, ("group", "blk"), None, "tensor", None),
        P(("group", "blk"), None, None, "tensor", None),
        P(("group", "blk"), None),
        P(("group", "blk"), None),
        P(("group", "blk")),
        P(("group", "blk"), None),
        P(("group", "blk"), None),
    )
    out_specs = (
        P(("group", "blk"), None, "tensor", None),
        P(("group", "blk"), None, None, "tensor", None),
    )
    return jax.shard_map(
        per_device, mesh=mesh, in_specs=in_specs, out_specs=out_specs, check_vma=False
    )
```

```python
import functools
import math

import jax
import jax.numpy as jnp
from jax import lax
from jax.experimental import pallas as pl
from jax.experimental.pallas import tpu as pltpu
from jax.sharding import PartitionSpec as P

ANY = pl.BlockSpec(memory_space=pl.ANY)
HBM = pl.BlockSpec(memory_space=pltpu.HBM)
SMEM = pl.BlockSpec(memory_space=pltpu.SMEM)
VMEM = pl.BlockSpec(memory_space=pltpu.VMEM)
WHOLE_LIMIT = 60 * 1024 * 1024
VMEM_LIMIT = 16 * 1024 * 1024
ATTEND_LIMIT = 32 * 1024 * 1024
QUERY_ROWS = 1024
SAFE_ROWS = 256
HEADROOM = 60.0


def prepare_kernel(capacity, to, *refs):
    sources, refs = refs[:6], refs[6:]
    num_blk = refs[0].shape[1] // 2
    count_ref, asked, refs = refs[0], refs[1 : 1 + num_blk], refs[1 + num_blk :]
    fresh_ref, refs = refs[0], refs[1:]
    held, (table_ref, used_ref, counted_ref, load_sems, store_sem) = refs[:6], refs[6:]
    loads = [
        pltpu.make_async_copy(source, target, load_sems.at[i])
        for i, (source, target) in enumerate(zip(sources, held))
    ]
    for load in loads:
        load.start()
    slot_ref, owner_ref, len_ref, write_slot_ref, write_owner_ref, new_ref = held
    me = lax.axis_index("blk")
    for owner in range(num_blk):
        used_ref[owner] = 0
        counted_ref[owner] = 0
        for k in range(capacity):
            table_ref[owner, k] = 0
    for load in loads:
        load.wait()
    target = lax.rem(me + to, num_blk)
    chosen = jnp.int32(0)
    for b in range(write_owner_ref.shape[1]):
        chosen = jnp.where(write_owner_ref[0, b] == target, b, chosen)
    block_rows = fresh_ref.shape[2]
    rows = pl.ds(pl.multiple_of(chosen * block_rows, block_rows), block_rows)
    store = pltpu.make_async_copy(new_ref.at[:, rows], fresh_ref.at[0], store_sem)
    store.start()

    def step(j, carry):
        owner = owner_ref[0, j]
        place = used_ref[owner]
        table_ref[owner, jnp.minimum(place, capacity)] = slot_ref[0, j]
        used_ref[owner] = place + 1
        counted_ref[owner] += jnp.where(j < len_ref[0], 1, 0)
        return carry

    lax.fori_loop(0, owner_ref.shape[1], step, 0, unroll=8)
    for d in range(num_blk):
        owner = lax.rem(me + d, num_blk)
        count_ref[0, d] = counted_ref[owner]
        for k in range(capacity):
            asked[d][0, k] = table_ref[owner, k]
        slot = jnp.int32(-1)
        chosen = jnp.int32(0)
        for b in range(write_owner_ref.shape[1]):
            goes = write_owner_ref[0, b] == owner
            slot = jnp.where(goes, write_slot_ref[0, b], slot)
            chosen = jnp.where(goes, b, chosen)
        asked[d][0, capacity] = slot
        count_ref[0, num_blk + d] = chosen
    store.wait()


def prepare(
    prefix_slot, prefix_owner, prefix_len, write_slot, write_owner, new_rows, block_rows, to,
    capacity, num_blk,
):
    operands = (prefix_slot, prefix_owner, prefix_len, write_slot, write_owner, new_rows)
    block = jax.ShapeDtypeStruct((1, 2, block_rows, new_rows.shape[2]), new_rows.dtype)
    row = jax.ShapeDtypeStruct((1, capacity + 1), jnp.int32)
    results = pl.pallas_call(
        functools.partial(prepare_kernel, capacity, to),
        out_shape=[jax.ShapeDtypeStruct((1, 2 * num_blk), jnp.int32)]
        + [row] * num_blk
        + [block],
        in_specs=[HBM] * 6,
        out_specs=[SMEM] * (num_blk + 1) + [HBM],
        scratch_shapes=[pltpu.SMEM(operand.shape, operand.dtype) for operand in operands[:5]]
        + [
            pltpu.VMEM(new_rows.shape, new_rows.dtype),
            pltpu.SMEM((num_blk, capacity + 1), jnp.int32),
            pltpu.SMEM((num_blk,), jnp.int32),
            pltpu.SMEM((num_blk,), jnp.int32),
            pltpu.SemaphoreType.DMA((6,)),
            pltpu.SemaphoreType.DMA,
        ],
        compiler_params=pltpu.CompilerParams(vmem_limit_bytes=WHOLE_LIMIT),
    )(*operands)
    return results[0], results[1:-1], results[-1]


def gather_kernel(plan, count, block_rows, direct, whole, count_ref, *refs):
    asked, pool_ref, new_ref = refs[:count], refs[count], refs[count + 1]
    refs = refs[-len(plan) - whole - (1 if direct else 3) :]
    outs, refs = refs[: len(plan) + whole], refs[len(plan) + whole :]
    sems = refs[0]
    moves = []

    def move(source, target):
        i = len(moves)
        if direct:
            load, store = None, pltpu.make_async_copy(source, target, sems.at[i])
            store.start()
        else:
            held, in_sems = refs[1:]
            load = pltpu.make_async_copy(source, held.at[i], in_sems.at[i])
            store = pltpu.make_async_copy(held.at[i], target, sems.at[i])
            load.start()
        moves.append((load, store))

    for (row, start, size, to), out in zip(plan, outs):
        for place in range(size):
            move(pool_ref.at[asked[row][0, start + place]], out.at[place])
        if to is not None:
            chosen = count_ref[0, count_ref.shape[1] // 2 + to]
            at = pl.ds(pl.multiple_of(chosen * block_rows, block_rows), block_rows)
            move(new_ref.at[:, at], out.at[size])
    if whole:
        for b in range(pool_ref.shape[0]):
            move(pool_ref.at[b], outs[-1].at[b])
    if not direct:
        for load, store in moves:
            load.wait()
            store.start()
    for _, store in moves:
        store.wait()


def gather(counts, asked, pool, new_rows, plan, after=(), direct=True, whole=False):
    sizes = [size + (to is not None) for _, _, size, to in plan] + [pool.shape[0]] * whole
    blocks = sum(sizes)
    scratch = [pltpu.SemaphoreType.DMA((blocks,))]
    if not direct:
        scratch.append(pltpu.VMEM((blocks,) + pool.shape[1:], pool.dtype))
        scratch.append(pltpu.SemaphoreType.DMA((blocks,)))
    return pl.pallas_call(
        functools.partial(gather_kernel, plan, len(asked), pool.shape[2], direct, whole),
        out_shape=[jax.ShapeDtypeStruct((size,) + pool.shape[1:], pool.dtype) for size in sizes],
        in_specs=[SMEM] * (1 + len(asked)) + [VMEM if direct else HBM] * 2 + [ANY] * len(after),
        out_specs=[ANY if direct else HBM] * len(sizes),
        scratch_shapes=scratch,
        compiler_params=pltpu.CompilerParams(
            vmem_limit_bytes=VMEM_LIMIT if direct else WHOLE_LIMIT
        ),
        cost_estimate=pl.CostEstimate(
            flops=0, bytes_accessed=4 * blocks * math.prod(pool.shape[1:]), transcendentals=0
        ),
    )(counts, *asked, pool, new_rows, *after)


def write_back_kernel(capacity, block_rows, count, owner_ref, slot_ref, *refs):
    asked, refs = refs[:count], refs[count:]
    new_ref, fresh = refs[0], refs[1 : count + 1]
    out_ref, token_ref, sem = refs[count + 2 :]
    me = lax.axis_index("blk")
    token_ref[0, 0] = 0

    def put(wanted, src, slot):
        @pl.when(wanted)
        def write():
            copy = pltpu.make_async_copy(src, out_ref.at[slot], sem)
            copy.start()
            copy.wait()

    for i in range(count):
        slot = asked[i][0, capacity]
        put(slot >= 0, fresh[i].at[fresh[i].shape[0] - 1], slot)
    for b in range(owner_ref.shape[1]):
        rows = pl.ds(b * block_rows, block_rows)
        put(owner_ref[0, b] == me, new_ref.at[:, rows], slot_ref[0, b])


def write_back(write_owner, write_slot, asked, new_rows, fresh, pool, capacity):
    count = len(asked)
    return pl.pallas_call(
        functools.partial(write_back_kernel, capacity, pool.shape[2], count),
        out_shape=[
            jax.ShapeDtypeStruct(pool.shape, pool.dtype),
            jax.ShapeDtypeStruct((1, 1), jnp.int32),
        ],
        in_specs=[SMEM] * (count + 2) + [VMEM] * (count + 1) + [ANY],
        out_specs=[ANY, SMEM],
        scratch_shapes=[pltpu.SemaphoreType.DMA],
        input_output_aliases={2 * count + 3: 0},
        compiler_params=pltpu.CompilerParams(vmem_limit_bytes=VMEM_LIMIT),
        cost_estimate=pl.CostEstimate(flops=0, bytes_accessed=1 << 20, transcendentals=0),
    )(write_owner, write_slot, *asked, new_rows, *fresh, pool)


def attend_kernel(
    spans, relays, afters, kv_dev, group, block_tok, rows, first, final, count_ref, q_ref, *refs
):
    parts, refs = refs[: len(spans)], refs[len(spans) :]
    ins = 1 if first else 2
    outs = 1 if final else 3 if first else 2
    rest = refs[ins + relays + afters :]
    refs = refs[:ins] + rest[:outs] + rest[-3:]
    if first:
        new_ref, q_out, acc_out, stat_out = refs[:4]
        head_dim = q_ref.shape[2]
        suffix = new_ref.shape[1] // kv_dev
    else:
        acc_in, stat_in = refs[:2]
        head_dim = q_ref.shape[2]
        suffix = 0
        if final:
            out_ref = refs[2]
        else:
            acc_out, stat_out = refs[2:4]
    key_ref, value_ref, stage_ref = refs[-3:]
    factor = head_dim**-0.5 * math.log2(math.e)
    prefix_keys = sum(size for _, _, size in spans) * block_tok
    keys = prefix_keys + suffix

    def unpack(raw, kv, at):
        stage_ref[...] = raw.astype(jnp.float32)
        for h in range(kv_dev):
            head = stage_ref[pl.ds(h, block_tok, stride=kv_dev), :]
            if kv == 0:
                key_ref[h, pl.ds(at, block_tok)] = head.astype(jnp.bfloat16)
            else:
                value_ref[h, :head_dim, pl.ds(at, block_tok)] = head.T.astype(jnp.bfloat16)

    value_ref[:, head_dim:, :] = jnp.ones(
        (kv_dev, value_ref.shape[1] - head_dim, keys), jnp.bfloat16
    )
    base = 0
    for part, (row, start, size) in zip(parts, spans):
        for b in range(size):
            counts = count_ref[0, row] > start + b
            at = pl.ds(base + b * block_tok, block_tok)

            @pl.when(counts)
            def take(part=part, b=b, base=base):
                for kv in range(2):
                    unpack(part[b, kv], kv, base + b * block_tok)

            @pl.when(jnp.logical_not(counts))
            def leave_out(at=at):
                for h in range(kv_dev):
                    key_ref[h, at] = jnp.zeros((block_tok, head_dim), jnp.bfloat16)
                    value_ref[h, :, at] = jnp.zeros((value_ref.shape[1], block_tok), jnp.bfloat16)

        base += size * block_tok
    for piece in range(suffix // block_tok):
        for kv in range(2):
            raw = new_ref[kv, pl.ds(piece * block_tok * kv_dev, block_tok * kv_dev), :]
            unpack(raw, kv, base + piece * block_tok)

    if first:
        for h in range(kv_dev):
            heads = q_ref[...].astype(jnp.float32)[:, h * group : (h + 1) * group, :]
            q_out[h] = heads.reshape(-1, head_dim).astype(jnp.bfloat16)
        q_rows = q_out
    else:
        q_rows = q_ref

    def run(safe, rows):
        def product(start, stop, h, at):
            return lax.dot_general(
                key_ref[h, start:stop],
                q_rows[h, at],
                (((1,), (1,)), ((), ())),
                preferred_element_type=jnp.float32,
            )

        def sub(index, worst):
            at = pl.ds(pl.multiple_of(index * rows, rows), rows)
            results = []
            for h in range(kv_dev):
                pieces = []
                if spans:
                    scores = product(0, prefix_keys, h, at)
                    if first or safe:
                        place = lax.broadcasted_iota(jnp.int32, (prefix_keys, 1), 0)
                        allowed = jnp.zeros((prefix_keys, 1), jnp.bool_)
                        base = 0
                        for row, start, size in spans:
                            end = base + jnp.minimum(count_ref[0, row] - start, size) * block_tok
                            allowed |= (place >= base) & (place < end)
                            base += size * block_tok
                        scores = jnp.where(allowed, scores, -jnp.inf)
                    pieces.append((scores, 0))
                if first:
                    scores = product(prefix_keys, keys, h, at)
                    token = lax.broadcasted_iota(jnp.int32, (1, rows), 1) + index * rows
                    place = lax.broadcasted_iota(jnp.int32, (suffix, rows), 0)
                    scores = jnp.where(place * group <= token, scores, -jnp.inf)
                    pieces.append((scores, prefix_keys))
                peak = factor * functools.reduce(
                    jnp.maximum, [jnp.max(scores, axis=0, keepdims=True) for scores, _ in pieces]
                )
                if not first:
                    old = stat_in[h, 0:1, at]
                    if safe:
                        peak = jnp.maximum(peak, old)
                    else:
                        worst = jnp.maximum(worst, peak - old)
                        peak = old
                both = sum(
                    jnp.dot(
                        value_ref[h, :, start : start + scores.shape[0]],
                        jnp.exp2(scores * factor - peak).astype(jnp.bfloat16),
                        preferred_element_type=jnp.float32,
                    )
                    for scores, start in pieces
                )
                summed = both[:head_dim]
                total = both[head_dim : head_dim + 1]
                if not first:
                    shrink = jnp.exp2(old - peak) if safe else 1.0
                    summed += acc_in[h, :, at] * shrink
                    total += stat_in[h, 1:2, at] * shrink
                if final:
                    results.append((summed / total).T.reshape(rows // group, group, head_dim))
                else:
                    acc_out[h, :, at] = summed
                    stat_out[h, 0:1, at] = peak
                    stat_out[h, 1:2, at] = total
            if final:
                tok = pl.multiple_of(index * (rows // group), rows // group)
                out_ref[pl.ds(tok, rows // group)] = jnp.concatenate(results, axis=1).astype(
                    jnp.bfloat16
                )
            return worst

        worst = lax.fori_loop(
            0,
            q_rows.shape[1] // rows,
            sub,
            jnp.full((1, rows), -jnp.inf, jnp.float32),
            unroll=not safe,
        )
        if not first and not safe:

            @pl.when(jnp.max(worst) > HEADROOM)
            def again():
                run(True, min(rows, SAFE_ROWS))

    run(first, rows)


def attend(
    counts, queries, parts, spans, kv_dev, block_tok, new_rows=None, state=None, final=False, relay=(), after=()
):
    suffix, heads_dev, head_dim = queries.shape
    group = heads_dev // kv_dev
    first = state is None
    rows = min(QUERY_ROWS, suffix * group)
    keys = sum(size for _, _, size in spans) * block_tok + (suffix if first else 0)
    state_shape = [
        jax.ShapeDtypeStruct((kv_dev, suffix * group, head_dim), jnp.bfloat16),
        jax.ShapeDtypeStruct((kv_dev, head_dim, suffix * group), jnp.float32),
        jax.ShapeDtypeStruct((kv_dev, 8, suffix * group), jnp.float32),
    ]
    if first:
        operands = [queries, *parts, new_rows]
        out_shape = state_shape
    else:
        operands = [state[0], *parts, *state[1:]]
        out_shape = state_shape[1:]
        if final:
            out_shape = [jax.ShapeDtypeStruct(queries.shape, queries.dtype)]
    result = pl.pallas_call(
        functools.partial(
            attend_kernel, spans, len(relay), len(after), kv_dev, group, block_tok, rows, first, final
        ),
        out_shape=out_shape + [jax.ShapeDtypeStruct(x.shape, x.dtype) for x in relay],
        in_specs=[SMEM] + [VMEM] * len(operands) + [ANY] * (len(relay) + len(after)),
        out_specs=[VMEM] * len(out_shape) + [ANY] * len(relay),
        input_output_aliases={
            1 + len(operands) + i: len(out_shape) + i for i in range(len(relay))
        },
        scratch_shapes=[
            pltpu.VMEM((kv_dev, keys, head_dim), jnp.bfloat16),
            pltpu.VMEM((kv_dev, head_dim + 16, keys), jnp.bfloat16),
            pltpu.VMEM((block_tok * kv_dev, head_dim), jnp.float32),
        ],
        compiler_params=pltpu.CompilerParams(vmem_limit_bytes=ATTEND_LIMIT),
        cost_estimate=pl.CostEstimate(
            flops=4 * suffix * heads_dev * keys * head_dim,
            bytes_accessed=keys * kv_dev * head_dim * 4 + 16 * suffix * heads_dev * head_dim,
            transcendentals=suffix * heads_dev * keys,
        ),
    )(counts, *operands, *relay, *after)
    step, relayed = result[: len(out_shape)], result[len(out_shape) :]
    return (step if first or final else [state[0], *step]), relayed


def per_device(
    queries, new_kv, pool, prefix_slot, prefix_owner, prefix_len, write_slot, write_owner
):
    num_blk = lax.axis_size("blk")
    pool_dev, _, block_tok, kv_dev, head_dim = pool.shape
    suffix = queries.shape[1]
    prefix_blocks = prefix_slot.shape[1]
    capacity = max(2, (prefix_blocks + num_blk - 1) // num_blk)
    shifts = sorted(range(1, num_blk), key=lambda d: -min(d, num_blk - d))
    pool_rows = pool.reshape(pool_dev, 2, block_tok * kv_dev, head_dim)
    new_rows = new_kv.reshape(2, suffix * kv_dev, head_dim)

    def shift(array, d):
        return lax.ppermute(array, "blk", [(i, (i + d) % num_blk) for i in range(num_blk)])

    ahead = num_blk - shifts[0]
    counts, asks, farthest = prepare(
        prefix_slot,
        prefix_owner,
        prefix_len,
        write_slot,
        write_owner,
        new_rows,
        block_tok * kv_dev,
        ahead,
        capacity,
        num_blk,
    )
    farthest = shift(farthest, ahead)
    asked = {d: shift(asks[d], d) for d in shifts}
    rows = [asked[d] for d in shifts]

    first = max(1, 3 * capacity // 8)
    cuts = sorted({0, first, 2 * first, capacity})
    plans = [[(d, start, end - start) for d in shifts] for start, end in zip(cuts, cuts[1:])]

    def load(plan, first, after=()):
        return gather(
            counts,
            rows,
            pool_rows,
            new_rows,
            tuple(
                (shifts.index(d), start, size, num_blk - d if first and d != shifts[0] else None)
                for d, start, size in plan
            ),
            after,
            not first,
        )

    def send(plan, blocks):
        return [shift(x, num_blk - d) for (d, _, _), x in zip(plan, blocks)]

    loaded = load(plans[0], True)
    arrived = [send(plans[0], loaded)]
    local, new_pool = gather(
        counts, [asks[0]], pool_rows, new_rows, ((0, 0, capacity, None),), [loaded[0], farthest], whole=True
    )
    step = functools.partial(attend, counts, queries[0], kv_dev=kv_dev, block_tok=block_tok)
    state, _ = step([local], ((0, 0, capacity),), new_rows=new_rows)

    later = load(sum(plans[1:], []), False, [state[2]])
    arrived.append(send(plans[1], later[: len(shifts)]))
    token = None
    for i, plan in enumerate(plans):
        relay = later[len(shifts) :] if i == 0 else []
        groups = [slice(at, at + 8) for at in range(0, len(plan), 8)]
        for j, group in enumerate(groups):
            ends = j == len(groups) - 1
            state, relayed = step(
                arrived[i][group],
                tuple(plan[group]),
                state=state,
                final=ends and i == len(plans) - 1,
                relay=relay if ends else [],
                after=[token] if i == 1 and j == 0 else [],
            )
        if i == 0:
            for k in range(2, len(plans)):
                blocks, relayed = relayed[: len(plans[k])], relayed[len(plans[k]) :]
                arrived.append(send(plans[k], blocks))
            new_pool, token = write_back(
                write_owner,
                write_slot,
                [asked[num_blk - d] for d in shifts],
                new_rows,
                [farthest, *arrived[0][1:]],
                new_pool,
                capacity,
            )
    return state[0][None], new_pool.reshape(pool.shape)


def solution(mesh):
    in_specs = (
        P(("group", "blk"), None, "tensor", None),
        P(None, ("group", "blk"), None, "tensor", None),
        P(("group", "blk"), None, None, "tensor", None),
        P(("group", "blk"), None),
        P(("group", "blk"), None),
        P(("group", "blk")),
        P(("group", "blk"), None),
        P(("group", "blk"), None),
    )
    out_specs = (
        P(("group", "blk"), None, "tensor", None),
        P(("group", "blk"), None, None, "tensor", None),
    )
    return jax.shard_map(
        per_device, mesh=mesh, in_specs=in_specs, out_specs=out_specs, check_vma=False
    )
```

```python
import functools
import math

import jax
import jax.numpy as jnp
from jax import lax
from jax.experimental import pallas as pl
from jax.experimental.pallas import tpu as pltpu
from jax.sharding import PartitionSpec as P

ANY = pl.BlockSpec(memory_space=pl.ANY)
HBM = pl.BlockSpec(memory_space=pltpu.HBM)
SMEM = pl.BlockSpec(memory_space=pltpu.SMEM)
VMEM = pl.BlockSpec(memory_space=pltpu.VMEM)
WHOLE_LIMIT = 60 * 1024 * 1024
VMEM_LIMIT = 16 * 1024 * 1024
ATTEND_LIMIT = 32 * 1024 * 1024
QUERY_ROWS = 1024
SAFE_ROWS = 256
HEADROOM = 60.0


def prepare_kernel(capacity, to, *refs):
    sources, refs = refs[:6], refs[6:]
    num_blk = refs[0].shape[1] // 2
    count_ref, asked, refs = refs[0], refs[1 : 1 + num_blk], refs[1 + num_blk :]
    fresh, refs = refs[: len(to)], refs[len(to) :]
    held, (table_ref, used_ref, counted_ref, load_sems, store_sems) = refs[:6], refs[6:]
    loads = [
        pltpu.make_async_copy(source, target, load_sems.at[i])
        for i, (source, target) in enumerate(zip(sources, held))
    ]
    for load in loads:
        load.start()
    slot_ref, owner_ref, len_ref, write_slot_ref, write_owner_ref, new_ref = held
    me = lax.axis_index("blk")
    for owner in range(num_blk):
        used_ref[owner] = 0
        counted_ref[owner] = 0
        for k in range(capacity):
            table_ref[owner, k] = 0
    for load in loads:
        load.wait()
    stores = []
    for i, (d, out) in enumerate(zip(to, fresh)):
        target = lax.rem(me + d, num_blk)
        chosen = jnp.int32(0)
        for b in range(write_owner_ref.shape[1]):
            chosen = jnp.where(write_owner_ref[0, b] == target, b, chosen)
        block_rows = out.shape[2]
        rows = pl.ds(pl.multiple_of(chosen * block_rows, block_rows), block_rows)
        stores.append(pltpu.make_async_copy(new_ref.at[:, rows], out.at[0], store_sems.at[i]))
    for store in stores:
        store.start()

    def step(j, carry):
        owner = owner_ref[0, j]
        place = used_ref[owner]
        table_ref[owner, jnp.minimum(place, capacity)] = slot_ref[0, j]
        used_ref[owner] = place + 1
        counted_ref[owner] += jnp.where(j < len_ref[0], 1, 0)
        return carry

    lax.fori_loop(0, owner_ref.shape[1], step, 0, unroll=8)
    for d in range(num_blk):
        owner = lax.rem(me + d, num_blk)
        count_ref[0, d] = counted_ref[owner]
        for k in range(capacity):
            asked[d][0, k] = table_ref[owner, k]
        slot = jnp.int32(-1)
        chosen = jnp.int32(0)
        for b in range(write_owner_ref.shape[1]):
            goes = write_owner_ref[0, b] == owner
            slot = jnp.where(goes, write_slot_ref[0, b], slot)
            chosen = jnp.where(goes, b, chosen)
        asked[d][0, capacity] = slot
        count_ref[0, num_blk + d] = chosen
    for store in stores:
        store.wait()


def prepare(
    prefix_slot, prefix_owner, prefix_len, write_slot, write_owner, new_rows, block_rows, to,
    capacity, num_blk,
):
    operands = (prefix_slot, prefix_owner, prefix_len, write_slot, write_owner, new_rows)
    block = jax.ShapeDtypeStruct((1, 2, block_rows, new_rows.shape[2]), new_rows.dtype)
    row = jax.ShapeDtypeStruct((1, capacity + 1), jnp.int32)
    results = pl.pallas_call(
        functools.partial(prepare_kernel, capacity, to),
        out_shape=[jax.ShapeDtypeStruct((1, 2 * num_blk), jnp.int32)]
        + [row] * num_blk
        + [block] * len(to),
        in_specs=[HBM] * 6,
        out_specs=[SMEM] * (num_blk + 1) + [HBM] * len(to),
        scratch_shapes=[pltpu.SMEM(operand.shape, operand.dtype) for operand in operands[:5]]
        + [
            pltpu.VMEM(new_rows.shape, new_rows.dtype),
            pltpu.SMEM((num_blk, capacity + 1), jnp.int32),
            pltpu.SMEM((num_blk,), jnp.int32),
            pltpu.SMEM((num_blk,), jnp.int32),
            pltpu.SemaphoreType.DMA((6,)),
            pltpu.SemaphoreType.DMA((len(to),)),
        ],
        compiler_params=pltpu.CompilerParams(vmem_limit_bytes=WHOLE_LIMIT),
    )(*operands)
    return results[0], results[1 : num_blk + 1], results[num_blk + 1 :]


def gather_kernel(plan, count, block_rows, direct, whole, count_ref, *refs):
    asked, pool_ref, new_ref = refs[:count], refs[count], refs[count + 1]
    refs = refs[-len(plan) - whole - (1 if direct else 3) :]
    outs, refs = refs[: len(plan) + whole], refs[len(plan) + whole :]
    sems = refs[0]
    moves = []

    def move(source, target):
        i = len(moves)
        if direct:
            load, store = None, pltpu.make_async_copy(source, target, sems.at[i])
            store.start()
        else:
            held, in_sems = refs[1:]
            load = pltpu.make_async_copy(source, held.at[i], in_sems.at[i])
            store = pltpu.make_async_copy(held.at[i], target, sems.at[i])
            load.start()
        moves.append((load, store))

    for (row, start, size, to), out in zip(plan, outs):
        for place in range(size):
            move(pool_ref.at[asked[row][0, start + place]], out.at[place])
        if to is not None:
            chosen = count_ref[0, count_ref.shape[1] // 2 + to]
            at = pl.ds(pl.multiple_of(chosen * block_rows, block_rows), block_rows)
            move(new_ref.at[:, at], out.at[size])
    if whole:
        for b in range(pool_ref.shape[0]):
            move(pool_ref.at[b], outs[-1].at[b])
    if not direct:
        for load, store in moves:
            load.wait()
            store.start()
    for _, store in moves:
        store.wait()


def gather(counts, asked, pool, new_rows, plan, after=(), direct=True, whole=False):
    sizes = [size + (to is not None) for _, _, size, to in plan] + [pool.shape[0]] * whole
    blocks = sum(sizes)
    scratch = [pltpu.SemaphoreType.DMA((blocks,))]
    if not direct:
        scratch.append(pltpu.VMEM((blocks,) + pool.shape[1:], pool.dtype))
        scratch.append(pltpu.SemaphoreType.DMA((blocks,)))
    return pl.pallas_call(
        functools.partial(gather_kernel, plan, len(asked), pool.shape[2], direct, whole),
        out_shape=[jax.ShapeDtypeStruct((size,) + pool.shape[1:], pool.dtype) for size in sizes],
        in_specs=[SMEM] * (1 + len(asked)) + [VMEM if direct else HBM] * 2 + [ANY] * len(after),
        out_specs=[ANY if direct else HBM] * len(sizes),
        scratch_shapes=scratch,
        compiler_params=pltpu.CompilerParams(
            vmem_limit_bytes=VMEM_LIMIT if direct else WHOLE_LIMIT
        ),
        cost_estimate=pl.CostEstimate(
            flops=0, bytes_accessed=4 * blocks * math.prod(pool.shape[1:]), transcendentals=0
        ),
    )(counts, *asked, pool, new_rows, *after)


def write_back_kernel(capacity, block_rows, count, owner_ref, slot_ref, *refs):
    asked, refs = refs[:count], refs[count:]
    new_ref, fresh = refs[0], refs[1 : count + 1]
    out_ref, token_ref, sem = refs[count + 2 :]
    me = lax.axis_index("blk")
    token_ref[0, 0] = 0

    def put(wanted, src, slot):
        @pl.when(wanted)
        def write():
            copy = pltpu.make_async_copy(src, out_ref.at[slot], sem)
            copy.start()
            copy.wait()

    for i in range(count):
        slot = asked[i][0, capacity]
        put(slot >= 0, fresh[i].at[fresh[i].shape[0] - 1], slot)
    for b in range(owner_ref.shape[1]):
        rows = pl.ds(b * block_rows, block_rows)
        put(owner_ref[0, b] == me, new_ref.at[:, rows], slot_ref[0, b])


def write_back(write_owner, write_slot, asked, new_rows, fresh, pool, capacity):
    count = len(asked)
    return pl.pallas_call(
        functools.partial(write_back_kernel, capacity, pool.shape[2], count),
        out_shape=[
            jax.ShapeDtypeStruct(pool.shape, pool.dtype),
            jax.ShapeDtypeStruct((1, 1), jnp.int32),
        ],
        in_specs=[SMEM] * (count + 2) + [VMEM] * (count + 1) + [ANY],
        out_specs=[ANY, SMEM],
        scratch_shapes=[pltpu.SemaphoreType.DMA],
        input_output_aliases={2 * count + 3: 0},
        compiler_params=pltpu.CompilerParams(vmem_limit_bytes=VMEM_LIMIT),
        cost_estimate=pl.CostEstimate(flops=0, bytes_accessed=1 << 20, transcendentals=0),
    )(write_owner, write_slot, *asked, new_rows, *fresh, pool)


def attend_kernel(
    spans, relays, afters, kv_dev, group, block_tok, rows, first, final, count_ref, q_ref, *refs
):
    parts, refs = refs[: len(spans)], refs[len(spans) :]
    ins = 1 if first else 2
    outs = 1 if final else 3 if first else 2
    rest = refs[ins + relays + afters :]
    refs = refs[:ins] + rest[:outs] + rest[-3:]
    if first:
        new_ref, q_out, acc_out, stat_out = refs[:4]
        head_dim = q_ref.shape[2]
        suffix = new_ref.shape[1] // kv_dev
    else:
        acc_in, stat_in = refs[:2]
        head_dim = q_ref.shape[2]
        suffix = 0
        if final:
            out_ref = refs[2]
        else:
            acc_out, stat_out = refs[2:4]
    key_ref, value_ref, stage_ref = refs[-3:]
    factor = head_dim**-0.5 * math.log2(math.e)
    prefix_keys = sum(size for _, _, size in spans) * block_tok
    keys = prefix_keys + suffix

    def unpack(raw, kv, at):
        stage_ref[...] = raw.astype(jnp.float32)
        for h in range(kv_dev):
            head = stage_ref[pl.ds(h, block_tok, stride=kv_dev), :]
            if kv == 0:
                key_ref[h, pl.ds(at, block_tok)] = head.astype(jnp.bfloat16)
            else:
                value_ref[h, :head_dim, pl.ds(at, block_tok)] = head.T.astype(jnp.bfloat16)

    value_ref[:, head_dim:, :] = jnp.ones(
        (kv_dev, value_ref.shape[1] - head_dim, keys), jnp.bfloat16
    )
    base = 0
    for part, (row, start, size) in zip(parts, spans):
        for b in range(size):
            counts = count_ref[0, row] > start + b
            at = pl.ds(base + b * block_tok, block_tok)

            @pl.when(counts)
            def take(part=part, b=b, base=base):
                for kv in range(2):
                    unpack(part[b, kv], kv, base + b * block_tok)

            @pl.when(jnp.logical_not(counts))
            def leave_out(at=at):
                for h in range(kv_dev):
                    key_ref[h, at] = jnp.zeros((block_tok, head_dim), jnp.bfloat16)
                    value_ref[h, :, at] = jnp.zeros((value_ref.shape[1], block_tok), jnp.bfloat16)

        base += size * block_tok
    for piece in range(suffix // block_tok):
        for kv in range(2):
            raw = new_ref[kv, pl.ds(piece * block_tok * kv_dev, block_tok * kv_dev), :]
            unpack(raw, kv, base + piece * block_tok)

    if first:
        for h in range(kv_dev):
            heads = q_ref[...].astype(jnp.float32)[:, h * group : (h + 1) * group, :]
            q_out[h] = heads.reshape(-1, head_dim).astype(jnp.bfloat16)
        q_rows = q_out
    else:
        q_rows = q_ref

    def run(safe, rows):
        def product(start, stop, h, at):
            return lax.dot_general(
                key_ref[h, start:stop],
                q_rows[h, at],
                (((1,), (1,)), ((), ())),
                preferred_element_type=jnp.float32,
            )

        def sub(index, worst):
            at = pl.ds(pl.multiple_of(index * rows, rows), rows)
            results = []
            for h in range(kv_dev):
                pieces = []
                if spans:
                    scores = product(0, prefix_keys, h, at)
                    if first or safe:
                        place = lax.broadcasted_iota(jnp.int32, (prefix_keys, 1), 0)
                        allowed = jnp.zeros((prefix_keys, 1), jnp.bool_)
                        base = 0
                        for row, start, size in spans:
                            end = base + jnp.minimum(count_ref[0, row] - start, size) * block_tok
                            allowed |= (place >= base) & (place < end)
                            base += size * block_tok
                        scores = jnp.where(allowed, scores, -jnp.inf)
                    pieces.append((scores, 0))
                if first:
                    scores = product(prefix_keys, keys, h, at)
                    token = lax.broadcasted_iota(jnp.int32, (1, rows), 1) + index * rows
                    place = lax.broadcasted_iota(jnp.int32, (suffix, rows), 0)
                    scores = jnp.where(place * group <= token, scores, -jnp.inf)
                    pieces.append((scores, prefix_keys))
                peak = factor * functools.reduce(
                    jnp.maximum, [jnp.max(scores, axis=0, keepdims=True) for scores, _ in pieces]
                )
                if not first:
                    old = stat_in[h, 0:1, at]
                    if safe:
                        peak = jnp.maximum(peak, old)
                    else:
                        worst = jnp.maximum(worst, peak - old)
                        peak = old
                both = sum(
                    jnp.dot(
                        value_ref[h, :, start : start + scores.shape[0]],
                        jnp.exp2(scores * factor - peak).astype(jnp.bfloat16),
                        preferred_element_type=jnp.float32,
                    )
                    for scores, start in pieces
                )
                summed = both[:head_dim]
                total = both[head_dim : head_dim + 1]
                if not first:
                    shrink = jnp.exp2(old - peak) if safe else 1.0
                    summed += acc_in[h, :, at] * shrink
                    total += stat_in[h, 1:2, at] * shrink
                if final:
                    results.append((summed / total).T.reshape(rows // group, group, head_dim))
                else:
                    acc_out[h, :, at] = summed
                    stat_out[h, 0:1, at] = peak
                    stat_out[h, 1:2, at] = total
            if final:
                tok = pl.multiple_of(index * (rows // group), rows // group)
                out_ref[pl.ds(tok, rows // group)] = jnp.concatenate(results, axis=1).astype(
                    jnp.bfloat16
                )
            return worst

        worst = lax.fori_loop(
            0,
            q_rows.shape[1] // rows,
            sub,
            jnp.full((1, rows), -jnp.inf, jnp.float32),
            unroll=not safe,
        )
        if not first and not safe:

            @pl.when(jnp.max(worst) > HEADROOM)
            def again():
                run(True, min(rows, SAFE_ROWS))

    run(first, rows)


def attend(
    counts, queries, parts, spans, kv_dev, block_tok, new_rows=None, state=None, final=False, relay=(), after=()
):
    suffix, heads_dev, head_dim = queries.shape
    group = heads_dev // kv_dev
    first = state is None
    rows = min(QUERY_ROWS, suffix * group)
    keys = sum(size for _, _, size in spans) * block_tok + (suffix if first else 0)
    state_shape = [
        jax.ShapeDtypeStruct((kv_dev, suffix * group, head_dim), jnp.bfloat16),
        jax.ShapeDtypeStruct((kv_dev, head_dim, suffix * group), jnp.float32),
        jax.ShapeDtypeStruct((kv_dev, 8, suffix * group), jnp.float32),
    ]
    if first:
        operands = [queries, *parts, new_rows]
        out_shape = state_shape
    else:
        operands = [state[0], *parts, *state[1:]]
        out_shape = state_shape[1:]
        if final:
            out_shape = [jax.ShapeDtypeStruct(queries.shape, queries.dtype)]
    result = pl.pallas_call(
        functools.partial(
            attend_kernel, spans, len(relay), len(after), kv_dev, group, block_tok, rows, first, final
        ),
        out_shape=out_shape + [jax.ShapeDtypeStruct(x.shape, x.dtype) for x in relay],
        in_specs=[SMEM] + [VMEM] * len(operands) + [ANY] * (len(relay) + len(after)),
        out_specs=[VMEM] * len(out_shape) + [ANY] * len(relay),
        input_output_aliases={
            1 + len(operands) + i: len(out_shape) + i for i in range(len(relay))
        },
        scratch_shapes=[
            pltpu.VMEM((kv_dev, keys, head_dim), jnp.bfloat16),
            pltpu.VMEM((kv_dev, head_dim + 16, keys), jnp.bfloat16),
            pltpu.VMEM((block_tok * kv_dev, head_dim), jnp.float32),
        ],
        compiler_params=pltpu.CompilerParams(vmem_limit_bytes=ATTEND_LIMIT),
        cost_estimate=pl.CostEstimate(
            flops=4 * suffix * heads_dev * keys * head_dim,
            bytes_accessed=keys * kv_dev * head_dim * 4 + 16 * suffix * heads_dev * head_dim,
            transcendentals=suffix * heads_dev * keys,
        ),
    )(counts, *operands, *relay, *after)
    step, relayed = result[: len(out_shape)], result[len(out_shape) :]
    return (step if first or final else [state[0], *step]), relayed


def per_device(
    queries, new_kv, pool, prefix_slot, prefix_owner, prefix_len, write_slot, write_owner
):
    num_blk = lax.axis_size("blk")
    pool_dev, _, block_tok, kv_dev, head_dim = pool.shape
    suffix = queries.shape[1]
    prefix_blocks = prefix_slot.shape[1]
    capacity = max(2, (prefix_blocks + num_blk - 1) // num_blk)
    shifts = sorted(range(1, num_blk), key=lambda d: -min(d, num_blk - d))
    pool_rows = pool.reshape(pool_dev, 2, block_tok * kv_dev, head_dim)
    new_rows = new_kv.reshape(2, suffix * kv_dev, head_dim)

    def shift(array, d):
        return lax.ppermute(array, "blk", [(i, (i + d) % num_blk) for i in range(num_blk)])

    ahead = shifts[:2]
    counts, asks, early = prepare(
        prefix_slot,
        prefix_owner,
        prefix_len,
        write_slot,
        write_owner,
        new_rows,
        block_tok * kv_dev,
        tuple(num_blk - d for d in ahead),
        capacity,
        num_blk,
    )
    early = [shift(block, num_blk - d) for d, block in zip(ahead, early)]
    asked = {d: shift(asks[d], d) for d in shifts}
    rows = [asked[d] for d in shifts]

    first = max(1, 3 * capacity // 8)
    cuts = sorted({0, first, 2 * first, capacity})
    plans = [[(d, start, end - start) for d in shifts] for start, end in zip(cuts, cuts[1:])]

    def load(plan, first, after=()):
        return gather(
            counts,
            rows,
            pool_rows,
            new_rows,
            tuple(
                (shifts.index(d), start, size, num_blk - d if first and d not in ahead else None)
                for d, start, size in plan
            ),
            after,
            not first,
        )

    def send(plan, blocks):
        return [shift(x, num_blk - d) for (d, _, _), x in zip(plan, blocks)]

    loaded = load(plans[0], True)
    arrived = [send(plans[0], loaded)]
    local, new_pool = gather(
        counts, [asks[0]], pool_rows, new_rows, ((0, 0, capacity, None),), [loaded[0], *early], whole=True
    )
    step = functools.partial(attend, counts, queries[0], kv_dev=kv_dev, block_tok=block_tok)
    state, _ = step([local], ((0, 0, capacity),), new_rows=new_rows)

    later = load(sum(plans[1:], []), False, [state[2]])
    arrived.append(send(plans[1], later[: len(shifts)]))
    token = None
    for i, plan in enumerate(plans):
        relay = later[len(shifts) :] if i == 0 else []
        groups = [slice(at, at + 8) for at in range(0, len(plan), 8)]
        for j, group in enumerate(groups):
            ends = j == len(groups) - 1
            state, relayed = step(
                arrived[i][group],
                tuple(plan[group]),
                state=state,
                final=ends and i == len(plans) - 1,
                relay=relay if ends else [],
                after=[token] if i == 1 and j == 0 else [],
            )
        if i == 0:
            for k in range(2, len(plans)):
                blocks, relayed = relayed[: len(plans[k])], relayed[len(plans[k]) :]
                arrived.append(send(plans[k], blocks))
            new_pool, token = write_back(
                write_owner,
                write_slot,
                [asked[num_blk - d] for d in shifts],
                new_rows,
                [*early, *arrived[0][len(early) :]],
                new_pool,
                capacity,
            )
    return state[0][None], new_pool.reshape(pool.shape)


def solution(mesh):
    in_specs = (
        P(("group", "blk"), None, "tensor", None),
        P(None, ("group", "blk"), None, "tensor", None),
        P(("group", "blk"), None, None, "tensor", None),
        P(("group", "blk"), None),
        P(("group", "blk"), None),
        P(("group", "blk")),
        P(("group", "blk"), None),
        P(("group", "blk"), None),
    )
    out_specs = (
        P(("group", "blk"), None, "tensor", None),
        P(("group", "blk"), None, None, "tensor", None),
    )
    return jax.shard_map(
        per_device, mesh=mesh, in_specs=in_specs, out_specs=out_specs, check_vma=False
    )
```
